32 devices in a mesh: band: 8 (over y, x, core), chan: 4 (over z).
Axes of the slice: x: 2, y: 2, z: 4, core: 2. Of those that a mesh axis runs over, the one named last changes fastest.
Arguments:
- image: bfloat16 [512, 32, 512], P('chan', 'band'), may hold values from -6 to 6
- filters: bfloat16 [9, 512, 512], P(None, None, 'chan'), may hold values from -0.09375 to 0.09375
- bias: bfloat16 [512], P('chan'), may hold values from -3 to 3
- upstream: bfloat16 [512, 32, 512], P('chan', 'band'), may hold values from -6 to 6
Outputs:
- features: bfloat16 [512, 32, 512], P('chan', 'band')
- image_grad: bfloat16 [512, 32, 512], P('chan', 'band')
The draws below stay inside these ranges and needn't reach their ends.
All inputs are finite; a program needn't handle non-finite values.
Results may differ from the reference program's by a relative error of at most 0.001.
Values may be sent and summed in bfloat16 or wider, within the bound.
No kernel may reach another device: no remote copies, remote signals or barrier semaphores. Data moves between devices by JAX's collectives and lax.ppermute only.
A program may use at most 64 MiB of HBM per device.

```python
import jax
import jax.numpy as jnp
from jax import lax

CH = 512
COLS = 512
ROWS = 32


def levels(stream_key, extent, cuts, smallest, top_value):
    def one(position, parts):
        draws = jax.random.uniform(jax.random.fold_in(jax.random.fold_in(stream_key, 6), position), (parts,), jnp.float32, smallest / len(cuts), top_value / len(cuts))
        return jnp.repeat(jnp.exp(draws), extent[position] // parts).reshape((-1,) + (1,) * (len(extent) - position - 1))

    gain = one(*cuts[0])
    for cut in cuts[1:]:
        gain = gain * one(*cut)
    return gain


def noise(own_key, dims, deviation, bound, pieces=(), kind=jnp.bfloat16):
    factor_of = levels(own_key, dims, pieces, -0.22, 0.18) if pieces else 1.0
    array = jax.random.normal(own_key, dims, jnp.float32) * deviation * factor_of
    return jnp.minimum(jnp.maximum(array, -bound), bound).astype(kind)


def setup_inputs(seed: int = 0) -> dict:
    key_of = jax.random.split(jax.random.key(seed), 5)
    return {
        "image": noise(key_of[0], (CH, ROWS, COLS), 1.0, 6.0, ((0, 4), (1, 8))),
        "filters": noise(key_of[1], (9, CH, CH), (9 * CH) ** -0.5, 0.09375, ((2, 4),)),
        "bias": noise(key_of[2], (CH,), 0.5, 3.0, ((0, 4),)),
        "upstream": noise(key_of[3], (CH, ROWS, COLS), 1.0, 6.0, ((0, 4), (1, 8))),
    }


def reference(image, filters, bias, upstream):
    image_pad = jnp.pad(image.astype(jnp.float32), ((0, 0), (1, 1), (1, 1)))
    upstream_pad = jnp.pad(upstream.astype(jnp.float32), ((0, 0), (1, 1), (1, 1)))
    weights = filters.astype(jnp.float32)
    forward_acc = jnp.zeros((CH, ROWS, COLS), jnp.float32)
    backward_acc = jnp.zeros((CH, ROWS, COLS), jnp.float32)
    for tap_row in range(3):
        for tap_col in range(3):
            tap_index = tap_row * 3 + tap_col
            forward_acc = forward_acc + jnp.einsum(
                "oi,irc->orc", weights[tap_index],
                image_pad[:, tap_row:tap_row + ROWS, tap_col:tap_col + COLS],
                precision=lax.Precision.HIGHEST)
            backward_acc = backward_acc + jnp.einsum(
                "oi,orc->irc", weights[tap_index],
                upstream_pad[:, 2 - tap_row:2 - tap_row + ROWS, 2 - tap_col:2 - tap_col + COLS],
                precision=lax.Precision.HIGHEST)
    features = (forward_acc + bias.astype(jnp.float32)[:, None, None]).astype(jnp.bfloat16)
    image_grad = backward_acc.astype(jnp.bfloat16)
    return features, image_grad
```

```python
import jax
import jax.numpy as jnp
from jax import lax
from jax.sharding import PartitionSpec as P


def swap(value, axis, step):
    size = lax.axis_size(axis)
    return lax.ppermute(value, axis, [(j, j ^ step) for j in range(size)])


def neighbours(first, last):
    size = lax.axis_size("band")
    up = [(j, j + 1) for j in range(size - 1)]
    down = [(j + 1, j) for j in range(size - 1)]
    return lax.ppermute(last, "band", up), lax.ppermute(first, "band", down)


def pick(pieces, index, axis):
    stacked = jnp.stack(pieces)
    return jnp.concatenate(
        [lax.dynamic_index_in_dim(stacked, i, 0, keepdims=False) for i in index], axis=axis
    )


def spread(value, me, width):
    n = lax.axis_size("chan")
    padded = jnp.pad(value, ((0, 0), (1, 1), (0, 0)))
    pieces = []
    for k in range(n):
        piece = lax.dynamic_slice_in_dim(padded, (me ^ k) * width, width + 2, axis=1)
        pieces.append(swap(piece, "chan", k) if k else piece)
    return pieces


def add_rows(value):
    before, after = neighbours(value[:1], value[-1:])
    return jnp.concatenate([before, value, after], axis=0)


def conv(source, taps):
    return lax.conv_general_dilated(
        source[None],
        taps,
        (1, 1),
        "VALID",
        dimension_numbers=("NHWC", "HWIO", "NHWC"),
        preferred_element_type=jnp.float32,
    )[0]


def per_device(image, filters, bias, upstream):
    n = lax.axis_size("chan")
    bands = lax.axis_size("band")
    me = lax.axis_index("chan")
    row = lax.axis_index("band")
    local = filters.shape[2]
    outs = filters.shape[1]
    width = image.shape[2] // n

    flat = filters.reshape(-1, local)
    share = flat.shape[0] // bands
    part = lax.dynamic_slice_in_dim(flat, row * share, share, axis=0)
    held = [jnp.concatenate([part, jnp.tile(bias[None], (16, 1))], axis=0)]
    step = n // 2
    while step:
        stacked = jnp.stack(held)
        there = swap(stacked, "chan", step)
        held = held + [there[j] for j in range(len(held))]
        step //= 2
    order = [0]
    step = n // 2
    while step:
        order = order + [o ^ step for o in order]
        step //= 2
    held = [held[order.index(k)] for k in range(n)]
    biases = [h[share] for h in held]
    whole = lax.all_gather(
        jnp.stack([h[:share] for h in held]), "band", axis=1, tiled=True
    ).reshape(n, 3, 3, outs, local)

    x_pieces = spread(jnp.transpose(image, (1, 2, 0)), me, width)
    u_pieces = spread(jnp.transpose(upstream, (1, 2, 0)), me, width)

    natural = [me ^ k for k in range(n)]
    x = add_rows(jnp.concatenate(x_pieces, axis=2))
    forward_taps = jnp.transpose(whole, (1, 2, 0, 4, 3)).reshape(3, 3, n * local, outs)
    total = conv(x, forward_taps) + pick(biases, natural, 0).astype(jnp.float32)
    features = back(total.astype(jnp.bfloat16), me, local, True)

    u = add_rows(pick(u_pieces, natural, 2))
    backward_taps = jnp.transpose(whole[:, ::-1, ::-1], (1, 2, 3, 0, 4)).reshape(
        3, 3, outs, n * local
    )
    image_grad = back(conv(u, backward_taps).astype(jnp.bfloat16), me, local, False)
    return features, image_grad


def back(value, me, local, is_natural):
    n = lax.axis_size("chan")
    pieces = []
    for k in range(n):
        start = (me ^ k) * local if is_natural else k * local
        piece = lax.dynamic_slice_in_dim(value, start, local, axis=2)
        pieces.append(swap(piece, "chan", k) if k else piece)
    whole = pick(pieces, [me ^ k for k in range(n)], 1)
    return jnp.transpose(whole, (2, 0, 1))


def solution(mesh):
    return jax.shard_map(
        per_device,
        mesh=mesh,
        in_specs=(
            P("chan", "band", None),
            P(None, None, "chan"),
            P("chan"),
            P("chan", "band", None),
        ),
        out_specs=(P("chan", "band", None), P("chan", "band", None)),
        check_vma=False,
    )
```

```python
import jax
import jax.numpy as jnp
from jax import lax
from jax.experimental import pallas as pl
from jax.experimental.pallas import tpu as pltpu
from jax.sharding import PartitionSpec as P


def swap(value, axis, step):
    size = lax.axis_size(axis)
    return lax.ppermute(value, axis, [(j, j ^ step) for j in range(size)])


def neighbours(first, last):
    size = lax.axis_size("band")
    up = [(j, j + 1) for j in range(size - 1)]
    down = [(j + 1, j) for j in range(size - 1)]
    return lax.ppermute(last, "band", up), lax.ppermute(first, "band", down)


def pick(pieces, index, axis):
    stacked = jnp.stack(pieces)
    return jnp.concatenate(
        [lax.dynamic_index_in_dim(stacked, i, 0, keepdims=False) for i in index], axis=axis
    )


def spread(value, me, width):
    n = lax.axis_size("chan")
    padded = jnp.pad(value, ((0, 0), (1, 1), (0, 0)))
    pieces = []
    for k in range(n):
        piece = lax.dynamic_slice_in_dim(padded, (me ^ k) * width, width + 2, axis=1)
        pieces.append(swap(piece, "chan", k) if k else piece)
    return pieces


def add_rows(value):
    before, after = neighbours(value[:1], value[-1:])
    return jnp.concatenate([before, value, after], axis=0)


def conv(source, taps):
    return lax.conv_general_dilated(
        source[None],
        taps,
        (1, 1),
        "VALID",
        dimension_numbers=("NHWC", "HWIO", "NHWC"),
        preferred_element_type=jnp.float32,
    )[0]


def plain(image, filters, bias, upstream):
    n = lax.axis_size("chan")
    bands = lax.axis_size("band")
    me = lax.axis_index("chan")
    row = lax.axis_index("band")
    local = filters.shape[2]
    outs = filters.shape[1]
    width = image.shape[2] // n

    flat = filters.reshape(-1, local)
    share = flat.shape[0] // bands
    part = lax.dynamic_slice_in_dim(flat, row * share, share, axis=0)
    held = [jnp.concatenate([part, jnp.tile(bias[None], (16, 1))], axis=0)]
    step = n // 2
    while step:
        stacked = jnp.stack(held)
        there = swap(stacked, "chan", step)
        held = held + [there[j] for j in range(len(held))]
        step //= 2
    order = [0]
    step = n // 2
    while step:
        order = order + [o ^ step for o in order]
        step //= 2
    held = [held[order.index(k)] for k in range(n)]
    biases = [h[share] for h in held]
    whole = lax.all_gather(
        jnp.stack([h[:share] for h in held]), "band", axis=1, tiled=True
    ).reshape(n, 3, 3, outs, local)

    x_pieces = spread(jnp.transpose(image, (1, 2, 0)), me, width)
    u_pieces = spread(jnp.transpose(upstream, (1, 2, 0)), me, width)

    natural = [me ^ k for k in range(n)]
    x = add_rows(jnp.concatenate(x_pieces, axis=2))
    forward_taps = jnp.transpose(whole, (1, 2, 0, 4, 3)).reshape(3, 3, n * local, outs)
    total = conv(x, forward_taps) + pick(biases, natural, 0).astype(jnp.float32)
    features = back(total.astype(jnp.bfloat16), me, local, True)

    u = add_rows(pick(u_pieces, natural, 2))
    backward_taps = jnp.transpose(whole[:, ::-1, ::-1], (1, 2, 3, 0, 4)).reshape(
        3, 3, outs, n * local
    )
    image_grad = back(conv(u, backward_taps).astype(jnp.bfloat16), me, local, False)
    return features, image_grad


def back(value, me, local, is_natural):
    n = lax.axis_size("chan")
    pieces = []
    for k in range(n):
        start = (me ^ k) * local if is_natural else k * local
        piece = lax.dynamic_slice_in_dim(value, start, local, axis=2)
        pieces.append(swap(piece, "chan", k) if k else piece)
    whole = pick(pieces, [me ^ k for k in range(n)], 1)
    return jnp.transpose(whole, (2, 0, 1))


def fill_rows(target, piece, row, lanes, width):
    for shift in range(3):
        target[shift, pl.ds(row * width, width), lanes] = piece[shift : shift + width, :]


def fill_source(target, pieces, before, after, blocks, local, width):
    rows = pieces[0].shape[0]
    for k, block in enumerate(blocks):
        lanes = pl.ds(pl.multiple_of(block * local, local), local)
        mine = slice(k * local, (k + 1) * local)
        fill_rows(target, before[0, :, mine], 0, lanes, width)
        for row in range(rows):
            fill_rows(target, pieces[k][row], row + 1, lanes, width)
        fill_rows(target, after[0, :, mine], rows + 1, lanes, width)


def forward_kernel(n, bands, halves, place, *refs):
    pieces, refs = refs[:n], refs[n:]
    before, after, filters, bias = refs[:4]
    shares, refs = refs[4 : 4 + 2 * len(halves)], refs[4 + 2 * len(halves) :]
    outs, (weights, source, total) = refs[:n], refs[n:]
    me, band = place[0], place[1]
    taps, channels, local = filters.shape
    rows, padded, _ = pieces[0].shape
    width = padded - 2
    share = taps * channels // bands
    part = share // len(halves)
    for tap in range(taps):
        weights[pl.ds(tap * channels, channels), :local] = filters[tap]
    for h, order in enumerate(halves):
        for side in range(2):
            held = shares[2 * h + side]
            for j, d in enumerate(order):
                start = pl.multiple_of((band ^ (d | side)) * share + h * part, 32)
                for k in range(1, n):
                    weights[pl.ds(start, part), pl.ds(k * local, local)] = held[j, k - 1]
    fill_source(source, pieces, before, after, range(n), local, width)
    acc = None
    for a in range(3):
        for b in range(3):
            term = lax.dot_general(
                source[b, pl.ds(a * width, rows * width), :],
                weights[pl.ds((3 * a + b) * channels, channels), :],
                (((1,), (1,)), ((), ())),
                preferred_element_type=jnp.float32,
            )
            acc = term if acc is None else acc + term
    for j in range(n):
        total[j] = acc[:, j * local : (j + 1) * local]
    for k in range(n):
        value = total[me ^ k] + bias[k : k + 1, :].astype(jnp.float32)
        outs[k][...] = value.astype(jnp.bfloat16)


def backward_kernel(n, place, *refs):
    pieces, refs = refs[:n], refs[n:]
    before, after, weights = refs[:3]
    outs, (source,) = refs[3 : 3 + n], refs[3 + n :]
    me = place[0]
    rows, padded, local = pieces[0].shape
    width = padded - 2
    channels = n * local
    fill_source(source, pieces, before, after, [me ^ k for k in range(n)], local, width)
    acc = None
    for a in range(3):
        for b in range(3):
            term = jnp.dot(
                source[2 - b, pl.ds((2 - a) * width, rows * width), :],
                weights[pl.ds((3 * a + b) * channels, channels), :],
                preferred_element_type=jnp.float32,
            )
            acc = term if acc is None else acc + term
    for k in range(n):
        outs[k][...] = acc[:, k * local : (k + 1) * local].astype(jnp.bfloat16)


SMEM = pl.BlockSpec(memory_space=pltpu.SMEM)
VMEM = pl.BlockSpec(memory_space=pltpu.VMEM)
PARAMS = pltpu.CompilerParams(vmem_limit_bytes=40 * 2**20)


def forward(place, pieces, before, after, filters, bias, shares, halves, bands):
    n = len(pieces)
    rows, padded, local = pieces[0].shape
    width = padded - 2
    channels = filters.shape[1]
    args = [*pieces, before, after, filters, bias, *shares]
    out = jax.ShapeDtypeStruct((rows * width, local), jnp.bfloat16)
    return pl.pallas_call(
        lambda *refs: forward_kernel(n, bands, halves, *refs),
        out_shape=[out] * n
        + [jax.ShapeDtypeStruct((9 * channels, n * local), jnp.bfloat16)],
        in_specs=[SMEM] + [VMEM] * len(args),
        out_specs=[VMEM] * (n + 1),
        scratch_shapes=[
            pltpu.VMEM((3, (rows + 2) * width, n * local), jnp.bfloat16),
            pltpu.VMEM((n, rows * width, local), jnp.float32),
        ],
        compiler_params=PARAMS,
        cost_estimate=pl.CostEstimate(
            flops=18 * rows * width * channels * n * local,
            bytes_accessed=10 * 2**20,
            transcendentals=0,
        ),
        name="forward",
    )(place, *args)


def backward(place, pieces, before, after, weights):
    n = len(pieces)
    rows, padded, local = pieces[0].shape
    width = padded - 2
    args = [*pieces, before, after, weights]
    out = jax.ShapeDtypeStruct((rows * width, local), jnp.bfloat16)
    return pl.pallas_call(
        lambda *refs: backward_kernel(n, *refs),
        out_shape=[out] * n,
        in_specs=[SMEM] + [VMEM] * len(args),
        out_specs=[VMEM] * n,
        scratch_shapes=[pltpu.VMEM((3, (rows + 2) * width, n * local), jnp.bfloat16)],
        compiler_params=PARAMS,
        cost_estimate=pl.CostEstimate(
            flops=18 * rows * width * weights.shape[0] // 9 * n * local,
            bytes_accessed=6 * 2**20,
            transcendentals=0,
        ),
        name="backward",
    )(place, *args)


def xor_gather(value, axis, steps):
    held, order = [value], [0]
    for step in steps:
        there = swap(jnp.stack(held) if len(held) > 1 else held[0][None], axis, step)
        held = held + [there[j] for j in range(len(held))]
        order = order + [o ^ step for o in order]
    return held, order


def halving(size):
    steps = []
    while size > 1:
        size //= 2
        steps.append(size)
    return steps


def rims(pieces):
    first = jnp.concatenate([p[:1] for p in pieces], axis=2)
    last = jnp.concatenate([p[-1:] for p in pieces], axis=2)
    return neighbours(first, last)


def home(pieces, me, rows, width):
    whole = pick([p.reshape(rows, width, -1) for p in pieces], [me ^ k for k in range(len(pieces))], 1)
    return jnp.transpose(whole, (2, 0, 1))


def per_device(image, filters, bias, upstream):
    n = lax.axis_size("chan")
    bands = lax.axis_size("band")
    taps, outs, local = filters.shape
    rows = image.shape[1]
    width = image.shape[2] // n
    share = taps * outs // bands
    if local % 128 or width % 128 or share % 32 or bands < 4:
        return plain(image, filters, bias, upstream)
    me = lax.axis_index("chan")
    band = lax.axis_index("band")
    place = jnp.stack([me, band]).astype(jnp.int32)

    part = lax.dynamic_slice_in_dim(filters.reshape(-1, local), band * share, share, axis=0)
    part = jnp.concatenate([part, jnp.tile(bias[None], (16, 1))], axis=0)
    held, order = xor_gather(part, "chan", halving(n))
    held = [held[order.index(k)] for k in range(n)]
    biases = jnp.concatenate([h[share : share + 1] for h in held], axis=0)

    steps = halving(bands)[:-1]
    shares, halves = [], []
    for h, path in enumerate((steps, steps[::-1])):
        half = jnp.stack([p[h * share // 2 : (h + 1) * share // 2] for p in held[1:]])
        got, order = xor_gather(half, "band", path)
        got = jnp.stack(got)
        shares += [got, swap(got, "band", 1)]
        halves.append(order)

    x = spread(jnp.transpose(image, (1, 2, 0)), me, width)
    u = spread(jnp.transpose(upstream, (1, 2, 0)), me, width)

    *sent, weights = forward(place, x, *rims(x), filters, biases, shares, halves, bands)
    features = [swap(p, "chan", k) if k else p for k, p in enumerate(sent)]
    sent = backward(place, u, *rims(u), weights)
    image_grad = [swap(p, "chan", k) if k else p for k, p in enumerate(sent)]
    return home(features, me, rows, width), home(image_grad, me, rows, width)


def solution(mesh):
    return jax.shard_map(
        per_device,
        mesh=mesh,
        in_specs=(
            P("chan", "band", None),
            P(None, None, "chan"),
            P("chan"),
            P("chan", "band", None),
        ),
        out_specs=(P("chan", "band", None), P("chan", "band", None)),
        check_vma=False,
    )
```

```python
import jax
import jax.numpy as jnp
from jax import lax
from jax.experimental import pallas as pl
from jax.experimental.pallas import tpu as pltpu
from jax.sharding import PartitionSpec as P


def swap(value, axis, step):
    size = lax.axis_size(axis)
    return lax.ppermute(value, axis, [(j, j ^ step) for j in range(size)])


def neighbours(first, last):
    size = lax.axis_size("band")
    up = [(j, j + 1) for j in range(size - 1)]
    down = [(j + 1, j) for j in range(size - 1)]
    return lax.ppermute(last, "band", up), lax.ppermute(first, "band", down)


def pick(pieces, index, axis):
    stacked = jnp.stack(pieces)
    return jnp.concatenate(
        [lax.dynamic_index_in_dim(stacked, i, 0, keepdims=False) for i in index], axis=axis
    )


def spread(value, me, width):
    n = lax.axis_size("chan")
    padded = jnp.pad(value, ((0, 0), (1, 1), (0, 0)))
    pieces = []
    for k in range(n):
        piece = lax.dynamic_slice_in_dim(padded, (me ^ k) * width, width + 2, axis=1)
        pieces.append(swap(piece, "chan", k) if k else piece)
    return pieces


def add_rows(value):
    before, after = neighbours(value[:1], value[-1:])
    return jnp.concatenate([before, value, after], axis=0)


def conv(source, taps):
    return lax.conv_general_dilated(
        source[None],
        taps,
        (1, 1),
        "VALID",
        dimension_numbers=("NHWC", "HWIO", "NHWC"),
        preferred_element_type=jnp.float32,
    )[0]


def plain(image, filters, bias, upstream):
    n = lax.axis_size("chan")
    bands = lax.axis_size("band")
    me = lax.axis_index("chan")
    row = lax.axis_index("band")
    local = filters.shape[2]
    outs = filters.shape[1]
    width = image.shape[2] // n

    flat = filters.reshape(-1, local)
    share = flat.shape[0] // bands
    part = lax.dynamic_slice_in_dim(flat, row * share, share, axis=0)
    held = [jnp.concatenate([part, jnp.tile(bias[None], (16, 1))], axis=0)]
    step = n // 2
    while step:
        stacked = jnp.stack(held)
        there = swap(stacked, "chan", step)
        held = held + [there[j] for j in range(len(held))]
        step //= 2
    order = [0]
    step = n // 2
    while step:
        order = order + [o ^ step for o in order]
        step //= 2
    held = [held[order.index(k)] for k in range(n)]
    biases = [h[share] for h in held]
    whole = lax.all_gather(
        jnp.stack([h[:share] for h in held]), "band", axis=1, tiled=True
    ).reshape(n, 3, 3, outs, local)

    x_pieces = spread(jnp.transpose(image, (1, 2, 0)), me, width)
    u_pieces = spread(jnp.transpose(upstream, (1, 2, 0)), me, width)

    natural = [me ^ k for k in range(n)]
    x = add_rows(jnp.concatenate(x_pieces, axis=2))
    forward_taps = jnp.transpose(whole, (1, 2, 0, 4, 3)).reshape(3, 3, n * local, outs)
    total = conv(x, forward_taps) + pick(biases, natural, 0).astype(jnp.float32)
    features = back(total.astype(jnp.bfloat16), me, local, True)

    u = add_rows(pick(u_pieces, natural, 2))
    backward_taps = jnp.transpose(whole[:, ::-1, ::-1], (1, 2, 3, 0, 4)).reshape(
        3, 3, outs, n * local
    )
    image_grad = back(conv(u, backward_taps).astype(jnp.bfloat16), me, local, False)
    return features, image_grad


def back(value, me, local, is_natural):
    n = lax.axis_size("chan")
    pieces = []
    for k in range(n):
        start = (me ^ k) * local if is_natural else k * local
        piece = lax.dynamic_slice_in_dim(value, start, local, axis=2)
        pieces.append(swap(piece, "chan", k) if k else piece)
    whole = pick(pieces, [me ^ k for k in range(n)], 1)
    return jnp.transpose(whole, (2, 0, 1))


def fill_rows(target, piece, row, lanes, width):
    for shift in range(3):
        target[shift, pl.ds(row * width, width), lanes] = piece[shift : shift + width, :]


def fill_source(target, pieces, before, after, blocks, local, width):
    rows = pieces[0].shape[0]
    for k, block in enumerate(blocks):
        lanes = pl.ds(pl.multiple_of(block * local, local), local)
        mine = slice(k * local, (k + 1) * local)
        fill_rows(target, before[0, :, mine], 0, lanes, width)
        for row in range(rows):
            fill_rows(target, pieces[k][row], row + 1, lanes, width)
        fill_rows(target, after[0, :, mine], rows + 1, lanes, width)


def forward_kernel(n, bands, halves, place, *refs):
    pieces, refs = refs[:n], refs[n:]
    before, after, filters = refs[:3]
    shares, refs = refs[3 : 3 + 2 * len(halves)], refs[3 + 2 * len(halves) :]
    outs, (weights, source, total) = refs[:n], refs[n:]
    me, band = place[0], place[1]
    taps, channels, local = filters.shape
    rows, padded, _ = pieces[0].shape
    width = padded - 3
    share = taps * channels // bands
    part = share // len(halves)
    for tap in range(taps):
        weights[pl.ds(tap * channels, channels), :local] = filters[tap]
    for h, order in enumerate(halves):
        for side in range(2):
            held = shares[2 * h + side]
            for j, d in enumerate(order):
                start = pl.multiple_of((band ^ (d | side)) * share + h * part, 32)
                for k in range(1, n):
                    weights[pl.ds(start, part), pl.ds(k * local, local)] = held[j, k - 1]
    fill_source(source, pieces, before, after, range(n), local, width)
    acc = None
    for a in range(3):
        for b in range(3):
            term = lax.dot_general(
                source[b, pl.ds(a * width, rows * width), :],
                weights[pl.ds((3 * a + b) * channels, channels), :],
                (((1,), (1,)), ((), ())),
                preferred_element_type=jnp.float32,
            )
            acc = term if acc is None else acc + term
    for j in range(n):
        total[j] = acc[:, j * local : (j + 1) * local]
    for k in range(n):
        bias = pieces[k][0, padded - 1 : padded, :].astype(jnp.float32)
        value = total[me ^ k] + bias
        outs[k][...] = value.astype(jnp.bfloat16)


def backward_kernel(n, place, *refs):
    pieces, refs = refs[:n], refs[n:]
    before, after, weights = refs[:3]
    outs, (source,) = refs[3 : 3 + n], refs[3 + n :]
    me = place[0]
    rows, padded, local = pieces[0].shape
    width = padded - 3
    channels = n * local
    fill_source(source, pieces, before, after, [me ^ k for k in range(n)], local, width)
    acc = None
    for a in range(3):
        for b in range(3):
            term = jnp.dot(
                source[2 - b, pl.ds((2 - a) * width, rows * width), :],
                weights[pl.ds((3 * a + b) * channels, channels), :],
                preferred_element_type=jnp.float32,
            )
            acc = term if acc is None else acc + term
    for k in range(n):
        outs[k][...] = acc[:, k * local : (k + 1) * local].astype(jnp.bfloat16)


SMEM = pl.BlockSpec(memory_space=pltpu.SMEM)
VMEM = pl.BlockSpec(memory_space=pltpu.VMEM)
PARAMS = pltpu.CompilerParams(vmem_limit_bytes=40 * 2**20)


def forward(place, pieces, before, after, filters, shares, halves, bands):
    n = len(pieces)
    rows, padded, local = pieces[0].shape
    width = padded - 3
    channels = filters.shape[1]
    args = [*pieces, before, after, filters, *shares]
    out = jax.ShapeDtypeStruct((rows * width, local), jnp.bfloat16)
    return pl.pallas_call(
        lambda *refs: forward_kernel(n, bands, halves, *refs),
        out_shape=[out] * n
        + [jax.ShapeDtypeStruct((9 * channels, n * local), jnp.bfloat16)],
        in_specs=[SMEM] + [VMEM] * len(args),
        out_specs=[VMEM] * (n + 1),
        scratch_shapes=[
            pltpu.VMEM((3, (rows + 2) * width, n * local), jnp.bfloat16),
            pltpu.VMEM((n, rows * width, local), jnp.float32),
        ],
        compiler_params=PARAMS,
        cost_estimate=pl.CostEstimate(
            flops=18 * rows * width * channels * n * local,
            bytes_accessed=10 * 2**20,
            transcendentals=0,
        ),
        name="forward",
    )(place, *args)


def backward(place, pieces, before, after, weights):
    n = len(pieces)
    rows, padded, local = pieces[0].shape
    width = padded - 3
    args = [*pieces, before, after, weights]
    out = jax.ShapeDtypeStruct((rows * width, local), jnp.bfloat16)
    return pl.pallas_call(
        lambda *refs: backward_kernel(n, *refs),
        out_shape=[out] * n,
        in_specs=[SMEM] + [VMEM] * len(args),
        out_specs=[VMEM] * n,
        scratch_shapes=[pltpu.VMEM((3, (rows + 2) * width, n * local), jnp.bfloat16)],
        compiler_params=PARAMS,
        cost_estimate=pl.CostEstimate(
            flops=18 * rows * width * weights.shape[0] // 9 * n * local,
            bytes_accessed=6 * 2**20,
            transcendentals=0,
        ),
        name="backward",
    )(place, *args)


def cut(value, bias, me, n):
    width = value.shape[2] // n
    padded = jnp.pad(jnp.transpose(value, (1, 2, 0)), ((0, 0), (1, 1), (0, 0)))
    extra = jnp.broadcast_to(bias, (value.shape[1], 1, value.shape[0]))
    return [
        jnp.concatenate(
            [lax.dynamic_slice_in_dim(padded, (me ^ k) * width, width + 2, axis=1), extra], axis=1
        )
        for k in range(n)
    ]


def exchange(pieces):
    far = [swap(pieces[k], "chan", k) for k in range(len(pieces) - 1, 0, -1)]
    return [pieces[0]] + far[::-1]


def xor_gather(value, axis, steps):
    held, order = [value], [0]
    for step in steps:
        there = swap(jnp.stack(held) if len(held) > 1 else held[0][None], axis, step)
        held = held + [there[j] for j in range(len(held))]
        order = order + [o ^ step for o in order]
    return held, order


def halving(size):
    steps = []
    while size > 1:
        size //= 2
        steps.append(size)
    return steps


def rims(pieces):
    first = jnp.concatenate([p[:1] for p in pieces], axis=2)
    last = jnp.concatenate([p[-1:] for p in pieces], axis=2)
    return neighbours(first, last)


def home(pieces, me, rows, width):
    whole = pick([p.reshape(rows, width, -1) for p in pieces], [me ^ k for k in range(len(pieces))], 1)
    return jnp.transpose(whole, (2, 0, 1))


def per_device(image, filters, bias, upstream):
    n = lax.axis_size("chan")
    bands = lax.axis_size("band")
    taps, outs, local = filters.shape
    rows = image.shape[1]
    width = image.shape[2] // n
    share = taps * outs // bands
    if local % 128 or width % 128 or share % 32 or bands < 4:
        return plain(image, filters, bias, upstream)
    me = lax.axis_index("chan")
    band = lax.axis_index("band")
    place = jnp.stack([me, band]).astype(jnp.int32)

    flat = filters.reshape(-1, local)
    held = [lax.dynamic_slice_in_dim(flat, band * share, share, axis=0)]
    x = cut(image, bias, me, n)
    u = cut(upstream, bias, me, n)
    order = [0]
    for step in halving(n):
        there = swap(jnp.stack(held), "chan", step)
        there, x = lax.optimization_barrier((there, x))
        held = held + [there[j] for j in range(len(held))]
        order = order + [o ^ step for o in order]
    held = [held[order.index(k)] for k in range(1, n)]
    held, u = lax.optimization_barrier((held, u))
    x = exchange(x)

    steps = halving(bands)[:-1]
    shares, halves = [], []
    for h, path in enumerate((steps, steps[::-1])):
        half = jnp.stack([p[h * share // 2 : (h + 1) * share // 2] for p in held])
        got, order = xor_gather(half, "band", path)
        got = jnp.stack(got)
        shares += [got, swap(got, "band", 1)]
        halves.append(order)

    u[0], x[1] = lax.optimization_barrier((u[0], x[1]))
    u = exchange(u)

    *sent, weights = forward(place, x, *rims(x), filters, shares, halves, bands)
    features = exchange(sent)
    sent = backward(place, u, *rims(u), weights)
    sent, features[1] = lax.optimization_barrier((sent, features[1]))
    image_grad = exchange(sent)
    return home(features, me, rows, width), home(image_grad, me, rows, width)


def solution(mesh):
    return jax.shard_map(
        per_device,
        mesh=mesh,
        in_specs=(
            P("chan", "band", None),
            P(None, None, "chan"),
            P("chan"),
            P("chan", "band", None),
        ),
        out_specs=(P("chan", "band", None), P("chan", "band", None)),
        check_vma=False,
    )
```

```python
import jax
import jax.numpy as jnp
from jax import lax
from jax.experimental import pallas as pl
from jax.experimental.pallas import tpu as pltpu
from jax.sharding import PartitionSpec as P


def swap(value, axis, step):
    size = lax.axis_size(axis)
    return lax.ppermute(value, axis, [(j, j ^ step) for j in range(size)])


def neighbours(first, last):
    size = lax.axis_size("band")
    up = [(j, j + 1) for j in range(size - 1)]
    down = [(j + 1, j) for j in range(size - 1)]
    return lax.ppermute(last, "band", up), lax.ppermute(first, "band", down)


def pick(pieces, index, axis):
    stacked = jnp.stack(pieces)
    return jnp.concatenate(
        [lax.dynamic_index_in_dim(stacked, i, 0, keepdims=False) for i in index], axis=axis
    )


def spread(value, me, width):
    n = lax.axis_size("chan")
    padded = jnp.pad(value, ((0, 0), (1, 1), (0, 0)))
    pieces = []
    for k in range(n):
        piece = lax.dynamic_slice_in_dim(padded, (me ^ k) * width, width + 2, axis=1)
        pieces.append(swap(piece, "chan", k) if k else piece)
    return pieces


def add_rows(value):
    before, after = neighbours(value[:1], value[-1:])
    return jnp.concatenate([before, value, after], axis=0)


def conv(source, taps):
    return lax.conv_general_dilated(
        source[None],
        taps,
        (1, 1),
        "VALID",
        dimension_numbers=("NHWC", "HWIO", "NHWC"),
        preferred_element_type=jnp.float32,
    )[0]


def plain(image, filters, bias, upstream):
    n = lax.axis_size("chan")
    bands = lax.axis_size("band")
    me = lax.axis_index("chan")
    row = lax.axis_index("band")
    local = filters.shape[2]
    outs = filters.shape[1]
    width = image.shape[2] // n

    flat = filters.reshape(-1, local)
    share = flat.shape[0] // bands
    part = lax.dynamic_slice_in_dim(flat, row * share, share, axis=0)
    held = [jnp.concatenate([part, jnp.tile(bias[None], (16, 1))], axis=0)]
    step = n // 2
    while step:
        stacked = jnp.stack(held)
        there = swap(stacked, "chan", step)
        held = held + [there[j] for j in range(len(held))]
        step //= 2
    order = [0]
    step = n // 2
    while step:
        order = order + [o ^ step for o in order]
        step //= 2
    held = [held[order.index(k)] for k in range(n)]
    biases = [h[share] for h in held]
    whole = lax.all_gather(
        jnp.stack([h[:share] for h in held]), "band", axis=1, tiled=True
    ).reshape(n, 3, 3, outs, local)

    x_pieces = spread(jnp.transpose(image, (1, 2, 0)), me, width)
    u_pieces = spread(jnp.transpose(upstream, (1, 2, 0)), me, width)

    natural = [me ^ k for k in range(n)]
    x = add_rows(jnp.concatenate(x_pieces, axis=2))
    forward_taps = jnp.transpose(whole, (1, 2, 0, 4, 3)).reshape(3, 3, n * local, outs)
    total = conv(x, forward_taps) + pick(biases, natural, 0).astype(jnp.float32)
    features = back(total.astype(jnp.bfloat16), me, local, True)

    u = add_rows(pick(u_pieces, natural, 2))
    backward_taps = jnp.transpose(whole[:, ::-1, ::-1], (1, 2, 3, 0, 4)).reshape(
        3, 3, outs, n * local
    )
    image_grad = back(conv(u, backward_taps).astype(jnp.bfloat16), me, local, False)
    return features, image_grad


def back(value, me, local, is_natural):
    n = lax.axis_size("chan")
    pieces = []
    for k in range(n):
        start = (me ^ k) * local if is_natural else k * local
        piece = lax.dynamic_slice_in_dim(value, start, local, axis=2)
        pieces.append(swap(piece, "chan", k) if k else piece)
    whole = pick(pieces, [me ^ k for k in range(n)], 1)
    return jnp.transpose(whole, (2, 0, 1))


def fill_rows(target, piece, row, lanes, width):
    for shift in range(3):
        target[shift, pl.ds(row * width, width), lanes] = piece[shift : shift + width, :]


def fill_source(target, pieces, before, after, width):
    rows, _, local = pieces[0].shape
    for k, piece in enumerate(pieces):
        lanes = slice(k * local, (k + 1) * local)
        fill_rows(target, before[0, :, lanes], 0, lanes, width)
        for row in range(rows):
            fill_rows(target, piece[row], row + 1, lanes, width)
        fill_rows(target, after[0, :, lanes], rows + 1, lanes, width)


def backward_kernel(order, place, *refs):
    pieces, (before, after, filters, near, far), refs = refs[:4], refs[4:9], refs[9:]
    mine, other, weights, source = refs
    me, band = place[0], place[1]
    taps, channels, local = filters.shape
    rows = pieces[0].shape[0]
    width = pieces[0].shape[1] - 3
    share = near.shape[2]
    for tap in range(taps):
        for j in range(4):
            start = pl.multiple_of((me ^ j) * local, local)
            weights[pl.ds(tap * channels + j * local, local), :local] = filters[
                tap, pl.ds(start, local), :
            ]
    for bit, held in enumerate((near, far)):
        for j, d in enumerate(order):
            first = (band ^ (d | bit)) * share
            block = lax.div(first, local)
            start = (block ^ me) * local + first - block * local
            for tap in range(taps):
                place_row = pl.multiple_of(tap * channels + start, 16)
                weights[pl.ds(place_row, share), local:] = held[j, tap]
    fill_source(source, pieces, before, after, width)
    acc = None
    for a in range(3):
        for b in range(3):
            term = jnp.dot(
                source[2 - b, pl.ds((2 - a) * width, rows * width), :],
                weights[pl.ds((3 * a + b) * channels, channels), :],
                preferred_element_type=jnp.float32,
            )
            acc = term if acc is None else acc + term
    mine[...] = acc[:, :local].astype(jnp.bfloat16)
    other[...] = acc[:, local:].astype(jnp.bfloat16)


def forward_kernel(order, place, *refs):
    pieces, (before, after, weights, near, far), refs = refs[:4], refs[4:9], refs[9:]
    mine, other, extra, source = refs
    me, band = place[0], place[1]
    rows, padded, local = pieces[0].shape
    width = padded - 3
    taps = 9
    channels = weights.shape[0] // taps
    share = near.shape[3]
    half = 2 * local
    for bit, held in enumerate((near, far)):
        for j, d in enumerate(order):
            first = (band ^ (d | bit)) * share
            block = lax.div(first, local)
            start = (block ^ (me & 1)) * local + first - block * local
            for tap in range(taps):
                place_row = pl.multiple_of(tap * half + start, 16)
                for k in range(2):
                    extra[pl.ds(place_row, share), k * local : (k + 1) * local] = held[j, k, tap]
    fill_source(source, pieces, before, after, width)
    acc = None
    for a in range(3):
        for b in range(3):
            tap = 3 * a + b
            for part in range(2):
                if part:
                    filters = extra[pl.ds(tap * half, half), :]
                else:
                    filters = weights[pl.ds(tap * channels, half), :]
                term = lax.dot_general(
                    source[b, pl.ds(a * width, rows * width), part * half : (part + 1) * half],
                    filters,
                    (((1,), (1,)), ((), ())),
                    preferred_element_type=jnp.float32,
                )
                acc = term if acc is None else acc + term
    for k, out in enumerate((mine, other)):
        bias = pieces[k][0, padded - 1 : padded, :].astype(jnp.float32)
        out[...] = (acc[:, k * local : (k + 1) * local] + bias).astype(jnp.bfloat16)


SMEM = pl.BlockSpec(memory_space=pltpu.SMEM)
VMEM = pl.BlockSpec(memory_space=pltpu.VMEM)


def kernel_call(body, order, place, args, outs, scratch, name):
    rows, padded, local = args[0].shape
    width = padded - 3
    return pl.pallas_call(
        lambda *refs: body(order, *refs),
        out_shape=[jax.ShapeDtypeStruct((rows * width, local), jnp.bfloat16)] * 2 + outs,
        in_specs=[SMEM] + [VMEM] * len(args),
        out_specs=[VMEM] * (2 + len(outs)),
        scratch_shapes=scratch
        + [pltpu.VMEM((3, (rows + 2) * width, 4 * local), jnp.bfloat16)],
        compiler_params=pltpu.CompilerParams(vmem_limit_bytes=40 * 2**20),
        cost_estimate=pl.CostEstimate(
            flops=18 * rows * width * 8 * local * local,
            bytes_accessed=8 * 2**20,
            transcendentals=0,
        ),
        name=name,
    )(place, *args)


def cut(value, bias, side):
    rows, local = value.shape[1], value.shape[0]
    width = value.shape[2] // 2
    padded = jnp.pad(jnp.transpose(value, (1, 2, 0)), ((0, 0), (1, 1), (0, 0)))
    extra = jnp.broadcast_to(bias, (rows, 1, local))
    return [
        jnp.concatenate(
            [lax.dynamic_slice_in_dim(padded, (side ^ k) * width, width + 2, axis=1), extra], axis=1
        )
        for k in range(2)
    ]


def exchange(mine, other):
    far = swap(other, "chan", 3)
    middle = swap(mine, "chan", 2)
    return [mine, swap(other, "chan", 1), middle, far]


def rims(pieces):
    first = jnp.concatenate([p[:1] for p in pieces], axis=2)
    last = jnp.concatenate([p[-1:] for p in pieces], axis=2)
    return neighbours(first, last)


def after(value, *others):
    return lax.optimization_barrier((value, others))[0]


def gather(value):
    bands = lax.axis_size("band")
    order = list(range(0, bands, 2))
    held = jnp.stack([swap(value, "band", d) if d else value for d in order])
    return held, swap(held, "band", 1), order


def home(mine, other, side, rows):
    mine = mine.reshape(rows, -1, mine.shape[1])
    other = other.reshape(mine.shape)
    first = jnp.where(side == 0, mine, other)
    second = jnp.where(side == 0, other, mine)
    return jnp.transpose(jnp.concatenate([first, second], axis=1), (2, 0, 1))


def per_device(image, filters, bias, upstream):
    n = lax.axis_size("chan")
    bands = lax.axis_size("band")
    taps, outs, local = filters.shape
    rows = image.shape[1]
    if n != 4 or local % 128 or image.shape[2] % 256 or outs % (32 * bands) or bands < 4:
        return plain(image, filters, bias, upstream)
    me = lax.axis_index("chan")
    band = lax.axis_index("band")
    side, half = me & 1, me >> 1
    place = jnp.stack([me, band]).astype(jnp.int32)

    share = outs // bands
    part = lax.dynamic_slice_in_dim(filters, band * share, share, axis=1)
    start = (1 - half) * (outs // 2) + band * (share // 2)
    part_across = lax.dynamic_slice_in_dim(filters, start, share // 2, axis=1)
    near = swap(part, "chan", 1)
    across = swap(part_across, "chan", 2)

    u = exchange(*after(cut(upstream, bias, side), part, part_across))
    held, there, order = gather(near)

    mine, other, weights = kernel_call(
        backward_kernel,
        order,
        place,
        [*u, *rims(u), filters, held, there],
        [jax.ShapeDtypeStruct((taps * outs, 2 * local), jnp.bfloat16)],
        [],
        "backward",
    )
    image_grad = home(mine, swap(other, "chan", 1), side, rows)

    x = exchange(*after(cut(image, bias, side), u[1]))
    across = after(jnp.stack([across, swap(across, "chan", 1)]), held)
    held, there, order = gather(across)
    x = after(x, mine)
    mine, other = kernel_call(
        forward_kernel,
        order,
        place,
        [*x, *rims(x), weights, held, there],
        [],
        [pltpu.VMEM((taps * 2 * local, 2 * local), jnp.bfloat16)],
        "forward",
    )
    return home(mine, swap(other, "chan", 1), side, rows), image_grad


def solution(mesh):
    return jax.shard_map(
        per_device,
        mesh=mesh,
        in_specs=(
            P("chan", "band", None),
            P(None, None, "chan"),
            P("chan"),
            P("chan", "band", None),
        ),
        out_specs=(P("chan", "band", None), P("chan", "band", None)),
        check_vma=False,
    )
```

```python
import jax
import jax.numpy as jnp
from jax import lax
from jax.experimental import pallas as pl
from jax.experimental.pallas import tpu as pltpu
from jax.sharding import PartitionSpec as P


def swap(value, axis, step):
    size = lax.axis_size(axis)
    return lax.ppermute(value, axis, [(j, j ^ step) for j in range(size)])


def neighbours(first, last):
    size = lax.axis_size("band")
    up = [(j, j + 1) for j in range(size - 1)]
    down = [(j + 1, j) for j in range(size - 1)]
    return lax.ppermute(last, "band", up), lax.ppermute(first, "band", down)


def pick(pieces, index, axis):
    stacked = jnp.stack(pieces)
    return jnp.concatenate(
        [lax.dynamic_index_in_dim(stacked, i, 0, keepdims=False) for i in index], axis=axis
    )


def spread(value, me, width):
    n = lax.axis_size("chan")
    padded = jnp.pad(value, ((0, 0), (1, 1), (0, 0)))
    pieces = []
    for k in range(n):
        piece = lax.dynamic_slice_in_dim(padded, (me ^ k) * width, width + 2, axis=1)
        pieces.append(swap(piece, "chan", k) if k else piece)
    return pieces


def add_rows(value):
    before, after = neighbours(value[:1], value[-1:])
    return jnp.concatenate([before, value, after], axis=0)


def conv(source, taps):
    return lax.conv_general_dilated(
        source[None],
        taps,
        (1, 1),
        "VALID",
        dimension_numbers=("NHWC", "HWIO", "NHWC"),
        preferred_element_type=jnp.float32,
    )[0]


def plain(image, filters, bias, upstream):
    n = lax.axis_size("chan")
    bands = lax.axis_size("band")
    me = lax.axis_index("chan")
    row = lax.axis_index("band")
    local = filters.shape[2]
    outs = filters.shape[1]
    width = image.shape[2] // n

    flat = filters.reshape(-1, local)
    share = flat.shape[0] // bands
    part = lax.dynamic_slice_in_dim(flat, row * share, share, axis=0)
    held = [jnp.concatenate([part, jnp.tile(bias[None], (16, 1))], axis=0)]
    step = n // 2
    while step:
        stacked = jnp.stack(held)
        there = swap(stacked, "chan", step)
        held = held + [there[j] for j in range(len(held))]
        step //= 2
    order = [0]
    step = n // 2
    while step:
        order = order + [o ^ step for o in order]
        step //= 2
    held = [held[order.index(k)] for k in range(n)]
    biases = [h[share] for h in held]
    whole = lax.all_gather(
        jnp.stack([h[:share] for h in held]), "band", axis=1, tiled=True
    ).reshape(n, 3, 3, outs, local)

    x_pieces = spread(jnp.transpose(image, (1, 2, 0)), me, width)
    u_pieces = spread(jnp.transpose(upstream, (1, 2, 0)), me, width)

    natural = [me ^ k for k in range(n)]
    x = add_rows(jnp.concatenate(x_pieces, axis=2))
    forward_taps = jnp.transpose(whole, (1, 2, 0, 4, 3)).reshape(3, 3, n * local, outs)
    total = conv(x, forward_taps) + pick(biases, natural, 0).astype(jnp.float32)
    features = back(total.astype(jnp.bfloat16), me, local, True)

    u = add_rows(pick(u_pieces, natural, 2))
    backward_taps = jnp.transpose(whole[:, ::-1, ::-1], (1, 2, 3, 0, 4)).reshape(
        3, 3, outs, n * local
    )
    image_grad = back(conv(u, backward_taps).astype(jnp.bfloat16), me, local, False)
    return features, image_grad


def back(value, me, local, is_natural):
    n = lax.axis_size("chan")
    pieces = []
    for k in range(n):
        start = (me ^ k) * local if is_natural else k * local
        piece = lax.dynamic_slice_in_dim(value, start, local, axis=2)
        pieces.append(swap(piece, "chan", k) if k else piece)
    whole = pick(pieces, [me ^ k for k in range(n)], 1)
    return jnp.transpose(whole, (2, 0, 1))


def assemble_kernel(order, place, filters, near, far, weights, extra):
    me, band = place[0], place[1]
    taps, channels, local = filters.shape
    share = near.shape[1] // (2 * taps)
    half = share // 2
    for tap in range(taps):
        for j in range(4):
            start = pl.multiple_of((me ^ j) * local, local)
            weights[pl.ds(tap * channels + j * local, local), :local] = filters[
                tap, pl.ds(start, local), :
            ]
    for bit, held in enumerate((near, far)):
        for j, d in enumerate(order):
            first = (band ^ (d | bit)) * share
            block = lax.div(first, local)
            start = (block ^ me) * local + first - block * local
            for tap in range(taps):
                row = pl.multiple_of(tap * channels + start, 16)
                weights[pl.ds(row, share), local:] = held[j, tap * share : (tap + 1) * share]
            first = (band ^ (d | bit)) * half
            block = lax.div(first, local)
            start = (block ^ (me & 1)) * local + first - block * local
            for tap in range(taps):
                row = pl.multiple_of(tap * 2 * local + start, 16)
                for k in range(2):
                    at = taps * share + (k * taps + tap) * half
                    extra[pl.ds(row, half), k * local : (k + 1) * local] = held[j, at : at + half]


def fill_rows(target, piece, start, row, lanes, width):
    for shift in range(3):
        target[shift, pl.ds(row * width, width), lanes] = piece[
            start + shift : start + shift + width, :
        ]


def fill_source(target, pieces, before, after, which, rows, width):
    pitch = width + 8
    local = before.shape[1]
    for k, piece in enumerate(pieces):
        lanes = slice(k * local, (k + 1) * local)
        rim = (2 * k + which) * pitch
        fill_rows(target, before, rim, 0, lanes, width)
        for row in range(rows):
            fill_rows(target, piece, (which * rows + row) * pitch, row + 1, lanes, width)
        fill_rows(target, after, rim, rows + 1, lanes, width)


def conv_kernel(rows, width, *refs):
    pieces, (before, after, weights, extra), refs = refs[:4], refs[4:8], refs[8:]
    grad, feat, other, upstream, image = refs
    size, local = grad.shape
    channels, half = 4 * local, 2 * local
    fill_source(upstream, pieces, before, after, 0, rows, width)
    acc = None
    for a in range(3):
        for b in range(3):
            term = jnp.dot(
                upstream[2 - b, pl.ds((2 - a) * width, size), :],
                weights[pl.ds((3 * a + b) * channels, channels), :],
                preferred_element_type=jnp.float32,
            )
            acc = term if acc is None else acc + term
    grad[...] = acc[:, :local].astype(jnp.bfloat16)
    other[:size] = acc[:, local:].astype(jnp.bfloat16)
    fill_source(image, pieces, before, after, 1, rows, width)
    acc = None
    for a in range(3):
        for b in range(3):
            tap = 3 * a + b
            for part in range(2):
                if part:
                    filters = extra[pl.ds(tap * half, half), :]
                else:
                    filters = weights[pl.ds(tap * channels, half), :]
                term = lax.dot_general(
                    image[b, pl.ds(a * width, size), part * half : (part + 1) * half],
                    filters,
                    (((1,), (1,)), ((), ())),
                    preferred_element_type=jnp.float32,
                )
                acc = term if acc is None else acc + term
    bias = [p[rows * (width + 8) + width + 2 :][:1].astype(jnp.float32) for p in pieces[:2]]
    feat[...] = (acc[:, :local] + bias[0]).astype(jnp.bfloat16)
    other[size:] = (acc[:, local:] + bias[1]).astype(jnp.bfloat16)


SMEM = pl.BlockSpec(memory_space=pltpu.SMEM)
VMEM = pl.BlockSpec(memory_space=pltpu.VMEM)
COST = pl.CostEstimate(flops=2**20, bytes_accessed=2**20, transcendentals=0)
PARAMS = pltpu.CompilerParams(vmem_limit_bytes=32 * 2**20)


def assemble(order, place, filters, near, far):
    taps, channels, local = filters.shape
    return pl.pallas_call(
        lambda *refs: assemble_kernel(order, *refs),
        out_shape=[
            jax.ShapeDtypeStruct((taps * channels, 2 * local), jnp.bfloat16),
            jax.ShapeDtypeStruct((taps * 2 * local, 2 * local), jnp.bfloat16),
        ],
        in_specs=[SMEM] + [VMEM] * 3,
        out_specs=[VMEM] * 2,
        compiler_params=PARAMS,
        cost_estimate=COST,
        name="assemble",
    )(place, filters, near, far)


def convolve(rows, width, pieces, before, after, weights, extra):
    local = pieces[0].shape[1]
    size = rows * width
    args = [*pieces, before, after, weights, extra]
    return pl.pallas_call(
        lambda *refs: conv_kernel(rows, width, *refs),
        out_shape=[
            jax.ShapeDtypeStruct((n * size, local), jnp.bfloat16) for n in (1, 1, 2)
        ],
        in_specs=[VMEM] * len(args),
        out_specs=[VMEM] * 3,
        scratch_shapes=[pltpu.VMEM((3, (rows + 2) * width, 4 * local), jnp.bfloat16)] * 2,
        compiler_params=PARAMS,
        cost_estimate=COST,
        name="conv",
    )(*args)


def channels_last(value):
    return jnp.pad(jnp.transpose(value, (1, 2, 0)), ((0, 0), (1, 1), (0, 0)))


def cut(value, bias, start, width):
    rows, _, local = value.shape
    extra = jnp.broadcast_to(bias, (rows, 6, local))
    piece = lax.dynamic_slice_in_dim(value, start, width + 2, axis=1)
    return jnp.concatenate([piece, extra], axis=1).reshape(-1, local)


def exchange(mine, near, middle, far):
    far = swap(far, "chan", 3)
    middle = swap(middle, "chan", 2)
    return [mine, swap(near, "chan", 1), middle, far]


def rims(pieces, pitch):
    rows = pieces[0].shape[0] // (2 * pitch)
    row = lambda p, at: p[at * pitch : (at + 1) * pitch]
    first = jnp.concatenate([row(p, i * rows) for p in pieces for i in range(2)])
    last = jnp.concatenate([row(p, i * rows + rows - 1) for p in pieces for i in range(2)])
    return neighbours(first, last)


def after(value, *others):
    return lax.optimization_barrier((value, others))[0]


def gather(value):
    bands = lax.axis_size("band")
    order = list(range(0, bands, 2))
    held = jnp.stack([swap(value, "band", d) if d else value for d in order])
    return held, swap(held, "band", 1), order


def home(mine, other, side, rows):
    turn = lambda p: jnp.transpose(p.reshape(rows, -1, p.shape[1]), (2, 0, 1))
    mine = jnp.concatenate([turn(p) for p in mine], axis=2)
    other = jnp.concatenate([turn(p) for p in other], axis=2)
    first = jnp.where(side == 0, mine, other)
    second = jnp.where(side == 0, other, mine)
    return jnp.concatenate([first, second], axis=2)


CHUNKS = 2


def per_device(image, filters, bias, upstream):
    n = lax.axis_size("chan")
    bands = lax.axis_size("band")
    taps, outs, local = filters.shape
    rows, cols = image.shape[1:]
    if n != 4 or local % 128 or cols % (256 * CHUNKS) or outs % (32 * bands) or bands < 4:
        return plain(image, filters, bias, upstream)
    me = lax.axis_index("chan")
    band = lax.axis_index("band")
    side, half = me & 1, me >> 1
    place = jnp.stack([me, band]).astype(jnp.int32)
    width = cols // (2 * CHUNKS)
    pitch = width + 8

    share = outs // bands
    near = lax.dynamic_slice_in_dim(filters, band * share, share, axis=1).reshape(-1, local)
    start = (1 - half) * (outs // 2) + band * (share // 2)
    across = lax.dynamic_slice_in_dim(filters, start, share // 2, axis=1).reshape(-1, local)
    parts = [swap(near, "chan", 1), swap(across, "chan", 2), swap(across, "chan", 3)]

    full = [channels_last(upstream), channels_last(image)]
    payloads = []
    for chunk in range(CHUNKS):
        starts = [(side ^ k) * (cols // 2) + chunk * width for k in range(2)]
        payloads.append(
            [jnp.concatenate([cut(v, bias, at, width) for v in full]) for at in starts]
        )
    payloads[0] = after(payloads[0], near, across)
    got = []
    for mine, other in payloads:
        if got:
            mine, other = after((mine, other), got[-1][2])
        got.append(exchange(mine, other, mine, other))

    held, there, order = gather(jnp.concatenate(parts))
    weights, extra = assemble(order, place, filters, held, there)

    mine, other = [[], []], [[], []]
    for pieces in got:
        if mine[0]:
            pieces = after(pieces, mine[0][-1])
        grad, feat, sent = convolve(rows, width, pieces, *rims(pieces, pitch), weights, extra)
        sent = swap(sent, "chan", 1)
        size = grad.shape[0]
        for i, (kept, come) in enumerate(((grad, sent[:size]), (feat, sent[size:]))):
            mine[i].append(kept)
            other[i].append(come)
    return home(mine[1], other[1], side, rows), home(mine[0], other[0], side, rows)


def solution(mesh):
    return jax.shard_map(
        per_device,
        mesh=mesh,
        in_specs=(
            P("chan", "band", None),
            P(None, None, "chan"),
            P("chan"),
            P("chan", "band", None),
        ),
        out_specs=(P("chan", "band", None), P("chan", "band", None)),
        check_vma=False,
    )
```

```python
import jax
import jax.numpy as jnp
from jax import lax
from jax.experimental import pallas as pl
from jax.experimental.pallas import tpu as pltpu
from jax.sharding import PartitionSpec as P


def swap(value, axis, step):
    size = lax.axis_size(axis)
    return lax.ppermute(value, axis, [(j, j ^ step) for j in range(size)])


def neighbours(first, last):
    size = lax.axis_size("band")
    up = [(j, j + 1) for j in range(size - 1)]
    down = [(j + 1, j) for j in range(size - 1)]
    return lax.ppermute(last, "band", up), lax.ppermute(first, "band", down)


def pick(pieces, index, axis):
    stacked = jnp.stack(pieces)
    return jnp.concatenate(
        [lax.dynamic_index_in_dim(stacked, i, 0, keepdims=False) for i in index], axis=axis
    )


def spread(value, me, width):
    n = lax.axis_size("chan")
    padded = jnp.pad(value, ((0, 0), (1, 1), (0, 0)))
    pieces = []
    for k in range(n):
        piece = lax.dynamic_slice_in_dim(padded, (me ^ k) * width, width + 2, axis=1)
        pieces.append(swap(piece, "chan", k) if k else piece)
    return pieces


def add_rows(value):
    before, after = neighbours(value[:1], value[-1:])
    return jnp.concatenate([before, value, after], axis=0)


def conv(source, taps):
    return lax.conv_general_dilated(
        source[None],
        taps,
        (1, 1),
        "VALID",
        dimension_numbers=("NHWC", "HWIO", "NHWC"),
        preferred_element_type=jnp.float32,
    )[0]


def plain(image, filters, bias, upstream):
    n = lax.axis_size("chan")
    bands = lax.axis_size("band")
    me = lax.axis_index("chan")
    row = lax.axis_index("band")
    local = filters.shape[2]
    outs = filters.shape[1]
    width = image.shape[2] // n

    flat = filters.reshape(-1, local)
    share = flat.shape[0] // bands
    part = lax.dynamic_slice_in_dim(flat, row * share, share, axis=0)
    held = [jnp.concatenate([part, jnp.tile(bias[None], (16, 1))], axis=0)]
    step = n // 2
    while step:
        stacked = jnp.stack(held)
        there = swap(stacked, "chan", step)
        held = held + [there[j] for j in range(len(held))]
        step //= 2
    order = [0]
    step = n // 2
    while step:
        order = order + [o ^ step for o in order]
        step //= 2
    held = [held[order.index(k)] for k in range(n)]
    biases = [h[share] for h in held]
    whole = lax.all_gather(
        jnp.stack([h[:share] for h in held]), "band", axis=1, tiled=True
    ).reshape(n, 3, 3, outs, local)

    x_pieces = spread(jnp.transpose(image, (1, 2, 0)), me, width)
    u_pieces = spread(jnp.transpose(upstream, (1, 2, 0)), me, width)

    natural = [me ^ k for k in range(n)]
    x = add_rows(jnp.concatenate(x_pieces, axis=2))
    forward_taps = jnp.transpose(whole, (1, 2, 0, 4, 3)).reshape(3, 3, n * local, outs)
    total = conv(x, forward_taps) + pick(biases, natural, 0).astype(jnp.float32)
    features = back(total.astype(jnp.bfloat16), me, local, True)

    u = add_rows(pick(u_pieces, natural, 2))
    backward_taps = jnp.transpose(whole[:, ::-1, ::-1], (1, 2, 3, 0, 4)).reshape(
        3, 3, outs, n * local
    )
    image_grad = back(conv(u, backward_taps).astype(jnp.bfloat16), me, local, False)
    return features, image_grad


def back(value, me, local, is_natural):
    n = lax.axis_size("chan")
    pieces = []
    for k in range(n):
        start = (me ^ k) * local if is_natural else k * local
        piece = lax.dynamic_slice_in_dim(value, start, local, axis=2)
        pieces.append(swap(piece, "chan", k) if k else piece)
    whole = pick(pieces, [me ^ k for k in range(n)], 1)
    return jnp.transpose(whole, (2, 0, 1))


def assemble_kernel(order, place, filters, near, far, weights, extra):
    me, band = place[0], place[1]
    taps, channels, local = filters.shape
    share = near.shape[1] // (2 * taps)
    half = share // 2
    for tap in range(taps):
        for j in range(4):
            start = pl.multiple_of((me ^ j) * local, local)
            weights[pl.ds(tap * channels + j * local, local), :local] = filters[
                tap, pl.ds(start, local), :
            ]
    for bit, held in enumerate((near, far)):
        for j, d in enumerate(order):
            first = (band ^ (d | bit)) * share
            block = lax.div(first, local)
            start = (block ^ me) * local + first - block * local
            for tap in range(taps):
                row = pl.multiple_of(tap * channels + start, 16)
                weights[pl.ds(row, share), local:] = held[j, tap * share : (tap + 1) * share]
            first = (band ^ (d | bit)) * half
            block = lax.div(first, local)
            start = (block ^ (me & 1)) * local + first - block * local
            for tap in range(taps):
                row = pl.multiple_of(tap * 2 * local + start, 16)
                for k in range(2):
                    at = taps * share + (k * taps + tap) * half
                    extra[pl.ds(row, half), k * local : (k + 1) * local] = held[j, at : at + half]


def assemble_kernel(order, place, filters, near, far, weights, extra):
    me, band = place[0], place[1]
    taps, channels, local = filters.shape
    share = near.shape[1] // (2 * taps)
    half = share // 2
    for tap in range(taps):
        for j in range(4):
            start = pl.multiple_of((me ^ j) * local, local)
            weights[pl.ds(tap * channels + j * local, local), :local] = filters[
                tap, pl.ds(start, local), :
            ]
    for bit, held in enumerate((near, far)):
        for j, d in enumerate(order):
            first = (band ^ (d | bit)) * share
            block = lax.div(first, local)
            start = (block ^ me) * local + first - block * local
            for tap in range(taps):
                row = pl.multiple_of(tap * channels + start, 16)
                weights[pl.ds(row, share), local:] = held[j, tap * share : (tap + 1) * share]
            first = (band ^ (d | bit)) * half
            block = lax.div(first, local)
            start = (block ^ (me & 1)) * local + first - block * local
            for tap in range(taps):
                row = pl.multiple_of(tap * 2 * local + start, 16)
                for k in range(2):
                    at = taps * share + (k * taps + tap) * half
                    extra[pl.ds(row, half), k * local : (k + 1) * local] = held[j, at : at + half]


def cut_kernel(upstream, image, bias, edge, first, second):
    rows, cols, local = upstream.shape
    width = cols // 2
    line = bias[...].astype(jnp.float32)
    zero = jnp.zeros((1, local), jnp.float32)
    for out, parts in (
        (edge, [(v, r) for v in (upstream, image) for r in (0, rows - 1)]),
        (first, [(upstream, r) for r in range(1, rows - 1)]),
        (second, [(image, r) for r in range(1, rows - 1)]),
    ):
        for t in range(2):
            sides = []
            for at, (v, r) in enumerate(parts):
                piece = v[r, t * width : (t + 1) * width]
                for p in range(t, 4, 2):
                    out[p, at * width : (at + 1) * width] = piece
                left = v[r, width - 16 : width].astype(jnp.float32)[15:]
                right = v[r, width : width + 16].astype(jnp.float32)[:1]
                sides += [left, zero] if t else [zero, right]
            sides += [line] + [zero] * (15 - len(sides))
            tail = jnp.concatenate(sides).astype(jnp.bfloat16)
            for p in range(t, 4, 2):
                out[p, len(parts) * width :] = tail


def rim_kernel(width, edge, first, last):
    base = 4 * width
    for p in range(4):
        ends = edge[p, base:].astype(jnp.float32)
        for out, shift in ((first, 0), (last, 1)):
            pairs = []
            for i in range(2):
                at = 2 * i + shift
                out[p, i * width : (i + 1) * width] = edge[p, at * width : (at + 1) * width]
                pairs.append(ends[2 * at : 2 * at + 2])
            tail = jnp.concatenate(pairs + [jnp.zeros((12, ends.shape[1]), jnp.float32)])
            out[p, 2 * width :] = tail.astype(jnp.bfloat16)


def fill_source(target, me, which, width, edge, inner, before, after):
    local = edge.shape[2]
    count = inner.shape[1] // width
    rows = [(before, which, 2)]
    rows += [(edge, 2 * which, 4)]
    rows += [(inner, r, count) for r in range(count)]
    rows += [(edge, 2 * which + 1, 4), (after, which, 2)]
    for k in range(4):
        p = me ^ k
        lanes = slice(k * local, (k + 1) * local)
        for r, (ref, at, total) in enumerate(rows):
            middle = ref[p, at * width : (at + 1) * width]
            ends = ref[p, total * width : total * width + 16]
            target[1, r * width : (r + 1) * width, lanes] = middle
            target[0, r * width : (r + 1) * width, lanes] = jnp.concatenate(
                [ends[2 * at : 2 * at + 1], middle[:-1]]
            )
            target[2, r * width : (r + 1) * width, lanes] = jnp.concatenate(
                [middle[1:], ends[2 * at + 1 : 2 * at + 2]]
            )


def backward_kernel(place, edge, inner, before, after, weights, mine, other, source):
    size, local = mine.shape
    width = (before.shape[1] - 16) // 2
    channels = 4 * local
    fill_source(source, place[0], 0, width, edge, inner, before, after)
    acc = None
    for a in range(3):
        for b in range(3):
            term = jnp.dot(
                source[2 - b, pl.ds((2 - a) * width, size), :],
                weights[pl.ds((3 * a + b) * channels, channels), :],
                preferred_element_type=jnp.float32,
            )
            acc = term if acc is None else acc + term
    mine[...] = acc[:, :local].astype(jnp.bfloat16)
    other[...] = acc[:, local:].astype(jnp.bfloat16)


def forward_kernel(place, edge, inner, before, after, weights, extra, mine, other, source):
    size, local = mine.shape
    width = (before.shape[1] - 16) // 2
    channels, half = 4 * local, 2 * local
    me = place[0]
    fill_source(source, me, 1, width, edge, inner, before, after)
    acc = None
    for a in range(3):
        for b in range(3):
            tap = 3 * a + b
            for part in range(2):
                if part:
                    filters = extra[pl.ds(tap * half, half), :]
                else:
                    filters = weights[pl.ds(tap * channels, half), :]
                term = lax.dot_general(
                    source[b, pl.ds(a * width, size), part * half : (part + 1) * half],
                    filters,
                    (((1,), (1,)), ((), ())),
                    preferred_element_type=jnp.float32,
                )
                acc = term if acc is None else acc + term
    for k, out in enumerate((mine, other)):
        bias = edge[me ^ k, 4 * width :].astype(jnp.float32)[8:9]
        out[...] = (acc[:, k * local : (k + 1) * local] + bias).astype(jnp.bfloat16)


SMEM = pl.BlockSpec(memory_space=pltpu.SMEM)
VMEM = pl.BlockSpec(memory_space=pltpu.VMEM)


def kernel(body, shapes, args, scratch, name, placed=True):
    return pl.pallas_call(
        body,
        out_shape=[jax.ShapeDtypeStruct(s, jnp.bfloat16) for s in shapes],
        in_specs=[SMEM] * placed + [VMEM] * (len(args) - placed),
        out_specs=[VMEM] * len(shapes),
        scratch_shapes=[pltpu.VMEM(s, jnp.bfloat16) for s in scratch],
        compiler_params=pltpu.CompilerParams(vmem_limit_bytes=32 * 2**20),
        cost_estimate=pl.CostEstimate(flops=2**20, bytes_accessed=2**20, transcendentals=0),
        name=name,
    )(*args)


def exchange(payload):
    return lax.all_to_all(payload, "chan", split_axis=0, concat_axis=0, tiled=True)


def after(value, *others):
    return lax.optimization_barrier((value, others))[0]


def gather(value):
    bands = lax.axis_size("band")
    order = list(range(0, bands, 2))
    held = jnp.stack([swap(value, "band", d) if d else value for d in order])
    return held, swap(held, "band", 1), order


def home(mine, other, side, rows):
    turn = lambda p: jnp.transpose(p.reshape(rows, -1, p.shape[1]), (2, 0, 1))
    mine, other = turn(mine), turn(other)
    first = jnp.where(side == 0, mine, other)
    second = jnp.where(side == 0, other, mine)
    return jnp.concatenate([first, second], axis=2)


def per_device(image, filters, bias, upstream):
    n = lax.axis_size("chan")
    bands = lax.axis_size("band")
    taps, outs, local = filters.shape
    rows, cols = image.shape[1:]
    if n != 4 or local % 128 or cols % 256 or rows != 4 or outs % (32 * bands) or bands < 4:
        return plain(image, filters, bias, upstream)
    me = lax.axis_index("chan")
    band = lax.axis_index("band")
    side, half = me & 1, me >> 1
    place = jnp.stack([me, band]).astype(jnp.int32)
    width = cols // 2

    share = outs // bands
    near = lax.dynamic_slice_in_dim(filters, band * share, share, axis=1).reshape(-1, local)
    start = (1 - half) * (outs // 2) + band * (share // 2)
    across = lax.dynamic_slice_in_dim(filters, start, share // 2, axis=1).reshape(-1, local)
    parts = [swap(near, "chan", 1), swap(across, "chan", 2), swap(across, "chan", 3)]

    last = [jnp.transpose(v, (1, 2, 0)) for v in (upstream, image)]
    inner = (4, (rows - 2) * width + 16, local)
    rim = (4, 2 * width + 16, local)
    edge, first, second = kernel(
        cut_kernel,
        [(4, 4 * width + 16, local), inner, inner],
        [*last, bias[None]],
        [],
        "cut",
        False,
    )
    edge = exchange(after(edge, near, across))
    first = exchange(after(first, edge))
    second = exchange(after(second, first))

    held, there, order = gather(jnp.concatenate(parts))
    weights, extra = kernel(
        lambda *refs: assemble_kernel(order, *refs),
        [(taps * outs, 2 * local), (taps * 2 * local, 2 * local)],
        [place, filters, held, there],
        [],
        "assemble",
    )
    ends = kernel(lambda *refs: rim_kernel(width, *refs), [rim, rim], [edge], [], "rim", False)
    rims = neighbours(*ends)

    out = [(rows * width, local)] * 2
    source = [(3, (rows + 2) * width, 4 * local)]
    args = [place, edge, first, *rims, weights]
    mine, other = kernel(backward_kernel, out, args, source, "backward")
    image_grad = home(mine, swap(other, "chan", 1), side, rows)
    args = [place, edge, after(second, mine), *rims, weights, extra]
    mine, other = kernel(forward_kernel, out, args, source, "forward")
    return home(mine, swap(other, "chan", 1), side, rows), image_grad


def solution(mesh):
    return jax.shard_map(
        per_device,
        mesh=mesh,
        in_specs=(
            P("chan", "band", None),
            P(None, None, "chan"),
            P("chan"),
            P("chan", "band", None),
        ),
        out_specs=(P("chan", "band", None), P("chan", "band", None)),
        check_vma=False,
    )
```

```python
import jax
import jax.numpy as jnp
from jax import lax
from jax.experimental import pallas as pl
from jax.experimental.pallas import tpu as pltpu
from jax.sharding import PartitionSpec as P


def swap(value, axis, step):
    size = lax.axis_size(axis)
    return lax.ppermute(value, axis, [(j, j ^ step) for j in range(size)])


def neighbours(first, last):
    size = lax.axis_size("band")
    up = [(j, j + 1) for j in range(size - 1)]
    down = [(j + 1, j) for j in range(size - 1)]
    return lax.ppermute(last, "band", up), lax.ppermute(first, "band", down)


def pick(pieces, index, axis):
    stacked = jnp.stack(pieces)
    return jnp.concatenate(
        [lax.dynamic_index_in_dim(stacked, i, 0, keepdims=False) for i in index], axis=axis
    )


def spread(value, me, width):
    n = lax.axis_size("chan")
    padded = jnp.pad(value, ((0, 0), (1, 1), (0, 0)))
    pieces = []
    for k in range(n):
        piece = lax.dynamic_slice_in_dim(padded, (me ^ k) * width, width + 2, axis=1)
        pieces.append(swap(piece, "chan", k) if k else piece)
    return pieces


def add_rows(value):
    before, after = neighbours(value[:1], value[-1:])
    return jnp.concatenate([before, value, after], axis=0)


def conv(source, taps):
    return lax.conv_general_dilated(
        source[None],
        taps,
        (1, 1),
        "VALID",
        dimension_numbers=("NHWC", "HWIO", "NHWC"),
        preferred_element_type=jnp.float32,
    )[0]


def plain(image, filters, bias, upstream):
    n = lax.axis_size("chan")
    bands = lax.axis_size("band")
    me = lax.axis_index("chan")
    row = lax.axis_index("band")
    local = filters.shape[2]
    outs = filters.shape[1]
    width = image.shape[2] // n

    flat = filters.reshape(-1, local)
    share = flat.shape[0] // bands
    part = lax.dynamic_slice_in_dim(flat, row * share, share, axis=0)
    held = [jnp.concatenate([part, jnp.tile(bias[None], (16, 1))], axis=0)]
    step = n // 2
    while step:
        stacked = jnp.stack(held)
        there = swap(stacked, "chan", step)
        held = held + [there[j] for j in range(len(held))]
        step //= 2
    order = [0]
    step = n // 2
    while step:
        order = order + [o ^ step for o in order]
        step //= 2
    held = [held[order.index(k)] for k in range(n)]
    biases = [h[share] for h in held]
    whole = lax.all_gather(
        jnp.stack([h[:share] for h in held]), "band", axis=1, tiled=True
    ).reshape(n, 3, 3, outs, local)

    x_pieces = spread(jnp.transpose(image, (1, 2, 0)), me, width)
    u_pieces = spread(jnp.transpose(upstream, (1, 2, 0)), me, width)

    natural = [me ^ k for k in range(n)]
    x = add_rows(jnp.concatenate(x_pieces, axis=2))
    forward_taps = jnp.transpose(whole, (1, 2, 0, 4, 3)).reshape(3, 3, n * local, outs)
    total = conv(x, forward_taps) + pick(biases, natural, 0).astype(jnp.float32)
    features = back(total.astype(jnp.bfloat16), me, local, True)

    u = add_rows(pick(u_pieces, natural, 2))
    backward_taps = jnp.transpose(whole[:, ::-1, ::-1], (1, 2, 3, 0, 4)).reshape(
        3, 3, outs, n * local
    )
    image_grad = back(conv(u, backward_taps).astype(jnp.bfloat16), me, local, False)
    return features, image_grad


def back(value, me, local, is_natural):
    n = lax.axis_size("chan")
    pieces = []
    for k in range(n):
        start = (me ^ k) * local if is_natural else k * local
        piece = lax.dynamic_slice_in_dim(value, start, local, axis=2)
        pieces.append(swap(piece, "chan", k) if k else piece)
    whole = pick(pieces, [me ^ k for k in range(n)], 1)
    return jnp.transpose(whole, (2, 0, 1))


def assemble_kernel(order, place, filters, near, far, weights, extra):
    me, band = place[0], place[1]
    taps, channels, local = filters.shape
    share = near.shape[1] // (2 * taps)
    half = share // 2
    for tap in range(taps):
        for j in range(4):
            start = pl.multiple_of((me ^ j) * local, local)
            weights[pl.ds(tap * channels + j * local, local), :local] = filters[
                tap, pl.ds(start, local), :
            ]
    for bit, held in enumerate((near, far)):
        for j, d in enumerate(order):
            first = (band ^ (d | bit)) * share
            block = lax.div(first, local)
            start = (block ^ me) * local + first - block * local
            for tap in range(taps):
                row = pl.multiple_of(tap * channels + start, 16)
                weights[pl.ds(row, share), local:] = held[j, tap * share : (tap + 1) * share]
            first = (band ^ (d | bit)) * half
            block = lax.div(first, local)
            start = (block ^ (me & 1)) * local + first - block * local
            for tap in range(taps):
                row = pl.multiple_of(tap * 2 * local + start, 16)
                for k in range(2):
                    at = taps * share + (k * taps + tap) * half
                    extra[pl.ds(row, half), k * local : (k + 1) * local] = held[j, at : at + half]


def assemble_kernel(order, place, filters, near, far, weights, extra):
    me, band = place[0], place[1]
    taps, channels, local = filters.shape
    share = near.shape[1] // (2 * taps)
    half = share // 2
    for tap in range(taps):
        for j in range(4):
            start = pl.multiple_of((me ^ j) * local, local)
            weights[pl.ds(tap * channels + j * local, local), :local] = filters[
                tap, pl.ds(start, local), :
            ]
    for bit, held in enumerate((near, far)):
        for j, d in enumerate(order):
            first = (band ^ (d | bit)) * share
            block = lax.div(first, local)
            start = (block ^ me) * local + first - block * local
            for tap in range(taps):
                row = pl.multiple_of(tap * channels + start, 16)
                weights[pl.ds(row, share), local:] = held[j, tap * share : (tap + 1) * share]
            first = (band ^ (d | bit)) * half
            block = lax.div(first, local)
            start = (block ^ (me & 1)) * local + first - block * local
            for tap in range(taps):
                row = pl.multiple_of(tap * 2 * local + start, 16)
                for k in range(2):
                    at = taps * share + (k * taps + tap) * half
                    extra[pl.ds(row, half), k * local : (k + 1) * local] = held[j, at : at + half]


def cut_kernel(rows, place, *refs):
    sources, (bias, mine, other) = refs[:-3], refs[-3:]
    side = place[0] & 1
    local = bias.shape[1]
    width = sources[0].shape[1] // 2
    pitch = width + 8
    line = bias[...].astype(jnp.float32)
    zero = jnp.zeros((1, local), jnp.float32)
    rest = jnp.concatenate([line, zero, zero, zero, zero, zero])
    at = 0
    for source in sources:
        for r in rows:
            left = source[r, width - 16 : width].astype(jnp.float32)[15:]
            right = source[r, width : width + 16].astype(jnp.float32)[:1]
            ends = (zero, right), (left, zero)
            pieces = []
            for t, (before, behind) in enumerate(ends):
                tail = jnp.concatenate([behind, line, rest]).astype(jnp.bfloat16)
                pieces.append(
                    jnp.concatenate(
                        [
                            before.astype(jnp.bfloat16),
                            source[r, t * width : (t + 1) * width],
                            tail[:7],
                        ]
                    )
                )
            first = side == 0
            mine[at : at + pitch] = jnp.where(first, pieces[0], pieces[1])
            other[at : at + pitch] = jnp.where(first, pieces[1], pieces[0])
            at += pitch


def rim_kernel(width, *refs):
    pieces, (first, last) = refs[:4], refs[4:]
    pitch = width + 8
    for k, piece in enumerate(pieces):
        for i in range(2):
            for out, end in ((first, 0), (last, 1)):
                at = (2 * i + end) * pitch
                out[(2 * k + i) * pitch : (2 * k + i + 1) * pitch] = piece[at : at + pitch]


def fill_rows(target, piece, start, row, lanes, width):
    for shift in range(3):
        target[shift, row * width : (row + 1) * width, lanes] = piece[
            start + shift : start + shift + width
        ]


def fill_source(target, which, width, edges, inners, before, after):
    local = before.shape[1]
    pitch = width + 8
    count = inners[0].shape[0] // pitch
    for k in range(4):
        lanes = slice(k * local, (k + 1) * local)
        rows = [(before, 2 * k + which), (edges[k], 2 * which)]
        rows += [(inners[k], r) for r in range(count)]
        rows += [(edges[k], 2 * which + 1), (after, 2 * k + which)]
        for r, (ref, at) in enumerate(rows):
            fill_rows(target, ref, at * pitch, r, lanes, width)


def backward_kernel(*refs):
    edges, inners, (before, after, weights, mine, other, source) = refs[:4], refs[4:8], refs[8:]
    size, local = mine.shape
    width = before.shape[0] // 8 - 8
    channels = 4 * local
    fill_source(source, 0, width, edges, inners, before, after)
    acc = None
    for a in range(3):
        for b in range(3):
            term = jnp.dot(
                source[2 - b, pl.ds((2 - a) * width, size), :],
                weights[pl.ds((3 * a + b) * channels, channels), :],
                preferred_element_type=jnp.float32,
            )
            acc = term if acc is None else acc + term
    mine[...] = acc[:, :local].astype(jnp.bfloat16)
    other[...] = acc[:, local:].astype(jnp.bfloat16)


def forward_kernel(*refs):
    edges, inners, refs = refs[:4], refs[4:8], refs[8:]
    before, after, weights, extra, mine, other, source = refs
    size, local = mine.shape
    width = before.shape[0] // 8 - 8
    channels, half = 4 * local, 2 * local
    fill_source(source, 1, width, edges, inners, before, after)
    acc = None
    for a in range(3):
        for b in range(3):
            tap = 3 * a + b
            for part in range(2):
                if part:
                    filters = extra[pl.ds(tap * half, half), :]
                else:
                    filters = weights[pl.ds(tap * channels, half), :]
                term = lax.dot_general(
                    source[b, pl.ds(a * width, size), part * half : (part + 1) * half],
                    filters,
                    (((1,), (1,)), ((), ())),
                    preferred_element_type=jnp.float32,
                )
                acc = term if acc is None else acc + term
    for k, out in enumerate((mine, other)):
        bias = edges[k][width : width + 8, :].astype(jnp.float32)[2:3]
        out[...] = (acc[:, k * local : (k + 1) * local] + bias).astype(jnp.bfloat16)


SMEM = pl.BlockSpec(memory_space=pltpu.SMEM)
VMEM = pl.BlockSpec(memory_space=pltpu.VMEM)


def kernel(body, shapes, args, scratch, name, placed=False, flops=2**20):
    return pl.pallas_call(
        body,
        out_shape=[jax.ShapeDtypeStruct(s, jnp.bfloat16) for s in shapes],
        in_specs=[SMEM] * placed + [VMEM] * (len(args) - placed),
        out_specs=[VMEM] * len(shapes),
        scratch_shapes=[pltpu.VMEM(s, jnp.bfloat16) for s in scratch],
        compiler_params=pltpu.CompilerParams(vmem_limit_bytes=32 * 2**20),
        cost_estimate=pl.CostEstimate(flops=flops, bytes_accessed=2**20, transcendentals=0),
        name=name,
    )(*args)


def cut(place, sources, bias, rows, name, flops):
    local = bias.shape[1]
    shape = (len(sources) * len(rows) * (sources[0].shape[1] // 2 + 8), local)
    body = lambda *refs: cut_kernel(rows, *refs)
    return kernel(body, [shape] * 2, [place, *sources, bias], [], name, True, flops)


def exchange(mine, other):
    far = swap(other, "chan", 3)
    middle = swap(mine, "chan", 2)
    return [mine, swap(other, "chan", 1), middle, far]


def after(value, *others):
    return lax.optimization_barrier((value, others))[0]


def gather(value):
    bands = lax.axis_size("band")
    order = list(range(0, bands, 2))
    held = jnp.stack([swap(value, "band", d) if d else value for d in order])
    return held, swap(held, "band", 1), order


def home(mine, other, side, rows):
    turn = lambda p: jnp.transpose(p.reshape(rows, -1, p.shape[1]), (2, 0, 1))
    mine, other = turn(mine), turn(other)
    first = jnp.where(side == 0, mine, other)
    second = jnp.where(side == 0, other, mine)
    return jnp.concatenate([first, second], axis=2)


MICROSECOND = 10**9


def per_device(image, filters, bias, upstream):
    n = lax.axis_size("chan")
    bands = lax.axis_size("band")
    taps, outs, local = filters.shape
    rows, cols = image.shape[1:]
    if n != 4 or local % 128 or cols % 256 or rows != 4 or outs % (32 * bands) or bands < 4:
        return plain(image, filters, bias, upstream)
    me = lax.axis_index("chan")
    band = lax.axis_index("band")
    side, half = me & 1, me >> 1
    place = jnp.stack([me, band]).astype(jnp.int32)
    width = cols // 2

    share = outs // bands
    near = lax.dynamic_slice_in_dim(filters, band * share, share, axis=1).reshape(-1, local)
    start = (1 - half) * (outs // 2) + band * (share // 2)
    across = lax.dynamic_slice_in_dim(filters, start, share // 2, axis=1).reshape(-1, local)
    parts = [swap(near, "chan", 1), swap(across, "chan", 2), swap(across, "chan", 3)]

    upstream, image = [jnp.transpose(v, (1, 2, 0)) for v in (upstream, image)]
    line = bias[None]
    edge = cut(place, [upstream, image], line, (0, rows - 1), "cut_edge", 2**20)
    edge = exchange(*after(edge, near, across))
    middle = range(1, rows - 1)
    upstream = after(upstream, edge[1])
    early = cut(place, [upstream], line, middle, "cut_first", 5 * MICROSECOND)
    edge = after(edge, early)
    first = exchange(*early)
    image = after(image, first[1:])
    late = cut(place, [image], line, middle, "cut_second", 18 * MICROSECOND)
    first = after(first, late)
    second = exchange(*late)

    held, there, order = gather(jnp.concatenate(parts))
    weights, extra = kernel(
        lambda *refs: assemble_kernel(order, *refs),
        [(taps * outs, 2 * local), (taps * 2 * local, 2 * local)],
        [place, filters, held, there],
        [],
        "assemble",
        True,
    )
    rim = (8 * (width + 8), local)
    rims = neighbours(*kernel(lambda *refs: rim_kernel(width, *refs), [rim] * 2, edge, [], "rim", False, 16 * MICROSECOND))

    out = [(rows * width, local)] * 2
    source = [(3, (rows + 2) * width, 4 * local)]
    args = [*edge, *first, *rims, weights]
    mine, other = kernel(backward_kernel, out, args, source, "backward", False, 10 * MICROSECOND)
    other = swap(other, "chan", 1)
    image_grad = home(mine, other, side, rows)
    args = [*edge, *after(second, mine), *rims, weights, extra]
    mine, sent = kernel(forward_kernel, out, args, source, "forward", False, 5 * MICROSECOND)
    other = swap(after(sent, other), "chan", 1)
    return home(mine, other, side, rows), image_grad


def solution(mesh):
    return jax.shard_map(
        per_device,
        mesh=mesh,
        in_specs=(
            P("chan", "band", None),
            P(None, None, "chan"),
            P("chan"),
            P("chan", "band", None),
        ),
        out_specs=(P("chan", "band", None), P("chan", "band", None)),
        check_vma=False,
    )
```

```python
import jax
import jax.numpy as jnp
from jax import lax
from jax.experimental import pallas as pl
from jax.experimental.pallas import tpu as pltpu
from jax.sharding import PartitionSpec as P


def swap(value, axis, step):
    size = lax.axis_size(axis)
    return lax.ppermute(value, axis, [(j, j ^ step) for j in range(size)])


def neighbours(first, last):
    size = lax.axis_size("band")
    up = [(j, j + 1) for j in range(size - 1)]
    down = [(j + 1, j) for j in range(size - 1)]
    return lax.ppermute(last, "band", up), lax.ppermute(first, "band", down)


def pick(pieces, index, axis):
    stacked = jnp.stack(pieces)
    return jnp.concatenate(
        [lax.dynamic_index_in_dim(stacked, i, 0, keepdims=False) for i in index], axis=axis
    )


def spread(value, me, width):
    n = lax.axis_size("chan")
    padded = jnp.pad(value, ((0, 0), (1, 1), (0, 0)))
    pieces = []
    for k in range(n):
        piece = lax.dynamic_slice_in_dim(padded, (me ^ k) * width, width + 2, axis=1)
        pieces.append(swap(piece, "chan", k) if k else piece)
    return pieces


def add_rows(value):
    before, after = neighbours(value[:1], value[-1:])
    return jnp.concatenate([before, value, after], axis=0)


def conv(source, taps):
    return lax.conv_general_dilated(
        source[None],
        taps,
        (1, 1),
        "VALID",
        dimension_numbers=("NHWC", "HWIO", "NHWC"),
        preferred_element_type=jnp.float32,
    )[0]


def plain(image, filters, bias, upstream):
    n = lax.axis_size("chan")
    bands = lax.axis_size("band")
    me = lax.axis_index("chan")
    row = lax.axis_index("band")
    local = filters.shape[2]
    outs = filters.shape[1]
    width = image.shape[2] // n

    flat = filters.reshape(-1, local)
    share = flat.shape[0] // bands
    part = lax.dynamic_slice_in_dim(flat, row * share, share, axis=0)
    held = [jnp.concatenate([part, jnp.tile(bias[None], (16, 1))], axis=0)]
    step = n // 2
    while step:
        stacked = jnp.stack(held)
        there = swap(stacked, "chan", step)
        held = held + [there[j] for j in range(len(held))]
        step //= 2
    order = [0]
    step = n // 2
    while step:
        order = order + [o ^ step for o in order]
        step //= 2
    held = [held[order.index(k)] for k in range(n)]
    biases = [h[share] for h in held]
    whole = lax.all_gather(
        jnp.stack([h[:share] for h in held]), "band", axis=1, tiled=True
    ).reshape(n, 3, 3, outs, local)

    x_pieces = spread(jnp.transpose(image, (1, 2, 0)), me, width)
    u_pieces = spread(jnp.transpose(upstream, (1, 2, 0)), me, width)

    natural = [me ^ k for k in range(n)]
    x = add_rows(jnp.concatenate(x_pieces, axis=2))
    forward_taps = jnp.transpose(whole, (1, 2, 0, 4, 3)).reshape(3, 3, n * local, outs)
    total = conv(x, forward_taps) + pick(biases, natural, 0).astype(jnp.float32)
    features = back(total.astype(jnp.bfloat16), me, local, True)

    u = add_rows(pick(u_pieces, natural, 2))
    backward_taps = jnp.transpose(whole[:, ::-1, ::-1], (1, 2, 3, 0, 4)).reshape(
        3, 3, outs, n * local
    )
    image_grad = back(conv(u, backward_taps).astype(jnp.bfloat16), me, local, False)
    return features, image_grad


def back(value, me, local, is_natural):
    n = lax.axis_size("chan")
    pieces = []
    for k in range(n):
        start = (me ^ k) * local if is_natural else k * local
        piece = lax.dynamic_slice_in_dim(value, start, local, axis=2)
        pieces.append(swap(piece, "chan", k) if k else piece)
    whole = pick(pieces, [me ^ k for k in range(n)], 1)
    return jnp.transpose(whole, (2, 0, 1))


def assemble_kernel(orders, place, filters, near, near_far, across, across_far, weights, extra):
    me, band = place[0], place[1]
    taps, channels, local = filters.shape
    share = near.shape[1] // taps
    half = share // 2
    for tap in range(taps):
        for j in range(4):
            start = pl.multiple_of((me ^ j) * local, local)
            weights[pl.ds(tap * channels + j * local, local), :local] = filters[
                tap, pl.ds(start, local), :
            ]
    for bit, held in enumerate((near, near_far)):
        for j, d in enumerate(orders[0]):
            first = (band ^ (d | bit)) * share
            block = lax.div(first, local)
            start = (block ^ me) * local + first - block * local
            for tap in range(taps):
                row = pl.multiple_of(tap * channels + start, 16)
                weights[pl.ds(row, share), local:] = held[j, tap * share : (tap + 1) * share]
    for bit, held in enumerate((across, across_far)):
        for j, d in enumerate(orders[1]):
            first = (band ^ (d | bit)) * half
            block = lax.div(first, local)
            start = (block ^ (me & 1)) * local + first - block * local
            for tap in range(taps):
                row = pl.multiple_of(tap * 2 * local + start, 16)
                for k in range(2):
                    at = (k * taps + tap) * half
                    extra[pl.ds(row, half), k * local : (k + 1) * local] = held[j, at : at + half]


def cut_kernel(parts, place, *refs):
    sources, (bias, mine, other) = refs[:-3], refs[-3:]
    side = place[0] & 1
    local = bias.shape[1]
    width = sources[0].shape[1] // 2
    pitch = width + 8
    line = bias[...].astype(jnp.float32)
    zero = jnp.zeros((1, local), jnp.float32)
    rest = jnp.concatenate([line, zero, zero, zero, zero, zero])
    for n, (i, r) in enumerate(parts):
        source = sources[i]
        left = source[r, width - 16 : width].astype(jnp.float32)[15:]
        right = source[r, width : width + 16].astype(jnp.float32)[:1]
        pieces = []
        for t, (before, behind) in enumerate(((zero, right), (left, zero))):
            tail = jnp.concatenate([behind, line, rest]).astype(jnp.bfloat16)
            middle = source[r, t * width : (t + 1) * width]
            pieces.append(jnp.concatenate([before.astype(jnp.bfloat16), middle, tail[:7]]))
        at = n * pitch
        mine[at : at + pitch] = jnp.where(side == 0, pieces[0], pieces[1])
        other[at : at + pitch] = jnp.where(side == 0, pieces[1], pieces[0])


def rim_kernel(width, rows, *refs):
    pieces, (first, last) = refs[:4], refs[4:]
    pitch = width + 8
    for k, piece in enumerate(pieces):
        for i in range(2):
            for out, end in ((first, 0), (last, 1)):
                at = (i * rows + end * (1 if i else rows - 1)) * pitch
                out[(2 * k + i) * pitch : (2 * k + i + 1) * pitch] = piece[at : at + pitch]


def fill_rows(target, piece, start, row, lanes, width):
    for shift in range(3):
        target[shift, row * width : (row + 1) * width, lanes] = piece[
            start + shift : start + shift + width
        ]


def fill_source(target, which, width, rows, before, after):
    local = before.shape[1]
    pitch = width + 8
    for k, held in enumerate(rows):
        lanes = slice(k * local, (k + 1) * local)
        held = [(before, 2 * k + which), *held, (after, 2 * k + which)]
        for r, (ref, at) in enumerate(held):
            fill_rows(target, ref, at * pitch, r, lanes, width)


def backward_kernel(*refs):
    edges, (before, after, weights, mine, other, source) = refs[:4], refs[4:]
    size, local = mine.shape
    width = before.shape[0] // 8 - 8
    channels = 4 * local
    rows = [[(p, r) for r in range(size // width)] for p in edges]
    fill_source(source, 0, width, rows, before, after)
    acc = None
    for a in range(3):
        for b in range(3):
            term = jnp.dot(
                source[2 - b, pl.ds((2 - a) * width, size), :],
                weights[pl.ds((3 * a + b) * channels, channels), :],
                preferred_element_type=jnp.float32,
            )
            acc = term if acc is None else acc + term
    mine[...] = acc[:, :local].astype(jnp.bfloat16)
    other[...] = acc[:, local:].astype(jnp.bfloat16)


def forward_kernel(*refs):
    edges, inners, refs = refs[:4], refs[4:8], refs[8:]
    before, after, weights, extra, mine, other, source = refs
    size, local = mine.shape
    width = before.shape[0] // 8 - 8
    channels, half = 4 * local, 2 * local
    count = size // width
    rows = [
        [(p, count), *((q, r) for r in range(count - 2)), (p, count + 1)]
        for p, q in zip(edges, inners)
    ]
    fill_source(source, 1, width, rows, before, after)
    acc = None
    for a in range(3):
        for b in range(3):
            tap = 3 * a + b
            for part in range(2):
                if part:
                    filters = extra[pl.ds(tap * half, half), :]
                else:
                    filters = weights[pl.ds(tap * channels, half), :]
                term = lax.dot_general(
                    source[b, pl.ds(a * width, size), part * half : (part + 1) * half],
                    filters,
                    (((1,), (1,)), ((), ())),
                    preferred_element_type=jnp.float32,
                )
                acc = term if acc is None else acc + term
    for k, out in enumerate((mine, other)):
        bias = edges[k][width : width + 8, :].astype(jnp.float32)[2:3]
        out[...] = (acc[:, k * local : (k + 1) * local] + bias).astype(jnp.bfloat16)


SMEM = pl.BlockSpec(memory_space=pltpu.SMEM)
VMEM = pl.BlockSpec(memory_space=pltpu.VMEM)
ANY = pl.BlockSpec(memory_space=pl.ANY)


def kernel(body, shapes, args, scratch, name, placed=False, flops=2**20):
    return pl.pallas_call(
        body,
        out_shape=[jax.ShapeDtypeStruct(s, jnp.bfloat16) for s in shapes],
        in_specs=[SMEM] * placed + [VMEM] * (len(args) - placed),
        out_specs=[VMEM] * len(shapes),
        scratch_shapes=[pltpu.VMEM(s, jnp.bfloat16) for s in scratch],
        compiler_params=pltpu.CompilerParams(vmem_limit_bytes=32 * 2**20),
        cost_estimate=pl.CostEstimate(flops=flops, bytes_accessed=2**20, transcendentals=0),
        name=name,
    )(*args)


def cut(place, sources, bias, parts, name, flops):
    local = bias.shape[1]
    shape = (len(parts) * (sources[0].shape[1] // 2 + 8), local)
    body = lambda *refs: cut_kernel(parts, *refs)
    return kernel(body, [shape] * 2, [place, *sources, bias], [], name, True, flops)


def exchange(mine, other):
    far = swap(other, "chan", 3)
    middle = swap(mine, "chan", 2)
    return [mine, swap(other, "chan", 1), middle, far]


def after(value, *others):
    return lax.optimization_barrier((value, others))[0]


def gather(value, steps):
    held, order = value[None], [0]
    for step in steps:
        held = jnp.concatenate([held, swap(held, "band", step)])
        order = order + [o ^ step for o in order]
    return held, order


def halving(size):
    steps = []
    while size > 1:
        size //= 2
        steps.append(size)
    return steps


def home_kernel(place, mine, other, out, sems):
    width = mine.shape[2]
    side = place[0] & 1
    copies = []
    for i, ref in enumerate((mine, other)):
        start = pl.multiple_of((side ^ i) * width, width)
        copies.append(pltpu.make_async_copy(ref, out.at[:, :, pl.ds(start, width)], sems.at[i]))
    for copy in copies:
        copy.start()
    for copy in copies:
        copy.wait()


def home(place, mine, other, rows):
    turn = lambda p: jnp.transpose(p.reshape(rows, -1, p.shape[1]), (2, 0, 1))
    mine, other = turn(mine), turn(other)
    channels, rows, width = mine.shape
    return pl.pallas_call(
        home_kernel,
        out_shape=jax.ShapeDtypeStruct((channels, rows, 2 * width), jnp.bfloat16),
        in_specs=[SMEM, ANY, ANY],
        out_specs=ANY,
        scratch_shapes=[pltpu.SemaphoreType.DMA((2,))],
        cost_estimate=pl.CostEstimate(flops=2**20, bytes_accessed=2**20, transcendentals=0),
        name="home",
    )(place, mine, other)


MICROSECOND = 10**9


def per_device(image, filters, bias, upstream):
    n = lax.axis_size("chan")
    bands = lax.axis_size("band")
    taps, outs, local = filters.shape
    rows, cols = image.shape[1:]
    if n != 4 or local % 128 or cols % 256 or rows < 3 or outs % (32 * bands) or bands < 4:
        return plain(image, filters, bias, upstream)
    me = lax.axis_index("chan")
    band = lax.axis_index("band")
    half = me >> 1
    place = jnp.stack([me, band]).astype(jnp.int32)
    width = cols // 2

    share = outs // bands
    near = lax.dynamic_slice_in_dim(filters, band * share, share, axis=1).reshape(-1, local)
    start = (1 - half) * (outs // 2) + band * (share // 2)
    across = lax.dynamic_slice_in_dim(filters, start, share // 2, axis=1).reshape(-1, local)
    near = swap(near, "chan", 1)
    across = jnp.concatenate([swap(across, "chan", k) for k in (2, 3)])

    upstream, image = [jnp.transpose(v, (1, 2, 0)) for v in (upstream, image)]
    parts = [(0, r) for r in range(rows)] + [(1, 0), (1, rows - 1)]
    edge = cut(place, [upstream, image], bias[None], parts, "cut_first", 2**20)
    near, across = after((near, across), edge)
    edge = exchange(*edge)
    parts = [(0, r) for r in range(1, rows - 1)]
    late = cut(place, [after(image, edge[1])], bias[None], parts, "cut_second", 2**20)
    edge = after(edge, late)
    second = exchange(*late)

    steps = halving(bands)[:-1]
    near, near_order = gather(near, steps)
    across, across_order = gather(across, steps[::-1])
    held = [near, swap(near, "band", 1), across, swap(across, "band", 1)]
    weights, extra = kernel(
        lambda *refs: assemble_kernel((near_order, across_order), *refs),
        [(taps * outs, 2 * local), (taps * 2 * local, 2 * local)],
        [place, filters, *held],
        [],
        "assemble",
        True,
        2 * MICROSECOND,
    )
    rim = (8 * (width + 8), local)
    body = lambda *refs: rim_kernel(width, rows, *refs)
    rims = neighbours(*kernel(body, [rim] * 2, edge, [], "rim", False, 4 * MICROSECOND))

    out = [(rows * width, local)] * 2
    source = [(3, (rows + 2) * width, 4 * local)]
    args = [*edge, *rims, weights]
    mine, other = kernel(backward_kernel, out, args, source, "backward", False, 10 * MICROSECOND)
    other = swap(other, "chan", 1)
    image_grad = home(place, mine, other, rows)
    args = [*edge, *after(second, mine), *rims, weights, extra]
    mine, sent = kernel(forward_kernel, out, args, source, "forward", False, 5 * MICROSECOND)
    other = swap(after(sent, other), "chan", 1)
    return home(place, mine, other, rows), image_grad


def solution(mesh):
    return jax.shard_map(
        per_device,
        mesh=mesh,
        in_specs=(
            P("chan", "band", None),
            P(None, None, "chan"),
            P("chan"),
            P("chan", "band", None),
        ),
        out_specs=(P("chan", "band", None), P("chan", "band", None)),
        check_vma=False,
    )
```

```python
import jax
import jax.numpy as jnp
from jax import lax
from jax.experimental import pallas as pl
from jax.experimental.pallas import tpu as pltpu
from jax.sharding import PartitionSpec as P


def swap(value, axis, step):
    size = lax.axis_size(axis)
    return lax.ppermute(value, axis, [(j, j ^ step) for j in range(size)])


def neighbours(first, last):
    size = lax.axis_size("band")
    up = [(j, j + 1) for j in range(size - 1)]
    down = [(j + 1, j) for j in range(size - 1)]
    return lax.ppermute(last, "band", up), lax.ppermute(first, "band", down)


def pick(pieces, index, axis):
    stacked = jnp.stack(pieces)
    return jnp.concatenate(
        [lax.dynamic_index_in_dim(stacked, i, 0, keepdims=False) for i in index], axis=axis
    )


def spread(value, me, width):
    n = lax.axis_size("chan")
    padded = jnp.pad(value, ((0, 0), (1, 1), (0, 0)))
    pieces = []
    for k in range(n):
        piece = lax.dynamic_slice_in_dim(padded, (me ^ k) * width, width + 2, axis=1)
        pieces.append(swap(piece, "chan", k) if k else piece)
    return pieces


def add_rows(value):
    before, after = neighbours(value[:1], value[-1:])
    return jnp.concatenate([before, value, after], axis=0)


def conv(source, taps):
    return lax.conv_general_dilated(
        source[None],
        taps,
        (1, 1),
        "VALID",
        dimension_numbers=("NHWC", "HWIO", "NHWC"),
        preferred_element_type=jnp.float32,
    )[0]


def plain(image, filters, bias, upstream):
    n = lax.axis_size("chan")
    bands = lax.axis_size("band")
    me = lax.axis_index("chan")
    row = lax.axis_index("band")
    local = filters.shape[2]
    outs = filters.shape[1]
    width = image.shape[2] // n

    flat = filters.reshape(-1, local)
    share = flat.shape[0] // bands
    part = lax.dynamic_slice_in_dim(flat, row * share, share, axis=0)
    held = [jnp.concatenate([part, jnp.tile(bias[None], (16, 1))], axis=0)]
    step = n // 2
    while step:
        stacked = jnp.stack(held)
        there = swap(stacked, "chan", step)
        held = held + [there[j] for j in range(len(held))]
        step //= 2
    order = [0]
    step = n // 2
    while step:
        order = order + [o ^ step for o in order]
        step //= 2
    held = [held[order.index(k)] for k in range(n)]
    biases = [h[share] for h in held]
    whole = lax.all_gather(
        jnp.stack([h[:share] for h in held]), "band", axis=1, tiled=True
    ).reshape(n, 3, 3, outs, local)

    x_pieces = spread(jnp.transpose(image, (1, 2, 0)), me, width)
    u_pieces = spread(jnp.transpose(upstream, (1, 2, 0)), me, width)

    natural = [me ^ k for k in range(n)]
    x = add_rows(jnp.concatenate(x_pieces, axis=2))
    forward_taps = jnp.transpose(whole, (1, 2, 0, 4, 3)).reshape(3, 3, n * local, outs)
    total = conv(x, forward_taps) + pick(biases, natural, 0).astype(jnp.float32)
    features = back(total.astype(jnp.bfloat16), me, local, True)

    u = add_rows(pick(u_pieces, natural, 2))
    backward_taps = jnp.transpose(whole[:, ::-1, ::-1], (1, 2, 3, 0, 4)).reshape(
        3, 3, outs, n * local
    )
    image_grad = back(conv(u, backward_taps).astype(jnp.bfloat16), me, local, False)
    return features, image_grad


def back(value, me, local, is_natural):
    n = lax.axis_size("chan")
    pieces = []
    for k in range(n):
        start = (me ^ k) * local if is_natural else k * local
        piece = lax.dynamic_slice_in_dim(value, start, local, axis=2)
        pieces.append(swap(piece, "chan", k) if k else piece)
    whole = pick(pieces, [me ^ k for k in range(n)], 1)
    return jnp.transpose(whole, (2, 0, 1))


def assemble_kernel(orders, place, filters, near, near_far, across, across_far, weights, extra):
    me, band = place[0], place[1]
    taps, channels, local = filters.shape
    share = near.shape[1] // taps
    half = share // 2
    for tap in range(taps):
        for j in range(4):
            start = pl.multiple_of((me ^ j) * local, local)
            weights[pl.ds(tap * channels + j * local, local), :local] = filters[
                tap, pl.ds(start, local), :
            ]
    for bit, held in enumerate((near, near_far)):
        for j, d in enumerate(orders[0]):
            first = (band ^ (d | bit)) * share
            block = lax.div(first, local)
            start = (block ^ me) * local + first - block * local
            for tap in range(taps):
                row = pl.multiple_of(tap * channels + start, 16)
                weights[pl.ds(row, share), local:] = held[j, tap * share : (tap + 1) * share]
    for bit, held in enumerate((across, across_far)):
        for j, d in enumerate(orders[1]):
            first = (band ^ (d | bit)) * half
            block = lax.div(first, local)
            start = (block ^ (me & 1)) * local + first - block * local
            for tap in range(taps):
                row = pl.multiple_of(tap * 2 * local + start, 16)
                for k in range(2):
                    at = (k * taps + tap) * half
                    extra[pl.ds(row, half), k * local : (k + 1) * local] = held[j, at : at + half]


def cut_kernel(parts, place, *refs):
    sources, (bias, mine, other) = refs[:-3], refs[-3:]
    side = place[0] & 1
    local = bias.shape[1]
    width = sources[0].shape[1] // 2
    pitch = width + 8
    line = bias[...].astype(jnp.float32)
    zero = jnp.zeros((1, local), jnp.float32)
    rest = jnp.concatenate([line, zero, zero, zero, zero, zero])
    for n, (i, r) in enumerate(parts):
        source = sources[i]
        left = source[r, width - 16 : width].astype(jnp.float32)[15:]
        right = source[r, width : width + 16].astype(jnp.float32)[:1]
        pieces = []
        for t, (before, behind) in enumerate(((zero, right), (left, zero))):
            tail = jnp.concatenate([behind, line, rest]).astype(jnp.bfloat16)
            middle = source[r, t * width : (t + 1) * width]
            pieces.append(jnp.concatenate([before.astype(jnp.bfloat16), middle, tail[:7]]))
        at = n * pitch
        mine[at : at + pitch] = jnp.where(side == 0, pieces[0], pieces[1])
        other[at : at + pitch] = jnp.where(side == 0, pieces[1], pieces[0])


def rim_kernel(width, *refs):
    pieces, (first, last) = refs[:4], refs[4:]
    pitch = width + 8
    for k, piece in enumerate(pieces):
        for i in range(2):
            for out, end in ((first, 0), (last, 1)):
                at = (2 * i + end) * pitch
                out[(2 * k + i) * pitch : (2 * k + i + 1) * pitch] = piece[at : at + pitch]


def fill_rows(target, piece, start, row, lanes, width):
    for shift in range(3):
        target[shift, row * width : (row + 1) * width, lanes] = piece[
            start + shift : start + shift + width
        ]


def fill_source(target, which, width, rows, before, after):
    local = before.shape[1]
    pitch = width + 8
    for k, held in enumerate(rows):
        lanes = slice(k * local, (k + 1) * local)
        held = [(before, 2 * k + which), *held, (after, 2 * k + which)]
        for r, (ref, at) in enumerate(held):
            fill_rows(target, ref, at * pitch, r, lanes, width)


def inside(edges, inners, which, count):
    return [
        [(p, 2 * which), *((q, r) for r in range(count - 2)), (p, 2 * which + 1)]
        for p, q in zip(edges, inners)
    ]


def backward_kernel(*refs):
    edges, inners, (before, after, weights, _, mine, other, source) = refs[:4], refs[4:8], refs[8:]
    size, local = mine.shape
    width = before.shape[0] // 8 - 8
    channels = 4 * local
    fill_source(source, 0, width, inside(edges, inners, 0, size // width), before, after)
    acc = None
    for a in range(3):
        for b in range(3):
            term = jnp.dot(
                source[2 - b, pl.ds((2 - a) * width, size), :],
                weights[pl.ds((3 * a + b) * channels, channels), :],
                preferred_element_type=jnp.float32,
            )
            acc = term if acc is None else acc + term
    mine[...] = acc[:, :local].astype(jnp.bfloat16)
    other[...] = acc[:, local:].astype(jnp.bfloat16)


def forward_kernel(*refs):
    edges, inners, refs = refs[:4], refs[4:8], refs[8:]
    before, after, weights, extra, mine, other, source = refs
    size, local = mine.shape
    width = before.shape[0] // 8 - 8
    channels, half = 4 * local, 2 * local
    fill_source(source, 1, width, inside(edges, inners, 1, size // width), before, after)
    acc = None
    for a in range(3):
        for b in range(3):
            tap = 3 * a + b
            for part in range(2):
                if part:
                    filters = extra[pl.ds(tap * half, half), :]
                else:
                    filters = weights[pl.ds(tap * channels, half), :]
                term = lax.dot_general(
                    source[b, pl.ds(a * width, size), part * half : (part + 1) * half],
                    filters,
                    (((1,), (1,)), ((), ())),
                    preferred_element_type=jnp.float32,
                )
                acc = term if acc is None else acc + term
    for k, out in enumerate((mine, other)):
        bias = edges[k][width : width + 8, :].astype(jnp.float32)[2:3]
        out[...] = (acc[:, k * local : (k + 1) * local] + bias).astype(jnp.bfloat16)


SMEM = pl.BlockSpec(memory_space=pltpu.SMEM)
VMEM = pl.BlockSpec(memory_space=pltpu.VMEM)
ANY = pl.BlockSpec(memory_space=pl.ANY)


def cost(microseconds):
    work = 2**20 + 10**9 * microseconds
    return pl.CostEstimate(flops=work, bytes_accessed=2**20, transcendentals=0)


def kernel(body, shapes, args, scratch, name, placed=False, micros=0):
    return pl.pallas_call(
        body,
        out_shape=[jax.ShapeDtypeStruct(s, jnp.bfloat16) for s in shapes],
        in_specs=[SMEM] * placed + [VMEM] * (len(args) - placed),
        out_specs=[VMEM] * len(shapes),
        scratch_shapes=[pltpu.VMEM(s, jnp.bfloat16) for s in scratch],
        compiler_params=pltpu.CompilerParams(vmem_limit_bytes=32 * 2**20),
        cost_estimate=cost(micros),
        name=name,
    )(*args)


def cut(place, sources, bias, parts, name, micros):
    local = bias.shape[1]
    shape = (len(parts) * (sources[0].shape[1] // 2 + 8), local)
    body = lambda *refs: cut_kernel(parts, *refs)
    return kernel(body, [shape] * 2, [place, *sources, bias], [], name, True, micros)


def exchange(mine, other):
    far = swap(other, "chan", 3)
    middle = swap(mine, "chan", 2)
    return [mine, swap(other, "chan", 1), middle, far]


def after(value, *others):
    return lax.optimization_barrier((value, others))[0]


def gather(value, steps):
    held, order = value[None], [0]
    for step in steps:
        held = jnp.concatenate([held, swap(held, "band", step)])
        order = order + [o ^ step for o in order]
    return held, order


def halving(size):
    steps = []
    while size > 1:
        size //= 2
        steps.append(size)
    return steps


def home_kernel(place, mine, other, out):
    width = mine.shape[2]
    side = place[0] & 1
    for t in range(2):

        @pl.when(side == t)
        def _():
            out[:, :, t * width : (t + 1) * width] = mine[...]
            out[:, :, (1 - t) * width : (2 - t) * width] = other[...]


def home(place, mine, other, rows):
    turn = lambda p: jnp.transpose(p.reshape(rows, -1, p.shape[1]), (2, 0, 1))
    mine, other = turn(mine), turn(other)
    channels, rows, width = mine.shape
    shape = (channels, rows, 2 * width)
    return kernel(home_kernel, [shape], [place, mine, other], [], "home", True)[0]


def token_kernel(*refs):
    refs[-1][...] = jnp.zeros_like(refs[-1])


def token(pieces, micros):
    return pl.pallas_call(
        token_kernel,
        out_shape=jax.ShapeDtypeStruct((16, 128), jnp.bfloat16),
        in_specs=[ANY] * len(pieces),
        out_specs=VMEM,
        cost_estimate=cost(micros),
        name="token",
    )(*pieces)


def per_device(image, filters, bias, upstream):
    n = lax.axis_size("chan")
    bands = lax.axis_size("band")
    taps, outs, local = filters.shape
    rows, cols = image.shape[1:]
    if n != 4 or local % 128 or cols % 256 or rows < 3 or outs % (32 * bands) or bands < 4:
        return plain(image, filters, bias, upstream)
    me = lax.axis_index("chan")
    band = lax.axis_index("band")
    half = me >> 1
    place = jnp.stack([me, band]).astype(jnp.int32)
    width = cols // 2

    share = outs // bands
    near = lax.dynamic_slice_in_dim(filters, band * share, share, axis=1).reshape(-1, local)
    start = (1 - half) * (outs // 2) + band * (share // 2)
    across = lax.dynamic_slice_in_dim(filters, start, share // 2, axis=1).reshape(-1, local)
    near = swap(near, "chan", 1)
    across = jnp.concatenate([swap(across, "chan", k) for k in (2, 3)])

    upstream, image = [jnp.transpose(v, (1, 2, 0)) for v in (upstream, image)]
    parts = [(i, r) for i in range(2) for r in (0, rows - 1)]
    edge = cut(place, [upstream, image], bias[None], parts, "cut_edge", 0)
    near, across = after((near, across), edge)
    edge = exchange(*edge)
    parts = [(0, r) for r in range(1, rows - 1)]
    first = exchange(*cut(place, [upstream], bias[None], parts, "cut_first", 0))
    second = exchange(*cut(place, [image], bias[None], parts, "cut_second", 0))
    mark = token(first, 18)

    steps = halving(bands)[:-1]
    near, near_order = gather(near, steps)
    across, across_order = gather(across, steps[::-1])
    held = [near, swap(near, "band", 1), across, swap(across, "band", 1)]
    weights, extra = kernel(
        lambda *refs: assemble_kernel((near_order, across_order), *refs),
        [(taps * outs, 2 * local), (taps * 2 * local, 2 * local)],
        [place, filters, *held],
        [],
        "assemble",
        True,
        2,
    )
    rim = (8 * (width + 8), local)
    body = lambda *refs: rim_kernel(width, *refs)
    rims = neighbours(*kernel(body, [rim] * 2, edge, [], "rim", False, 16))

    out = [(rows * width, local)] * 2
    source = [(3, (rows + 2) * width, 4 * local)]
    args = [*edge, *first, *rims, weights, mark]
    mine, other = kernel(backward_kernel, out, args, source, "backward", False, 10)
    other = swap(other, "chan", 1)
    image_grad = home(place, mine, other, rows)
    args = [*edge, *after(second, mine), *rims, weights, extra]
    mine, sent = kernel(forward_kernel, out, args, source, "forward", False, 5)
    other = swap(after(sent, other), "chan", 1)
    return home(place, mine, other, rows), image_grad


def solution(mesh):
    return jax.shard_map(
        per_device,
        mesh=mesh,
        in_specs=(
            P("chan", "band", None),
            P(None, None, "chan"),
            P("chan"),
            P("chan", "band", None),
        ),
        out_specs=(P("chan", "band", None), P("chan", "band", None)),
        check_vma=False,
    )
```

```python
import jax
import jax.numpy as jnp
from jax import lax
from jax.experimental import pallas as pl
from jax.experimental.pallas import tpu as pltpu
from jax.sharding import PartitionSpec as P


def swap(value, axis, step):
    size = lax.axis_size(axis)
    return lax.ppermute(value, axis, [(j, j ^ step) for j in range(size)])


def neighbours(first, last):
    size = lax.axis_size("band")
    up = [(j, j + 1) for j in range(size - 1)]
    down = [(j + 1, j) for j in range(size - 1)]
    return lax.ppermute(last, "band", up), lax.ppermute(first, "band", down)


def pick(pieces, index, axis):
    stacked = jnp.stack(pieces)
    return jnp.concatenate(
        [lax.dynamic_index_in_dim(stacked, i, 0, keepdims=False) for i in index], axis=axis
    )


def spread(value, me, width):
    n = lax.axis_size("chan")
    padded = jnp.pad(value, ((0, 0), (1, 1), (0, 0)))
    pieces = []
    for k in range(n):
        piece = lax.dynamic_slice_in_dim(padded, (me ^ k) * width, width + 2, axis=1)
        pieces.append(swap(piece, "chan", k) if k else piece)
    return pieces


def add_rows(value):
    before, after = neighbours(value[:1], value[-1:])
    return jnp.concatenate([before, value, after], axis=0)


def conv(source, taps):
    return lax.conv_general_dilated(
        source[None],
        taps,
        (1, 1),
        "VALID",
        dimension_numbers=("NHWC", "HWIO", "NHWC"),
        preferred_element_type=jnp.float32,
    )[0]


def plain(image, filters, bias, upstream):
    n = lax.axis_size("chan")
    bands = lax.axis_size("band")
    me = lax.axis_index("chan")
    row = lax.axis_index("band")
    local = filters.shape[2]
    outs = filters.shape[1]
    width = image.shape[2] // n

    flat = filters.reshape(-1, local)
    share = flat.shape[0] // bands
    part = lax.dynamic_slice_in_dim(flat, row * share, share, axis=0)
    held = [jnp.concatenate([part, jnp.tile(bias[None], (16, 1))], axis=0)]
    step = n // 2
    while step:
        stacked = jnp.stack(held)
        there = swap(stacked, "chan", step)
        held = held + [there[j] for j in range(len(held))]
        step //= 2
    order = [0]
    step = n // 2
    while step:
        order = order + [o ^ step for o in order]
        step //= 2
    held = [held[order.index(k)] for k in range(n)]
    biases = [h[share] for h in held]
    whole = lax.all_gather(
        jnp.stack([h[:share] for h in held]), "band", axis=1, tiled=True
    ).reshape(n, 3, 3, outs, local)

    x_pieces = spread(jnp.transpose(image, (1, 2, 0)), me, width)
    u_pieces = spread(jnp.transpose(upstream, (1, 2, 0)), me, width)

    natural = [me ^ k for k in range(n)]
    x = add_rows(jnp.concatenate(x_pieces, axis=2))
    forward_taps = jnp.transpose(whole, (1, 2, 0, 4, 3)).reshape(3, 3, n * local, outs)
    total = conv(x, forward_taps) + pick(biases, natural, 0).astype(jnp.float32)
    features = back(total.astype(jnp.bfloat16), me, local, True)

    u = add_rows(pick(u_pieces, natural, 2))
    backward_taps = jnp.transpose(whole[:, ::-1, ::-1], (1, 2, 3, 0, 4)).reshape(
        3, 3, outs, n * local
    )
    image_grad = back(conv(u, backward_taps).astype(jnp.bfloat16), me, local, False)
    return features, image_grad


def back(value, me, local, is_natural):
    n = lax.axis_size("chan")
    pieces = []
    for k in range(n):
        start = (me ^ k) * local if is_natural else k * local
        piece = lax.dynamic_slice_in_dim(value, start, local, axis=2)
        pieces.append(swap(piece, "chan", k) if k else piece)
    whole = pick(pieces, [me ^ k for k in range(n)], 1)
    return jnp.transpose(whole, (2, 0, 1))


def assemble_kernel(orders, place, filters, near, near_far, across, across_far, weights, extra):
    me, band = place[0], place[1]
    taps, channels, local = filters.shape
    share = near.shape[1] // taps
    half = share // 2
    for tap in range(taps):
        for j in range(4):
            start = pl.multiple_of((me ^ j) * local, local)
            weights[pl.ds(tap * channels + j * local, local), :local] = filters[
                tap, pl.ds(start, local), :
            ]
    for bit, held in enumerate((near, near_far)):
        for j, d in enumerate(orders[0]):
            first = (band ^ (d | bit)) * share
            block = lax.div(first, local)
            start = (block ^ me) * local + first - block * local
            for tap in range(taps):
                row = pl.multiple_of(tap * channels + start, 16)
                weights[pl.ds(row, share), local:] = held[j, tap * share : (tap + 1) * share]
    for bit, held in enumerate((across, across_far)):
        for j, d in enumerate(orders[1]):
            first = (band ^ (d | bit)) * half
            block = lax.div(first, local)
            start = (block ^ (me & 1)) * local + first - block * local
            for tap in range(taps):
                row = pl.multiple_of(tap * 2 * local + start, 16)
                for k in range(2):
                    at = (k * taps + tap) * half
                    extra[pl.ds(row, half), k * local : (k + 1) * local] = held[j, at : at + half]


def cut_kernel(parts, place, *refs):
    sources, (bias, mine, other) = refs[:-3], refs[-3:]
    side = place[0] & 1
    local = bias.shape[1]
    width = sources[0].shape[1] // 2
    pitch = width + 8
    line = bias[...].astype(jnp.float32)
    zero = jnp.zeros((1, local), jnp.float32)
    rest = jnp.concatenate([line, zero, zero, zero, zero, zero])
    for n, (i, r) in enumerate(parts):
        source = sources[i]
        left = source[r, width - 16 : width].astype(jnp.float32)[15:]
        right = source[r, width : width + 16].astype(jnp.float32)[:1]
        pieces = []
        for t, (before, behind) in enumerate(((zero, right), (left, zero))):
            tail = jnp.concatenate([behind, line, rest]).astype(jnp.bfloat16)
            middle = source[r, t * width : (t + 1) * width]
            pieces.append(jnp.concatenate([before.astype(jnp.bfloat16), middle, tail[:7]]))
        at = n * pitch
        mine[at : at + pitch] = jnp.where(side == 0, pieces[0], pieces[1])
        other[at : at + pitch] = jnp.where(side == 0, pieces[1], pieces[0])


def rim_kernel(width, where, *refs):
    groups, (first, last) = [refs[at : at + 4] for at in range(0, len(refs) - 2, 4)], refs[-2:]
    pitch = width + 8
    for k in range(4):
        for i in range(2):
            for out, end in ((first, 0), (last, -1)):
                group, at = where[i][end]
                piece = groups[group][k][at * pitch : (at + 1) * pitch]
                out[(2 * k + i) * pitch : (2 * k + i + 1) * pitch] = piece


def fill_rows(target, piece, start, row, lanes, width):
    for shift in range(3):
        target[shift, row * width : (row + 1) * width, lanes] = piece[
            start + shift : start + shift + width
        ]


def fill_source(target, which, width, rows, before, after):
    local = before.shape[1]
    pitch = width + 8
    for k, held in enumerate(rows):
        lanes = slice(k * local, (k + 1) * local)
        held = [(before, 2 * k + which), *held, (after, 2 * k + which)]
        for r, (ref, at) in enumerate(held):
            fill_rows(target, ref, at * pitch, r, lanes, width)


def fill(source, which, where, refs, before, after, size):
    rows = [[(refs[4 * group + k], at) for group, at in where[which]] for k in range(4)]
    fill_source(source, which, size // len(where[which]), rows, before, after)


def backward_kernel(where, marks, *refs):
    mine, other, source = refs[-3:]
    before, after, weights = refs[-6 - marks : -3 - marks]
    size, local = mine.shape
    channels = 4 * local
    fill(source, 0, where, refs, before, after, size)
    width = size // len(where[0])
    acc = None
    for a in range(3):
        for b in range(3):
            term = jnp.dot(
                source[2 - b, pl.ds((2 - a) * width, size), :],
                weights[pl.ds((3 * a + b) * channels, channels), :],
                preferred_element_type=jnp.float32,
            )
            acc = term if acc is None else acc + term
    mine[...] = acc[:, :local].astype(jnp.bfloat16)
    other[...] = acc[:, local:].astype(jnp.bfloat16)


def forward_kernel(where, marks, *refs):
    mine, other, source = refs[-3:]
    before, after, weights, extra = refs[-7 - marks : -3 - marks]
    size, local = mine.shape
    channels, half = 4 * local, 2 * local
    fill(source, 1, where, refs, before, after, size)
    width = size // len(where[1])
    acc = None
    for a in range(3):
        for b in range(3):
            tap = 3 * a + b
            for part in range(2):
                if part:
                    filters = extra[pl.ds(tap * half, half), :]
                else:
                    filters = weights[pl.ds(tap * channels, half), :]
                term = lax.dot_general(
                    source[b, pl.ds(a * width, size), part * half : (part + 1) * half],
                    filters,
                    (((1,), (1,)), ((), ())),
                    preferred_element_type=jnp.float32,
                )
                acc = term if acc is None else acc + term
    group, at = where[1][0]
    at = at * (width + 8) + width
    for k, out in enumerate((mine, other)):
        bias = refs[4 * group + k][at : at + 8, :].astype(jnp.float32)[2:3]
        out[...] = (acc[:, k * local : (k + 1) * local] + bias).astype(jnp.bfloat16)


SMEM = pl.BlockSpec(memory_space=pltpu.SMEM)
VMEM = pl.BlockSpec(memory_space=pltpu.VMEM)
ANY = pl.BlockSpec(memory_space=pl.ANY)


def cost(microseconds):
    work = 2**20 + 10**9 * microseconds
    return pl.CostEstimate(flops=work, bytes_accessed=2**20, transcendentals=0)


def kernel(body, shapes, args, scratch, name, placed=False, micros=0):
    return pl.pallas_call(
        body,
        out_shape=[jax.ShapeDtypeStruct(s, jnp.bfloat16) for s in shapes],
        in_specs=[SMEM] * placed + [VMEM] * (len(args) - placed),
        out_specs=[VMEM] * len(shapes),
        scratch_shapes=[pltpu.VMEM(s, jnp.bfloat16) for s in scratch],
        compiler_params=pltpu.CompilerParams(vmem_limit_bytes=20 * 2**20),
        cost_estimate=cost(micros),
        name=name,
    )(*args)


def cut(place, sources, bias, parts, name, micros):
    local = bias.shape[1]
    shape = (len(parts) * (sources[0].shape[1] // 2 + 8), local)
    body = lambda *refs: cut_kernel(parts, *refs)
    return kernel(body, [shape] * 2, [place, *sources, bias], [], name, True, micros)


def exchange(mine, other):
    held = {k: swap(other if k & 1 else mine, "chan", k) for k in (2, 3, 1)}
    return [mine, held[1], held[2], held[3]]


def after(value, *others):
    return lax.optimization_barrier((value, others))[0]


def gather(value, steps):
    held, order = value[None], [0]
    for step in steps:
        held = jnp.concatenate([held, swap(held, "band", step)])
        order = order + [o ^ step for o in order]
    return held, order


def halving(size):
    steps = []
    while size > 1:
        size //= 2
        steps.append(size)
    return steps


def home_kernel(place, mine, other, out):
    width = mine.shape[2]
    side = place[0] & 1
    for t in range(2):

        @pl.when(side == t)
        def _():
            out[:, :, t * width : (t + 1) * width] = mine[...]
            out[:, :, (1 - t) * width : (2 - t) * width] = other[...]


def home(place, mine, other, rows):
    turn = lambda p: jnp.transpose(p.reshape(rows, -1, p.shape[1]), (2, 0, 1))
    mine, other = turn(mine), turn(other)
    channels, rows, width = mine.shape
    shape = (channels, rows, 2 * width)
    return kernel(home_kernel, [shape], [place, mine, other], [], "home", True)[0]


def token_kernel(*refs):
    refs[-1][...] = jnp.zeros_like(refs[-1])


def token(pieces, micros):
    return kernel(token_kernel, [(16, 128)], pieces, [], "token", False, micros)[0]


def per_device(image, filters, bias, upstream):
    n = lax.axis_size("chan")
    bands = lax.axis_size("band")
    taps, outs, local = filters.shape
    rows, cols = image.shape[1:]
    if n != 4 or local % 128 or cols % 256 or rows < 3 or outs % (32 * bands) or bands < 4:
        return plain(image, filters, bias, upstream)
    me = lax.axis_index("chan")
    band = lax.axis_index("band")
    half = me >> 1
    place = jnp.stack([me, band]).astype(jnp.int32)
    width = cols // 2

    share = outs // bands
    near = lax.dynamic_slice_in_dim(filters, band * share, share, axis=1).reshape(-1, local)
    start = (1 - half) * (outs // 2) + band * (share // 2)
    across = lax.dynamic_slice_in_dim(filters, start, share // 2, axis=1).reshape(-1, local)
    near = swap(near, "chan", 1)
    across = jnp.concatenate([swap(across, "chan", k) for k in (2, 3)])

    upstream, image = [jnp.transpose(v, (1, 2, 0)) for v in (upstream, image)]
    edges = [(i, r) for i in range(2) for r in (0, rows - 1)]
    groups = [edges, [(i, r) for i in range(2) for r in range(1, rows - 1)]]
    spot = {part: (g, at) for g, parts in enumerate(groups) for at, part in enumerate(parts)}
    where = [[spot[i, r] for r in range(rows)] for i in range(2)]
    needed = [sorted({g for g, _ in rows_of}) for rows_of in where]
    where = [[(need.index(g), at) for g, at in rows_of] for need, rows_of in zip(needed, where)]
    ends = [[rows_of[0], rows_of[-1]] for rows_of in where]

    sent = cut(place, [upstream, image], bias[None], groups[0], "cut", 0)
    got = [exchange(*sent)]
    sent = cut(place, after([upstream, image], got[-1][3]), bias[None], groups[1], "cut", 40)
    got[0] = after(got[0], sent)
    got.append(exchange(*sent))
    marks = [[], []]
    marks[0].append(token(got[1], 13))

    steps = halving(bands)[:-1]
    near, near_order = gather(near, steps)
    across, across_order = gather(across, steps[::-1])
    near, across = after((near, across), got[0][1:])
    held = jnp.concatenate([near, across], axis=1)
    there = swap(held, "band", 1)
    cutoff = near.shape[1]
    held = [near, there[:, :cutoff], across, there[:, cutoff:]]
    weights, extra = kernel(
        lambda *refs: assemble_kernel((near_order, across_order), *refs),
        [(taps * outs, 2 * local), (taps * 2 * local, 2 * local)],
        [place, filters, *held],
        [],
        "assemble",
        True,
        0,
    )
    rim = (8 * (width + 8), local)
    pieces = [p for p in after(got[0], held)]
    body = lambda *refs: rim_kernel(width, ends, *refs)
    rims = neighbours(*kernel(body, [rim] * 2, pieces, [], "rim", False, 0))

    out = [(rows * width, local)] * 2
    source = [(3, (rows + 2) * width, 4 * local)]
    args = [p for g in needed[0] for p in got[g]] + [*rims, weights, *marks[0]]
    body = lambda *refs: backward_kernel(where, len(marks[0]), *refs)
    mine, other = kernel(body, out, args, source, "backward", False, 4)
    other = swap(other, "chan", 1)
    image_grad = home(place, mine, other, rows)
    args = [p for g in needed[1] for p in got[g]] + [*rims, weights, extra, *marks[1]]
    body = lambda *refs: forward_kernel(where, len(marks[1]), *refs)
    mine, sent = kernel(body, out, args, source, "forward", False, 2)
    other = swap(sent, "chan", 1)
    return home(place, mine, other, rows), image_grad


def solution(mesh):
    return jax.shard_map(
        per_device,
        mesh=mesh,
        in_specs=(
            P("chan", "band", None),
            P(None, None, "chan"),
            P("chan"),
            P("chan", "band", None),
        ),
        out_specs=(P("chan", "band", None), P("chan", "band", None)),
        check_vma=False,
    )
```

```python
import jax
import jax.numpy as jnp
from jax import lax
from jax.experimental import pallas as pl
from jax.experimental.pallas import tpu as pltpu
from jax.sharding import PartitionSpec as P


def swap(value, axis, step):
    size = lax.axis_size(axis)
    return lax.ppermute(value, axis, [(j, j ^ step) for j in range(size)])


def neighbours(first, last):
    size = lax.axis_size("band")
    up = [(j, j + 1) for j in range(size - 1)]
    down = [(j + 1, j) for j in range(size - 1)]
    return lax.ppermute(last, "band", up), lax.ppermute(first, "band", down)


def pick(pieces, index, axis):
    stacked = jnp.stack(pieces)
    return jnp.concatenate(
        [lax.dynamic_index_in_dim(stacked, i, 0, keepdims=False) for i in index], axis=axis
    )


def spread(value, me, width):
    n = lax.axis_size("chan")
    padded = jnp.pad(value, ((0, 0), (1, 1), (0, 0)))
    pieces = []
    for k in range(n):
        piece = lax.dynamic_slice_in_dim(padded, (me ^ k) * width, width + 2, axis=1)
        pieces.append(swap(piece, "chan", k) if k else piece)
    return pieces


def add_rows(value):
    before, after = neighbours(value[:1], value[-1:])
    return jnp.concatenate([before, value, after], axis=0)


def conv(source, taps):
    return lax.conv_general_dilated(
        source[None],
        taps,
        (1, 1),
        "VALID",
        dimension_numbers=("NHWC", "HWIO", "NHWC"),
        preferred_element_type=jnp.float32,
    )[0]


def plain(image, filters, bias, upstream):
    n = lax.axis_size("chan")
    bands = lax.axis_size("band")
    me = lax.axis_index("chan")
    row = lax.axis_index("band")
    local = filters.shape[2]
    outs = filters.shape[1]
    width = image.shape[2] // n

    flat = filters.reshape(-1, local)
    share = flat.shape[0] // bands
    part = lax.dynamic_slice_in_dim(flat, row * share, share, axis=0)
    held = [jnp.concatenate([part, jnp.tile(bias[None], (16, 1))], axis=0)]
    step = n // 2
    while step:
        stacked = jnp.stack(held)
        there = swap(stacked, "chan", step)
        held = held + [there[j] for j in range(len(held))]
        step //= 2
    order = [0]
    step = n // 2
    while step:
        order = order + [o ^ step for o in order]
        step //= 2
    held = [held[order.index(k)] for k in range(n)]
    biases = [h[share] for h in held]
    whole = lax.all_gather(
        jnp.stack([h[:share] for h in held]), "band", axis=1, tiled=True
    ).reshape(n, 3, 3, outs, local)

    x_pieces = spread(jnp.transpose(image, (1, 2, 0)), me, width)
    u_pieces = spread(jnp.transpose(upstream, (1, 2, 0)), me, width)

    natural = [me ^ k for k in range(n)]
    x = add_rows(jnp.concatenate(x_pieces, axis=2))
    forward_taps = jnp.transpose(whole, (1, 2, 0, 4, 3)).reshape(3, 3, n * local, outs)
    total = conv(x, forward_taps) + pick(biases, natural, 0).astype(jnp.float32)
    features = back(total.astype(jnp.bfloat16), me, local, True)

    u = add_rows(pick(u_pieces, natural, 2))
    backward_taps = jnp.transpose(whole[:, ::-1, ::-1], (1, 2, 3, 0, 4)).reshape(
        3, 3, outs, n * local
    )
    image_grad = back(conv(u, backward_taps).astype(jnp.bfloat16), me, local, False)
    return features, image_grad


def back(value, me, local, is_natural):
    n = lax.axis_size("chan")
    pieces = []
    for k in range(n):
        start = (me ^ k) * local if is_natural else k * local
        piece = lax.dynamic_slice_in_dim(value, start, local, axis=2)
        pieces.append(swap(piece, "chan", k) if k else piece)
    whole = pick(pieces, [me ^ k for k in range(n)], 1)
    return jnp.transpose(whole, (2, 0, 1))


def assemble_kernel(orders, place, filters, near, near_far, across, across_far, weights, extra):
    me, band = place[0], place[1]
    taps, channels, local = filters.shape
    share = near.shape[1] // taps
    half = share // 2
    for tap in range(taps):
        for j in range(4):
            start = pl.multiple_of((me ^ j) * local, local)
            weights[pl.ds(tap * channels + j * local, local), :local] = filters[
                tap, pl.ds(start, local), :
            ]
    for bit, held in enumerate((near, near_far)):
        for j, d in enumerate(orders[0]):
            first = (band ^ (d | bit)) * share
            block = lax.div(first, local)
            start = (block ^ me) * local + first - block * local
            for tap in range(taps):
                row = pl.multiple_of(tap * channels + start, 16)
                weights[pl.ds(row, share), local:] = held[j, tap * share : (tap + 1) * share]
    for bit, held in enumerate((across, across_far)):
        for j, d in enumerate(orders[1]):
            first = (band ^ (d | bit)) * half
            block = lax.div(first, local)
            start = (block ^ (me & 1)) * local + first - block * local
            for tap in range(taps):
                row = pl.multiple_of(tap * 2 * local + start, 16)
                for k in range(2):
                    at = (k * taps + tap) * half
                    extra[pl.ds(row, half), k * local : (k + 1) * local] = held[j, at : at + half]


def cut_kernel(parts, place, *refs):
    sources, (bias, mine, other) = refs[:-3], refs[-3:]
    side = place[0] & 1
    local = bias.shape[1]
    width = sources[0].shape[1] // 2
    pitch = width + 8
    line = bias[...].astype(jnp.float32)
    zero = jnp.zeros((1, local), jnp.float32)
    rest = jnp.concatenate([line, zero, zero, zero, zero, zero])
    for n, (i, r) in enumerate(parts):
        source = sources[i]
        left = source[r, width - 16 : width].astype(jnp.float32)[15:]
        right = source[r, width : width + 16].astype(jnp.float32)[:1]
        pieces = []
        for t, (before, behind) in enumerate(((zero, right), (left, zero))):
            tail = jnp.concatenate([behind, line, rest]).astype(jnp.bfloat16)
            middle = source[r, t * width : (t + 1) * width]
            pieces.append(jnp.concatenate([before.astype(jnp.bfloat16), middle, tail[:7]]))
        at = n * pitch
        mine[at : at + pitch] = jnp.where(side == 0, pieces[0], pieces[1])
        other[at : at + pitch] = jnp.where(side == 0, pieces[1], pieces[0])


def rim_kernel(pitch, *refs):
    pieces, (first, last) = refs[:4], refs[4:]
    for k, piece in enumerate(pieces):
        for i in range(2):
            for out, end in ((first, 0), (last, 1)):
                at = (2 * i + end) * pitch
                out[(2 * k + i) * pitch : (2 * k + i + 1) * pitch] = piece[at : at + pitch]


def fill(target, rows):
    width = target.shape[1] // len(rows)
    for r, row in enumerate(rows):
        for k, (ref, start) in enumerate(row):
            local = ref.shape[1]
            for shift in range(3):
                target[
                    shift, r * width : (r + 1) * width, k * local : (k + 1) * local
                ] = ref[start + shift : start + shift + width]


def product(which, source, at, size, weights, extra, down, across):
    half = weights.shape[1]
    if which == 0:
        tap = 3 * (2 - down) + across
        filters = weights[pl.ds(tap * 2 * half, 2 * half), :]
        return jnp.dot(
            source[2 - across, at : at + size], filters, preferred_element_type=jnp.float32
        )
    tap = 3 * down + across
    total = None
    for block in range(2):
        if block:
            filters = extra[pl.ds(tap * half, half), :]
        else:
            filters = weights[pl.ds(tap * 2 * half, half), :]
        term = lax.dot_general(
            source[across, at : at + size, block * half : (block + 1) * half],
            filters,
            (((1,), (1,)), ((), ())),
            preferred_element_type=jnp.float32,
        )
        total = term if total is None else total + term
    return total


def outer_kernel(*refs):
    pieces, (before, after, weights, extra), (*totals, upstream, image) = (
        refs[:4],
        refs[4:8],
        refs[8:],
    )
    pitch = before.shape[0] // 8
    for which, (total, source) in enumerate(zip(totals, (upstream, image))):
        rims = [[(rim, (2 * k + which) * pitch) for k in range(4)] for rim in (before, after)]
        edges = [[(p, (2 * which + end) * pitch) for p in pieces] for end in range(2)]
        fill(source, [rims[0], *edges, rims[1]])
        size = total.shape[0] // 2
        row = size // 2
        top = middle = bottom = None
        for across in range(3):
            terms = [
                product(which, source, at, size, weights, extra, down, across)
                for down, at in ((0, 0), (1, row), (2, size))
            ]
            if across:
                terms = [old + term for old, term in zip((top, middle, bottom), terms)]
            top, middle, bottom = terms
        total[:row] = top[:row] + middle[:row]
        total[row:size] = top[row:]
        total[size : size + row] = bottom[:row]
        total[size + row :] = bottom[row:] + middle[row:]


def inner_kernel(which, *refs):
    inners, (total, weights, extra, lines) = refs[:4], refs[4:8]
    mine, other, source = refs[-3:]
    size = total.shape[0] // 2
    row = size // 2
    local = mine.shape[1]
    pitch = row + 8
    fill(source, [[(p, (2 * which + r) * pitch) for p in inners] for r in range(2)])
    top = middle = bottom = None
    for across in range(3):
        terms = [
            product(which, source, 0, size, weights, extra, down, across) for down in (2, 1, 0)
        ]
        if across:
            terms = [old + term for old, term in zip((top, middle, bottom), terms)]
        top, middle, bottom = terms
    parts = [top[:row], top[row:] + middle[:row], middle[row:] + bottom[:row], bottom[row:]]
    for r, part in enumerate(parts):
        value = total[r * row : (r + 1) * row] + part
        for k, out in enumerate((mine, other)):
            block = value[:, k * local : (k + 1) * local]
            if which:
                block = block + lines[k : k + 1, :]
            out[r * row : (r + 1) * row] = block.astype(jnp.bfloat16)


SMEM = pl.BlockSpec(memory_space=pltpu.SMEM)
VMEM = pl.BlockSpec(memory_space=pltpu.VMEM)
ANY = pl.BlockSpec(memory_space=pl.ANY)


def cost(microseconds):
    work = 2**20 + 10**9 * microseconds
    return pl.CostEstimate(flops=work, bytes_accessed=2**20, transcendentals=0)


def kernel(body, shapes, args, scratch, name, placed=False, micros=0, kind=jnp.bfloat16):
    return pl.pallas_call(
        body,
        out_shape=[jax.ShapeDtypeStruct(s, kind) for s in shapes],
        in_specs=[SMEM] * placed + [VMEM] * (len(args) - placed),
        out_specs=[VMEM] * len(shapes),
        scratch_shapes=[pltpu.VMEM(s, jnp.bfloat16) for s in scratch],
        compiler_params=pltpu.CompilerParams(vmem_limit_bytes=20 * 2**20),
        cost_estimate=cost(micros),
        name=name,
    )(*args)


def cut(place, sources, bias, parts, micros):
    local = bias.shape[1]
    shape = (len(parts) * (sources[0].shape[1] // 2 + 8), local)
    body = lambda *refs: cut_kernel(parts, *refs)
    return kernel(body, [shape] * 2, [place, *sources, bias], [], "cut", True, micros)


def exchange(mine, other, near=None):
    sent = {1: other if near is None else near, 2: mine, 3: other}
    held = {k: swap(sent[k], "chan", k) for k in (2, 3, 1)}
    return [mine, held[1], held[2], held[3]]


def after(value, *others):
    return lax.optimization_barrier((value, others))[0]


def gather(value, steps):
    held, order = value[None], [0]
    for step in steps:
        held = jnp.concatenate([held, swap(held, "band", step)])
        order = order + [o ^ step for o in order]
    return held, order


def halving(size):
    steps = []
    while size > 1:
        size //= 2
        steps.append(size)
    return steps


def home_kernel(place, mine, other, out):
    width = mine.shape[2]
    side = place[0] & 1
    for t in range(2):

        @pl.when(side == t)
        def _():
            out[:, :, t * width : (t + 1) * width] = mine[...]
            out[:, :, (1 - t) * width : (2 - t) * width] = other[...]


def home(place, mine, other, rows):
    turn = lambda p: jnp.transpose(p.reshape(rows, -1, p.shape[1]), (2, 0, 1))
    mine, other = turn(mine), turn(other)
    channels, rows, width = mine.shape
    shape = (channels, rows, 2 * width)
    return kernel(home_kernel, [shape], [place, mine, other], [], "home", True)[0]


def token_kernel(*refs):
    refs[-1][...] = jnp.zeros_like(refs[-1])


def token(pieces, micros):
    return kernel(token_kernel, [(16, 128)], pieces, [], "token", False, micros)[0]


def per_device(image, filters, bias, upstream):
    n = lax.axis_size("chan")
    bands = lax.axis_size("band")
    taps, outs, local = filters.shape
    rows, cols = image.shape[1:]
    if n != 4 or local % 128 or cols % 256 or rows != 4 or outs % (32 * bands) or bands < 4:
        return plain(image, filters, bias, upstream)
    me = lax.axis_index("chan")
    band = lax.axis_index("band")
    half = me >> 1
    place = jnp.stack([me, band]).astype(jnp.int32)
    width = cols // 2

    share = outs // bands
    near = lax.dynamic_slice_in_dim(filters, band * share, share, axis=1).reshape(-1, local)
    start = (1 - half) * (outs // 2) + band * (share // 2)
    across = lax.dynamic_slice_in_dim(filters, start, share // 2, axis=1).reshape(-1, local)
    near = swap(near, "chan", 1)
    across = jnp.concatenate([swap(across, "chan", k) for k in (2, 3)])

    upstream, image = [jnp.transpose(v, (1, 2, 0)) for v in (upstream, image)]
    parts = [(i, r) for i in range(2) for r in (0, rows - 1)]
    sent = cut(place, [upstream, image], bias[None], parts, 25)
    (near, across) = after((near, across), sent)
    pieces = exchange(*sent)
    parts = [(i, r) for i in range(2) for r in range(1, rows - 1)]
    sent = cut(place, after([upstream, image], pieces[1]), bias[None], parts, 25)
    pieces = after(pieces, sent)
    inners = exchange(*sent)

    steps = halving(bands)[:-1]
    near, near_order = gather(near, steps)
    across, across_order = gather(across, steps[::-1])
    held = [near, swap(near, "band", 1), across, swap(across, "band", 1)]
    filters = kernel(
        lambda *refs: assemble_kernel((near_order, across_order), *refs),
        [(taps * outs, 2 * local), (taps * 2 * local, 2 * local)],
        [place, filters, *held],
        [],
        "assemble",
        True,
        9,
    )
    pitch = width + 8
    body = lambda *refs: rim_kernel(pitch, *refs)
    rims = neighbours(*kernel(body, [(8 * pitch, local)] * 2, pieces, [], "rim", False, 40))

    size = rows * width
    totals = kernel(
        outer_kernel,
        [(size, 2 * local)] * 2,
        [*pieces, *rims, *filters],
        [(3, size, 4 * local)] * 2,
        "outer",
        False,
        6,
        jnp.float32,
    )
    lines = jnp.concatenate([p[width + 2 : width + 3] for p in pieces[:2]]).astype(jnp.float32)
    inners = after(inners, totals)
    mark = [token(inners, 0)]
    kept, came = [], []
    for which in range(2):
        mine, other = kernel(
            lambda *refs: inner_kernel(which, *refs),
            [(size, local)] * 2,
            [*inners, totals[which], *filters, lines, *mark],
            [(3, size // 2, 4 * local)],
            "inner",
            False,
            9,
        )
        kept.append(mine)
        came.append(swap(other, "chan", 1))
    image_grad = home(place, kept[0], came[0], rows)
    kept[1] = after(kept[1], image_grad)
    return home(place, kept[1], came[1], rows), image_grad


def solution(mesh):
    return jax.shard_map(
        per_device,
        mesh=mesh,
        in_specs=(
            P("chan", "band", None),
            P(None, None, "chan"),
            P("chan"),
            P("chan", "band", None),
        ),
        out_specs=(P("chan", "band", None), P("chan", "band", None)),
        check_vma=False,
    )
```

```python
import jax
import jax.numpy as jnp
from jax import lax
from jax.experimental import pallas as pl
from jax.experimental.pallas import tpu as pltpu
from jax.sharding import PartitionSpec as P


def swap(value, axis, step):
    size = lax.axis_size(axis)
    return lax.ppermute(value, axis, [(j, j ^ step) for j in range(size)])


def neighbours(first, last):
    size = lax.axis_size("band")
    up = [(j, j + 1) for j in range(size - 1)]
    down = [(j + 1, j) for j in range(size - 1)]
    return lax.ppermute(last, "band", up), lax.ppermute(first, "band", down)


def pick(pieces, index, axis):
    stacked = jnp.stack(pieces)
    return jnp.concatenate(
        [lax.dynamic_index_in_dim(stacked, i, 0, keepdims=False) for i in index], axis=axis
    )


def spread(value, me, width):
    n = lax.axis_size("chan")
    padded = jnp.pad(value, ((0, 0), (1, 1), (0, 0)))
    pieces = []
    for k in range(n):
        piece = lax.dynamic_slice_in_dim(padded, (me ^ k) * width, width + 2, axis=1)
        pieces.append(swap(piece, "chan", k) if k else piece)
    return pieces


def add_rows(value):
    before, after = neighbours(value[:1], value[-1:])
    return jnp.concatenate([before, value, after], axis=0)


def conv(source, taps):
    return lax.conv_general_dilated(
        source[None],
        taps,
        (1, 1),
        "VALID",
        dimension_numbers=("NHWC", "HWIO", "NHWC"),
        preferred_element_type=jnp.float32,
    )[0]


def plain(image, filters, bias, upstream):
    n = lax.axis_size("chan")
    bands = lax.axis_size("band")
    me = lax.axis_index("chan")
    row = lax.axis_index("band")
    local = filters.shape[2]
    outs = filters.shape[1]
    width = image.shape[2] // n

    flat = filters.reshape(-1, local)
    share = flat.shape[0] // bands
    part = lax.dynamic_slice_in_dim(flat, row * share, share, axis=0)
    held = [jnp.concatenate([part, jnp.tile(bias[None], (16, 1))], axis=0)]
    step = n // 2
    while step:
        stacked = jnp.stack(held)
        there = swap(stacked, "chan", step)
        held = held + [there[j] for j in range(len(held))]
        step //= 2
    order = [0]
    step = n // 2
    while step:
        order = order + [o ^ step for o in order]
        step //= 2
    held = [held[order.index(k)] for k in range(n)]
    biases = [h[share] for h in held]
    whole = lax.all_gather(
        jnp.stack([h[:share] for h in held]), "band", axis=1, tiled=True
    ).reshape(n, 3, 3, outs, local)

    x_pieces = spread(jnp.transpose(image, (1, 2, 0)), me, width)
    u_pieces = spread(jnp.transpose(upstream, (1, 2, 0)), me, width)

    natural = [me ^ k for k in range(n)]
    x = add_rows(jnp.concatenate(x_pieces, axis=2))
    forward_taps = jnp.transpose(whole, (1, 2, 0, 4, 3)).reshape(3, 3, n * local, outs)
    total = conv(x, forward_taps) + pick(biases, natural, 0).astype(jnp.float32)
    features = back(total.astype(jnp.bfloat16), me, local, True)

    u = add_rows(pick(u_pieces, natural, 2))
    backward_taps = jnp.transpose(whole[:, ::-1, ::-1], (1, 2, 3, 0, 4)).reshape(
        3, 3, outs, n * local
    )
    image_grad = back(conv(u, backward_taps).astype(jnp.bfloat16), me, local, False)
    return features, image_grad


def back(value, me, local, is_natural):
    n = lax.axis_size("chan")
    pieces = []
    for k in range(n):
        start = (me ^ k) * local if is_natural else k * local
        piece = lax.dynamic_slice_in_dim(value, start, local, axis=2)
        pieces.append(swap(piece, "chan", k) if k else piece)
    whole = pick(pieces, [me ^ k for k in range(n)], 1)
    return jnp.transpose(whole, (2, 0, 1))


def assemble_kernel(orders, place, filters, near, near_far, across, across_far, weights, extra):
    me, band = place[0], place[1]
    taps, channels, local = filters.shape
    share = near.shape[1] // taps
    half = share // 2
    for tap in range(taps):
        for j in range(4):
            start = pl.multiple_of((me ^ j) * local, local)
            weights[pl.ds(tap * channels + j * local, local), :local] = filters[
                tap, pl.ds(start, local), :
            ]
    for bit, held in enumerate((near, near_far)):
        for j, d in enumerate(orders[0]):
            first = (band ^ (d | bit)) * share
            block = lax.div(first, local)
            start = (block ^ me) * local + first - block * local
            for tap in range(taps):
                row = pl.multiple_of(tap * channels + start, 16)
                weights[pl.ds(row, share), local:] = held[j, tap * share : (tap + 1) * share]
    for bit, held in enumerate((across, across_far)):
        for j, d in enumerate(orders[1]):
            first = (band ^ (d | bit)) * half
            block = lax.div(first, local)
            start = (block ^ (me & 1)) * local + first - block * local
            for tap in range(taps):
                row = pl.multiple_of(tap * 2 * local + start, 16)
                for k in range(2):
                    at = (k * taps + tap) * half
                    extra[pl.ds(row, half), k * local : (k + 1) * local] = held[j, at : at + half]


def cut_kernel(parts, place, *refs):
    sources, (bias, mine, other) = refs[:-3], refs[-3:]
    side = place[0] & 1
    local = bias.shape[1]
    width = sources[0].shape[1] // 2
    pitch = width + 8
    line = bias[...].astype(jnp.float32)
    zero = jnp.zeros((1, local), jnp.float32)
    rest = jnp.concatenate([line, zero, zero, zero, zero, zero])
    for n, (i, r) in enumerate(parts):
        source = sources[i]
        left = source[r, width - 16 : width].astype(jnp.float32)[15:]
        right = source[r, width : width + 16].astype(jnp.float32)[:1]
        pieces = []
        for t, (before, behind) in enumerate(((zero, right), (left, zero))):
            tail = jnp.concatenate([behind, line, rest]).astype(jnp.bfloat16)
            middle = source[r, t * width : (t + 1) * width]
            pieces.append(jnp.concatenate([before.astype(jnp.bfloat16), middle, tail[:7]]))
        at = n * pitch
        mine[at : at + pitch] = jnp.where(side == 0, pieces[0], pieces[1])
        other[at : at + pitch] = jnp.where(side == 0, pieces[1], pieces[0])


def rim_kernel(pitch, *refs):
    pieces, (first, last) = refs[:4], refs[4:]
    for k, piece in enumerate(pieces):
        for i in range(2):
            for out, end in ((first, 0), (last, 1)):
                at = (2 * i + end) * pitch
                out[(2 * k + i) * pitch : (2 * k + i + 1) * pitch] = piece[at : at + pitch]


def fill(target, rows):
    width = target.shape[1] // len(rows)
    for r, row in enumerate(rows):
        for k, (ref, start) in enumerate(row):
            local = ref.shape[1]
            for shift in range(3):
                target[
                    shift, r * width : (r + 1) * width, k * local : (k + 1) * local
                ] = ref[start + shift : start + shift + width]


def product(which, source, at, size, weights, extra, down, across):
    half = weights.shape[1]
    if which == 0:
        tap = 3 * (2 - down) + across
        filters = weights[pl.ds(tap * 2 * half, 2 * half), :]
        return jnp.dot(
            source[2 - across, at : at + size], filters, preferred_element_type=jnp.float32
        )
    tap = 3 * down + across
    total = None
    for block in range(2):
        if block:
            filters = extra[pl.ds(tap * half, half), :]
        else:
            filters = weights[pl.ds(tap * 2 * half, half), :]
        term = lax.dot_general(
            source[across, at : at + size, block * half : (block + 1) * half],
            filters,
            (((1,), (1,)), ((), ())),
            preferred_element_type=jnp.float32,
        )
        total = term if total is None else total + term
    return total


def outer_kernel(*refs):
    pieces, (before, after, weights, extra), (*totals, upstream, image) = (
        refs[:4],
        refs[4:8],
        refs[8:],
    )
    pitch = before.shape[0] // 8
    for which, (total, source) in enumerate(zip(totals, (upstream, image))):
        rims = [[(rim, (2 * k + which) * pitch) for k in range(4)] for rim in (before, after)]
        edges = [[(p, (2 * which + end) * pitch) for p in pieces] for end in range(2)]
        fill(source, [rims[0], *edges, rims[1]])
        size = total.shape[0] // 2
        row = size // 2
        top = middle = bottom = None
        for across in range(3):
            terms = [
                product(which, source, at, size, weights, extra, down, across)
                for down, at in ((0, 0), (1, row), (2, size))
            ]
            if across:
                terms = [old + term for old, term in zip((top, middle, bottom), terms)]
            top, middle, bottom = terms
        total[:row] = top[:row] + middle[:row]
        total[row:size] = top[row:]
        total[size : size + row] = bottom[:row]
        total[size + row :] = bottom[row:] + middle[row:]


def inner_kernel(which, *refs):
    inners, (total, weights, extra, lines) = refs[:4], refs[4:8]
    mine, other, source = refs[-3:]
    size = total.shape[0] // 2
    row = size // 2
    local = mine.shape[1]
    pitch = row + 8
    fill(source, [[(p, r * pitch) for p in inners] for r in range(2)])
    top = middle = bottom = None
    for across in range(3):
        terms = [
            product(which, source, 0, size, weights, extra, down, across) for down in (2, 1, 0)
        ]
        if across:
            terms = [old + term for old, term in zip((top, middle, bottom), terms)]
        top, middle, bottom = terms
    parts = [top[:row], top[row:] + middle[:row], middle[row:] + bottom[:row], bottom[row:]]
    for r, part in enumerate(parts):
        value = total[r * row : (r + 1) * row] + part
        for k, out in enumerate((mine, other)):
            block = value[:, k * local : (k + 1) * local]
            if which:
                block = block + lines[k : k + 1, :]
            out[r * row : (r + 1) * row] = block.astype(jnp.bfloat16)


SMEM = pl.BlockSpec(memory_space=pltpu.SMEM)
VMEM = pl.BlockSpec(memory_space=pltpu.VMEM)
ANY = pl.BlockSpec(memory_space=pl.ANY)


def cost(microseconds):
    work = 2**20 + 10**9 * microseconds
    return pl.CostEstimate(flops=work, bytes_accessed=2**20, transcendentals=0)


def kernel(body, shapes, args, scratch, name, placed=False, micros=0, kind=jnp.bfloat16):
    return pl.pallas_call(
        body,
        out_shape=[jax.ShapeDtypeStruct(s, kind) for s in shapes],
        in_specs=[SMEM] * placed + [VMEM] * (len(args) - placed),
        out_specs=[VMEM] * len(shapes),
        scratch_shapes=[pltpu.VMEM(s, jnp.bfloat16) for s in scratch],
        compiler_params=pltpu.CompilerParams(vmem_limit_bytes=20 * 2**20),
        cost_estimate=cost(micros),
        name=name,
    )(*args)


def cut(place, sources, bias, parts, micros):
    local = bias.shape[1]
    shape = (len(parts) * (sources[0].shape[1] // 2 + 8), local)
    body = lambda *refs: cut_kernel(parts, *refs)
    return kernel(body, [shape] * 2, [place, *sources, bias], [], "cut", True, micros)


def exchange(mine, other, near=None):
    sent = {1: other if near is None else near, 2: mine, 3: other}
    held = {k: swap(sent[k], "chan", k) for k in (1, 2, 3)}
    return [mine, held[1], held[2], held[3]]


def after(value, *others):
    return lax.optimization_barrier((value, others))[0]


def gather(value, steps):
    held, order = value[None], [0]
    for step in steps:
        held = jnp.concatenate([held, swap(held, "band", step)])
        order = order + [o ^ step for o in order]
    return held, order


def halving(size):
    steps = []
    while size > 1:
        size //= 2
        steps.append(size)
    return steps


def place_kernel(slot, piece, *refs):
    refs[-1][...] = piece[...]


def put(slot, piece, whole, cols):
    channels, rows, width = piece.shape
    block = pl.BlockSpec((channels, rows, width), lambda i, slot: (0, 0, 0))
    spot = pl.BlockSpec((channels, rows, width), lambda i, slot: (0, 0, slot[0]))
    return pl.pallas_call(
        place_kernel,
        out_shape=jax.ShapeDtypeStruct((channels, rows, cols), jnp.bfloat16),
        grid_spec=pltpu.PrefetchScalarGridSpec(
            num_scalar_prefetch=1,
            grid=(1,),
            in_specs=[block] + [ANY] * len(whole),
            out_specs=spot,
        ),
        input_output_aliases={2: 0} if whole else {},
        cost_estimate=cost(0),
        name="put",
    )(slot, piece, *whole)


def home(place, mine, other, rows):
    side = place[:1] & 1
    mine, other = [
        jnp.transpose(p.reshape(rows, -1, p.shape[1]), (2, 0, 1)) for p in (mine, other)
    ]
    cols = 2 * mine.shape[2]
    return put(1 - side, other, [put(side, mine, [], cols)], cols)


def token_kernel(*refs):
    refs[-1][...] = jnp.zeros_like(refs[-1])


def token(pieces, micros):
    return kernel(token_kernel, [(16, 128)], pieces, [], "token", False, micros)[0]


def per_device(image, filters, bias, upstream):
    n = lax.axis_size("chan")
    bands = lax.axis_size("band")
    taps, outs, local = filters.shape
    rows, cols = image.shape[1:]
    if n != 4 or local % 128 or cols % 256 or rows != 4 or outs % (32 * bands) or bands < 4:
        return plain(image, filters, bias, upstream)
    me = lax.axis_index("chan")
    band = lax.axis_index("band")
    half = me >> 1
    place = jnp.stack([me, band]).astype(jnp.int32)
    width = cols // 2

    share = outs // bands
    near = lax.dynamic_slice_in_dim(filters, band * share, share, axis=1).reshape(-1, local)
    start = (1 - half) * (outs // 2) + band * (share // 2)
    across = lax.dynamic_slice_in_dim(filters, start, share // 2, axis=1).reshape(-1, local)
    near = swap(near, "chan", 1)
    across = jnp.concatenate([swap(across, "chan", k) for k in (2, 3)])

    upstream, image = [jnp.transpose(v, (1, 2, 0)) for v in (upstream, image)]
    parts = [(i, r) for i in range(2) for r in (0, rows - 1)]
    sent = cut(place, [upstream, image], bias[None], parts, 6)
    pieces = exchange(*sent)
    inner = [[(i, r) for r in range(1, rows - 1)] for i in range(2)]
    sent = cut(place, after([upstream, image], pieces[3]), bias[None], inner[0], 25)
    pieces = after(pieces, sent)
    first = exchange(*sent)
    sent = cut(place, after([upstream, image], first[1:]), bias[None], inner[1], 18)
    first = after(first, sent)
    second = exchange(*sent)

    steps = halving(bands)[:-1]
    near, near_order = gather(near, steps)
    across, across_order = gather(across, steps[::-1])
    near, across = after((near, across), pieces[1])
    there = swap(jnp.concatenate([near, across], axis=1), "band", 1)
    held = [near, there[:, : near.shape[1]], across, there[:, near.shape[1] :]]
    filters = kernel(
        lambda *refs: assemble_kernel((near_order, across_order), *refs),
        [(taps * outs, 2 * local), (taps * 2 * local, 2 * local)],
        [place, filters, *held],
        [],
        "assemble",
        True,
        2,
    )
    pitch = width + 8
    body = lambda *refs: rim_kernel(pitch, *refs)
    packed = kernel(body, [(8 * pitch, local)] * 2, pieces, [], "rim", False, 0)
    rims = neighbours(*packed)

    size = rows * width
    totals = kernel(
        outer_kernel,
        [(size, 2 * local)] * 2,
        [*pieces, *rims, *filters],
        [(3, size, 4 * local)] * 2,
        "outer",
        False,
        2,
        jnp.float32,
    )
    lines = jnp.concatenate([p[width + 2 : width + 3] for p in pieces[:2]]).astype(jnp.float32)
    marks = [[], []]
    marks[0].append(token(first, 2))
    kept, came = [], []
    for which in range(2):
        mine, other = kernel(
            lambda *refs: inner_kernel(which, *refs),
            [(size, local)] * 2,
            [*(first, second)[which], totals[which], *filters, lines, *marks[which]],
            [(3, size // 2, 4 * local)],
            "inner",
            False,
            9,
        )
        kept.append(mine)
        if not which:
            second = after(second, mine)
        came.append(swap(other, "chan", 1))
    image_grad = home(place, kept[0], came[0], rows)
    kept[1] = after(kept[1], image_grad)
    return home(place, kept[1], came[1], rows), image_grad


def solution(mesh):
    return jax.shard_map(
        per_device,
        mesh=mesh,
        in_specs=(
            P("chan", "band", None),
            P(None, None, "chan"),
            P("chan"),
            P("chan", "band", None),
        ),
        out_specs=(P("chan", "band", None), P("chan", "band", None)),
        check_vma=False,
    )
```

```python
import jax
import jax.numpy as jnp
from jax import lax
from jax.experimental import pallas as pl
from jax.experimental.pallas import tpu as pltpu
from jax.sharding import PartitionSpec as P


def swap(value, axis, step):
    size = lax.axis_size(axis)
    return lax.ppermute(value, axis, [(j, j ^ step) for j in range(size)])


def neighbours(first, last):
    size = lax.axis_size("band")
    up = [(j, j + 1) for j in range(size - 1)]
    down = [(j + 1, j) for j in range(size - 1)]
    return lax.ppermute(last, "band", up), lax.ppermute(first, "band", down)


def pick(pieces, index, axis):
    stacked = jnp.stack(pieces)
    return jnp.concatenate(
        [lax.dynamic_index_in_dim(stacked, i, 0, keepdims=False) for i in index], axis=axis
    )


def spread(value, me, width):
    n = lax.axis_size("chan")
    padded = jnp.pad(value, ((0, 0), (1, 1), (0, 0)))
    pieces = []
    for k in range(n):
        piece = lax.dynamic_slice_in_dim(padded, (me ^ k) * width, width + 2, axis=1)
        pieces.append(swap(piece, "chan", k) if k else piece)
    return pieces


def add_rows(value):
    before, after = neighbours(value[:1], value[-1:])
    return jnp.concatenate([before, value, after], axis=0)


def conv(source, taps):
    return lax.conv_general_dilated(
        source[None],
        taps,
        (1, 1),
        "VALID",
        dimension_numbers=("NHWC", "HWIO", "NHWC"),
        preferred_element_type=jnp.float32,
    )[0]


def plain(image, filters, bias, upstream):
    n = lax.axis_size("chan")
    bands = lax.axis_size("band")
    me = lax.axis_index("chan")
    row = lax.axis_index("band")
    local = filters.shape[2]
    outs = filters.shape[1]
    width = image.shape[2] // n

    flat = filters.reshape(-1, local)
    share = flat.shape[0] // bands
    part = lax.dynamic_slice_in_dim(flat, row * share, share, axis=0)
    held = [jnp.concatenate([part, jnp.tile(bias[None], (16, 1))], axis=0)]
    step = n // 2
    while step:
        stacked = jnp.stack(held)
        there = swap(stacked, "chan", step)
        held = held + [there[j] for j in range(len(held))]
        step //= 2
    order = [0]
    step = n // 2
    while step:
        order = order + [o ^ step for o in order]
        step //= 2
    held = [held[order.index(k)] for k in range(n)]
    biases = [h[share] for h in held]
    whole = lax.all_gather(
        jnp.stack([h[:share] for h in held]), "band", axis=1, tiled=True
    ).reshape(n, 3, 3, outs, local)

    x_pieces = spread(jnp.transpose(image, (1, 2, 0)), me, width)
    u_pieces = spread(jnp.transpose(upstream, (1, 2, 0)), me, width)

    natural = [me ^ k for k in range(n)]
    x = add_rows(jnp.concatenate(x_pieces, axis=2))
    forward_taps = jnp.transpose(whole, (1, 2, 0, 4, 3)).reshape(3, 3, n * local, outs)
    total = conv(x, forward_taps) + pick(biases, natural, 0).astype(jnp.float32)
    features = back(total.astype(jnp.bfloat16), me, local, True)

    u = add_rows(pick(u_pieces, natural, 2))
    backward_taps = jnp.transpose(whole[:, ::-1, ::-1], (1, 2, 3, 0, 4)).reshape(
        3, 3, outs, n * local
    )
    image_grad = back(conv(u, backward_taps).astype(jnp.bfloat16), me, local, False)
    return features, image_grad


def back(value, me, local, is_natural):
    n = lax.axis_size("chan")
    pieces = []
    for k in range(n):
        start = (me ^ k) * local if is_natural else k * local
        piece = lax.dynamic_slice_in_dim(value, start, local, axis=2)
        pieces.append(swap(piece, "chan", k) if k else piece)
    whole = pick(pieces, [me ^ k for k in range(n)], 1)
    return jnp.transpose(whole, (2, 0, 1))


def assemble_kernel(orders, place, filters, near, near_far, across, across_far, weights, extra):
    me, band = place[0], place[1]
    taps, channels, local = filters.shape
    share = near.shape[1] // taps
    half = share // 2
    for tap in range(taps):
        for j in range(4):
            start = pl.multiple_of((me ^ j) * local, local)
            weights[pl.ds(tap * channels + j * local, local), :local] = filters[
                tap, pl.ds(start, local), :
            ]
    for bit, held in enumerate((near, near_far)):
        for j, d in enumerate(orders[0]):
            first = (band ^ (d | bit)) * share
            block = lax.div(first, local)
            start = (block ^ me) * local + first - block * local
            for tap in range(taps):
                row = pl.multiple_of(tap * channels + start, 16)
                weights[pl.ds(row, share), local:] = held[j, tap * share : (tap + 1) * share]
    for bit, held in enumerate((across, across_far)):
        for j, d in enumerate(orders[1]):
            first = (band ^ (d | bit)) * half
            block = lax.div(first, local)
            start = (block ^ (me & 1)) * local + first - block * local
            for tap in range(taps):
                row = pl.multiple_of(tap * 2 * local + start, 16)
                for k in range(2):
                    at = (k * taps + tap) * half
                    extra[pl.ds(row, half), k * local : (k + 1) * local] = held[j, at : at + half]


def cut_kernel(parts, place, *refs):
    sources, (bias, mine, other) = refs[:-3], refs[-3:]
    side = place[0] & 1
    local = bias.shape[1]
    width = sources[0].shape[1] // 2
    pitch = width + 8
    line = bias[...].astype(jnp.float32)
    zero = jnp.zeros((1, local), jnp.float32)
    rest = jnp.concatenate([line, zero, zero, zero, zero, zero])
    for n, (i, r) in enumerate(parts):
        source = sources[i]
        left = source[r, width - 16 : width].astype(jnp.float32)[15:]
        right = source[r, width : width + 16].astype(jnp.float32)[:1]
        pieces = []
        for t, (before, behind) in enumerate(((zero, right), (left, zero))):
            tail = jnp.concatenate([behind, line, rest]).astype(jnp.bfloat16)
            middle = source[r, t * width : (t + 1) * width]
            pieces.append(jnp.concatenate([before.astype(jnp.bfloat16), middle, tail[:7]]))
        at = n * pitch
        mine[at : at + pitch] = jnp.where(side == 0, pieces[0], pieces[1])
        other[at : at + pitch] = jnp.where(side == 0, pieces[1], pieces[0])


def rim_kernel(pitch, *refs):
    pieces, (first, last) = refs[:4], refs[4:]
    for k, piece in enumerate(pieces):
        for i in range(2):
            for out, end in ((first, 0), (last, 1)):
                at = (2 * i + end) * pitch
                out[(2 * k + i) * pitch : (2 * k + i + 1) * pitch] = piece[at : at + pitch]


def fill(target, rows):
    width = target.shape[1] // len(rows)
    for r, row in enumerate(rows):
        for k, (ref, start) in enumerate(row):
            local = ref.shape[1]
            for shift in range(3):
                target[
                    shift, r * width : (r + 1) * width, k * local : (k + 1) * local
                ] = ref[start + shift : start + shift + width]


def product(which, source, at, size, weights, extra, down, across):
    half = weights.shape[1]
    if which == 0:
        tap = 3 * (2 - down) + across
        filters = weights[pl.ds(tap * 2 * half, 2 * half), :]
        return jnp.dot(
            source[2 - across, at : at + size], filters, preferred_element_type=jnp.float32
        )
    tap = 3 * down + across
    total = None
    for block in range(2):
        if block:
            filters = extra[pl.ds(tap * half, half), :]
        else:
            filters = weights[pl.ds(tap * 2 * half, half), :]
        term = lax.dot_general(
            source[across, at : at + size, block * half : (block + 1) * half],
            filters,
            (((1,), (1,)), ((), ())),
            preferred_element_type=jnp.float32,
        )
        total = term if total is None else total + term
    return total


def outer_kernel(*refs):
    pieces, (before, after, weights, extra), (*totals, upstream, image) = (
        refs[:4],
        refs[4:8],
        refs[8:],
    )
    pitch = before.shape[0] // 8
    for which, (total, source) in enumerate(zip(totals, (upstream, image))):
        rims = [[(rim, (2 * k + which) * pitch) for k in range(4)] for rim in (before, after)]
        edges = [[(p, (2 * which + end) * pitch) for p in pieces] for end in range(2)]
        fill(source, [rims[0], *edges, rims[1]])
        size = total.shape[0] // 2
        row = size // 2
        top = middle = bottom = None
        for across in range(3):
            terms = [
                product(which, source, at, size, weights, extra, down, across)
                for down, at in ((0, 0), (1, row), (2, size))
            ]
            if across:
                terms = [old + term for old, term in zip((top, middle, bottom), terms)]
            top, middle, bottom = terms
        total[:row] = top[:row] + middle[:row]
        total[row:size] = top[row:]
        total[size : size + row] = bottom[:row]
        total[size + row :] = bottom[row:] + middle[row:]


def inner_kernel(which, *refs):
    inners, (total, weights, extra, lines) = refs[:4], refs[4:8]
    mine, other, source = refs[-3:]
    size = total.shape[0] // 2
    row = size // 2
    local = mine.shape[1]
    pitch = row + 8
    fill(source, [[(p, r * pitch) for p in inners] for r in range(2)])
    top = middle = bottom = None
    for across in range(3):
        terms = [
            product(which, source, 0, size, weights, extra, down, across) for down in (2, 1, 0)
        ]
        if across:
            terms = [old + term for old, term in zip((top, middle, bottom), terms)]
        top, middle, bottom = terms
    parts = [top[:row], top[row:] + middle[:row], middle[row:] + bottom[:row], bottom[row:]]
    for r, part in enumerate(parts):
        value = total[r * row : (r + 1) * row] + part
        for k, out in enumerate((mine, other)):
            block = value[:, k * local : (k + 1) * local]
            if which:
                block = block + lines[k : k + 1, :]
            out[r * row : (r + 1) * row] = block.astype(jnp.bfloat16)


SMEM = pl.BlockSpec(memory_space=pltpu.SMEM)
VMEM = pl.BlockSpec(memory_space=pltpu.VMEM)
ANY = pl.BlockSpec(memory_space=pl.ANY)


def cost(microseconds):
    work = 2**20 + 10**9 * microseconds
    return pl.CostEstimate(flops=work, bytes_accessed=2**20, transcendentals=0)


def kernel(body, shapes, args, scratch, name, placed=False, micros=0, kind=jnp.bfloat16):
    return pl.pallas_call(
        body,
        out_shape=[jax.ShapeDtypeStruct(s, kind) for s in shapes],
        in_specs=[SMEM] * placed + [VMEM] * (len(args) - placed),
        out_specs=[VMEM] * len(shapes),
        scratch_shapes=[pltpu.VMEM(s, jnp.bfloat16) for s in scratch],
        compiler_params=pltpu.CompilerParams(vmem_limit_bytes=20 * 2**20),
        cost_estimate=cost(micros),
        name=name,
    )(*args)


def cut(place, sources, bias, parts, micros):
    local = bias.shape[1]
    shape = (len(parts) * (sources[0].shape[1] // 2 + 8), local)
    body = lambda *refs: cut_kernel(parts, *refs)
    return kernel(body, [shape] * 2, [place, *sources, bias], [], "cut", True, micros)


def exchange(mine, other, near=None):
    sent = {1: other if near is None else near, 2: mine, 3: other}
    held = {k: swap(sent[k], "chan", k) for k in (2, 3, 1)}
    return [mine, held[1], held[2], held[3]]


def after(value, *others):
    return lax.optimization_barrier((value, others))[0]


def gather(value, steps):
    held, order = value[None], [0]
    for step in steps:
        held = jnp.concatenate([held, swap(held, "band", step)])
        order = order + [o ^ step for o in order]
    return held, order


def halving(size):
    steps = []
    while size > 1:
        size //= 2
        steps.append(size)
    return steps


def place_kernel(slot, piece, *refs):
    refs[-1][...] = piece[...]


def put(slot, piece, whole, cols):
    channels, rows, width = piece.shape
    spot = pl.BlockSpec((channels, rows, width), lambda i, slot: (0, 0, slot[0]))
    return pl.pallas_call(
        place_kernel,
        out_shape=jax.ShapeDtypeStruct((channels, rows, cols), jnp.bfloat16),
        grid_spec=pltpu.PrefetchScalarGridSpec(
            num_scalar_prefetch=1,
            grid=(1,),
            in_specs=[VMEM] + [ANY] * len(whole),
            out_specs=spot,
        ),
        input_output_aliases={2: 0} if whole else {},
        cost_estimate=cost(0),
        name="put",
    )(slot, piece, *whole)


def home(place, mine, other, rows):
    side = place[:1] & 1
    mine, other = [
        jnp.transpose(p.reshape(rows, -1, p.shape[1]), (2, 0, 1)) for p in (mine, other)
    ]
    cols = 2 * mine.shape[2]
    return put(1 - side, other, [put(side, mine, [], cols)], cols)


def token_kernel(*refs):
    refs[-1][...] = jnp.zeros_like(refs[-1])


def token(pieces, micros):
    return kernel(token_kernel, [(16, 128)], pieces, [], "token", False, micros)[0]


def per_device(image, filters, bias, upstream):
    n = lax.axis_size("chan")
    bands = lax.axis_size("band")
    taps, outs, local = filters.shape
    rows, cols = image.shape[1:]
    if n != 4 or local % 128 or cols % 256 or rows != 4 or outs % (32 * bands) or bands < 4:
        return plain(image, filters, bias, upstream)
    me = lax.axis_index("chan")
    band = lax.axis_index("band")
    half = me >> 1
    place = jnp.stack([me, band]).astype(jnp.int32)
    width = cols // 2

    share = outs // bands
    near = lax.dynamic_slice_in_dim(filters, band * share, share, axis=1).reshape(-1, local)
    start = (1 - half) * (outs // 2) + band * (share // 2)
    across = lax.dynamic_slice_in_dim(filters, start, share // 2, axis=1).reshape(-1, local)
    near = swap(near, "chan", 1)
    across = jnp.concatenate([swap(across, "chan", k) for k in (2, 3)])

    upstream, image = [jnp.transpose(v, (1, 2, 0)) for v in (upstream, image)]
    parts = [(i, r) for i in range(2) for r in (0, rows - 1)]
    sent = cut(place, [upstream, image], bias[None], parts, 6)
    pieces = exchange(*sent)
    inner = [[(i, r) for r in range(1, rows - 1)] for i in range(2)]
    sent = cut(place, after([upstream, image], pieces[3]), bias[None], inner[0], 25)
    pieces = after(pieces, sent)
    first = exchange(*sent)
    sent = cut(place, after([upstream, image], first[1:]), bias[None], inner[1], 13)
    first = after(first, sent)
    second = exchange(*sent)

    steps = halving(bands)[:-1]
    near, near_order = gather(near, steps)
    across, across_order = gather(across, steps[::-1])
    near, across = after((near, across), pieces[1])
    held = [near, swap(near, "band", 1), across, swap(across, "band", 1)]
    filters = kernel(
        lambda *refs: assemble_kernel((near_order, across_order), *refs),
        [(taps * outs, 2 * local), (taps * 2 * local, 2 * local)],
        [place, filters, *held],
        [],
        "assemble",
        True,
        0,
    )
    pitch = width + 8
    body = lambda *refs: rim_kernel(pitch, *refs)
    packed = kernel(body, [(8 * pitch, local)] * 2, pieces, [], "rim", False, 0)
    rims = neighbours(*packed)

    size = rows * width
    totals = kernel(
        outer_kernel,
        [(size, 2 * local)] * 2,
        [*pieces, *rims, *filters],
        [(3, size, 4 * local)] * 2,
        "outer",
        False,
        40,
        jnp.float32,
    )
    lines = jnp.concatenate([p[width + 2 : width + 3] for p in pieces[:2]]).astype(jnp.float32)
    marks = [[], []]
    first = after(first, totals)
    kept, came = [], []
    for which in range(2):
        mine, other = kernel(
            lambda *refs: inner_kernel(which, *refs),
            [(size, local)] * 2,
            [*(first, second)[which], totals[which], *filters, lines, *marks[which]],
            [(3, size // 2, 4 * local)],
            "inner",
            False,
            40,
        )
        kept.append(mine)
        if not which:
            second = after(second, mine)
        came.append(swap(other, "chan", 1))
    image_grad = home(place, kept[0], came[0], rows)
    came[1] = after(came[1], image_grad)
    return home(place, kept[1], came[1], rows), image_grad


def solution(mesh):
    return jax.shard_map(
        per_device,
        mesh=mesh,
        in_specs=(
            P("chan", "band", None),
            P(None, None, "chan"),
            P("chan"),
            P("chan", "band", None),
        ),
        out_specs=(P("chan", "band", None), P("chan", "band", None)),
        check_vma=False,
    )
```

```python
import jax
import jax.numpy as jnp
from jax import lax
from jax.experimental import pallas as pl
from jax.experimental.pallas import tpu as pltpu
from jax.sharding import PartitionSpec as P


def swap(value, axis, step):
    size = lax.axis_size(axis)
    return lax.ppermute(value, axis, [(j, j ^ step) for j in range(size)])


def neighbours(first, last):
    size = lax.axis_size("band")
    up = [(j, j + 1) for j in range(size - 1)]
    down = [(j + 1, j) for j in range(size - 1)]
    return lax.ppermute(last, "band", up), lax.ppermute(first, "band", down)


def pick(pieces, index, axis):
    stacked = jnp.stack(pieces)
    return jnp.concatenate(
        [lax.dynamic_index_in_dim(stacked, i, 0, keepdims=False) for i in index], axis=axis
    )


def spread(value, me, width):
    n = lax.axis_size("chan")
    padded = jnp.pad(value, ((0, 0), (1, 1), (0, 0)))
    pieces = []
    for k in range(n):
        piece = lax.dynamic_slice_in_dim(padded, (me ^ k) * width, width + 2, axis=1)
        pieces.append(swap(piece, "chan", k) if k else piece)
    return pieces


def add_rows(value):
    before, after = neighbours(value[:1], value[-1:])
    return jnp.concatenate([before, value, after], axis=0)


def conv(source, taps):
    return lax.conv_general_dilated(
        source[None],
        taps,
        (1, 1),
        "VALID",
        dimension_numbers=("NHWC", "HWIO", "NHWC"),
        preferred_element_type=jnp.float32,
    )[0]


def plain(image, filters, bias, upstream):
    n = lax.axis_size("chan")
    bands = lax.axis_size("band")
    me = lax.axis_index("chan")
    row = lax.axis_index("band")
    local = filters.shape[2]
    outs = filters.shape[1]
    width = image.shape[2] // n

    flat = filters.reshape(-1, local)
    share = flat.shape[0] // bands
    part = lax.dynamic_slice_in_dim(flat, row * share, share, axis=0)
    held = [jnp.concatenate([part, jnp.tile(bias[None], (16, 1))], axis=0)]
    step = n // 2
    while step:
        stacked = jnp.stack(held)
        there = swap(stacked, "chan", step)
        held = held + [there[j] for j in range(len(held))]
        step //= 2
    order = [0]
    step = n // 2
    while step:
        order = order + [o ^ step for o in order]
        step //= 2
    held = [held[order.index(k)] for k in range(n)]
    biases = [h[share] for h in held]
    whole = lax.all_gather(
        jnp.stack([h[:share] for h in held]), "band", axis=1, tiled=True
    ).reshape(n, 3, 3, outs, local)

    x_pieces = spread(jnp.transpose(image, (1, 2, 0)), me, width)
    u_pieces = spread(jnp.transpose(upstream, (1, 2, 0)), me, width)

    natural = [me ^ k for k in range(n)]
    x = add_rows(jnp.concatenate(x_pieces, axis=2))
    forward_taps = jnp.transpose(whole, (1, 2, 0, 4, 3)).reshape(3, 3, n * local, outs)
    total = conv(x, forward_taps) + pick(biases, natural, 0).astype(jnp.float32)
    features = back(total.astype(jnp.bfloat16), me, local, True)

    u = add_rows(pick(u_pieces, natural, 2))
    backward_taps = jnp.transpose(whole[:, ::-1, ::-1], (1, 2, 3, 0, 4)).reshape(
        3, 3, outs, n * local
    )
    image_grad = back(conv(u, backward_taps).astype(jnp.bfloat16), me, local, False)
    return features, image_grad


def back(value, me, local, is_natural):
    n = lax.axis_size("chan")
    pieces = []
    for k in range(n):
        start = (me ^ k) * local if is_natural else k * local
        piece = lax.dynamic_slice_in_dim(value, start, local, axis=2)
        pieces.append(swap(piece, "chan", k) if k else piece)
    whole = pick(pieces, [me ^ k for k in range(n)], 1)
    return jnp.transpose(whole, (2, 0, 1))


def assemble_kernel(orders, place, filters, near, near_far, across, across_far, weights, extra):
    me, band = place[0], place[1]
    taps, channels, local = filters.shape
    share = near.shape[1] // taps
    half = share // 2
    for tap in range(taps):
        for j in range(4):
            start = pl.multiple_of((me ^ j) * local, local)
            weights[pl.ds(tap * channels + j * local, local), :local] = filters[
                tap, pl.ds(start, local), :
            ]
    for bit, held in enumerate((near, near_far)):
        for j, d in enumerate(orders[0]):
            first = (band ^ (d | bit)) * share
            block = lax.div(first, local)
            start = (block ^ me) * local + first - block * local
            for tap in range(taps):
                row = pl.multiple_of(tap * channels + start, 16)
                weights[pl.ds(row, share), local:] = held[j, tap * share : (tap + 1) * share]
    for bit, held in enumerate((across, across_far)):
        for j, d in enumerate(orders[1]):
            first = (band ^ (d | bit)) * half
            block = lax.div(first, local)
            start = (block ^ (me & 1)) * local + first - block * local
            for tap in range(taps):
                row = pl.multiple_of(tap * 2 * local + start, 16)
                for k in range(2):
                    at = (k * taps + tap) * half
                    extra[pl.ds(row, half), k * local : (k + 1) * local] = held[j, at : at + half]


def cut_kernel(parts, place, *refs):
    sources, (bias, mine, other) = refs[:-3], refs[-3:]
    side = place[0] & 1
    local = bias.shape[1]
    width = sources[0].shape[1] // 2
    pitch = width + 8
    line = bias[...].astype(jnp.float32)
    zero = jnp.zeros((1, local), jnp.float32)
    rest = jnp.concatenate([line, zero, zero, zero, zero, zero])
    for n, (i, r) in enumerate(parts):
        source = sources[i]
        left = source[r, width - 16 : width].astype(jnp.float32)[15:]
        right = source[r, width : width + 16].astype(jnp.float32)[:1]
        pieces = []
        for t, (before, behind) in enumerate(((zero, right), (left, zero))):
            tail = jnp.concatenate([behind, line, rest]).astype(jnp.bfloat16)
            middle = source[r, t * width : (t + 1) * width]
            pieces.append(jnp.concatenate([before.astype(jnp.bfloat16), middle, tail[:7]]))
        at = n * pitch
        mine[at : at + pitch] = jnp.where(side == 0, pieces[0], pieces[1])
        other[at : at + pitch] = jnp.where(side == 0, pieces[1], pieces[0])


def rim_kernel(pitch, *refs):
    pieces, (first, last) = refs[:4], refs[4:]
    for k, piece in enumerate(pieces):
        for i in range(2):
            for out, end in ((first, 0), (last, 1)):
                at = (2 * i + end) * pitch
                out[(2 * k + i) * pitch : (2 * k + i + 1) * pitch] = piece[at : at + pitch]


def fill(target, rows):
    width = target.shape[1] // len(rows)
    for r, row in enumerate(rows):
        for k, (ref, start) in enumerate(row):
            local = ref.shape[1]
            for shift in range(3):
                target[
                    shift, r * width : (r + 1) * width, k * local : (k + 1) * local
                ] = ref[start + shift : start + shift + width]


def product(which, source, at, size, weights, extra, down, across):
    half = weights.shape[1]
    if which == 0:
        tap = 3 * (2 - down) + across
        filters = weights[pl.ds(tap * 2 * half, 2 * half), :]
        return jnp.dot(
            source[2 - across, at : at + size], filters, preferred_element_type=jnp.float32
        )
    tap = 3 * down + across
    total = None
    for block in range(2):
        if block:
            filters = extra[pl.ds(tap * half, half), :]
        else:
            filters = weights[pl.ds(tap * 2 * half, half), :]
        term = lax.dot_general(
            source[across, at : at + size, block * half : (block + 1) * half],
            filters,
            (((1,), (1,)), ((), ())),
            preferred_element_type=jnp.float32,
        )
        total = term if total is None else total + term
    return total


def outer_kernel(*refs):
    pieces, (before, after, weights, extra), (*totals, upstream, image) = (
        refs[:4],
        refs[4:8],
        refs[8:],
    )
    pitch = before.shape[0] // 8
    for which, (total, source) in enumerate(zip(totals, (upstream, image))):
        rims = [[(rim, (2 * k + which) * pitch) for k in range(4)] for rim in (before, after)]
        edges = [[(p, (2 * which + end) * pitch) for p in pieces] for end in range(2)]
        fill(source, [rims[0], *edges, rims[1]])
        size = total.shape[0] // 2
        row = size // 2
        top = middle = bottom = None
        for across in range(3):
            terms = [
                product(which, source, at, size, weights, extra, down, across)
                for down, at in ((0, 0), (1, row), (2, size))
            ]
            if across:
                terms = [old + term for old, term in zip((top, middle, bottom), terms)]
            top, middle, bottom = terms
        total[:row] = top[:row] + middle[:row]
        total[row:size] = top[row:]
        total[size : size + row] = bottom[:row]
        total[size + row :] = bottom[row:] + middle[row:]


def inner_kernel(which, *refs):
    inners, (total, weights, extra, lines) = refs[:4], refs[4:8]
    mine, other, source = refs[-3:]
    size = total.shape[0] // 2
    row = size // 2
    local = mine.shape[1]
    pitch = row + 8
    fill(source, [[(p, r * pitch) for p in inners] for r in range(2)])
    top = middle = bottom = None
    for across in range(3):
        terms = [
            product(which, source, 0, size, weights, extra, down, across) for down in (2, 1, 0)
        ]
        if across:
            terms = [old + term for old, term in zip((top, middle, bottom), terms)]
        top, middle, bottom = terms
    parts = [top[:row], top[row:] + middle[:row], middle[row:] + bottom[:row], bottom[row:]]
    for r, part in enumerate(parts):
        value = total[r * row : (r + 1) * row] + part
        for k, out in enumerate((mine, other)):
            block = value[:, k * local : (k + 1) * local]
            if which:
                block = block + lines[k : k + 1, :]
            out[r * row : (r + 1) * row] = block.astype(jnp.bfloat16)


SMEM = pl.BlockSpec(memory_space=pltpu.SMEM)
VMEM = pl.BlockSpec(memory_space=pltpu.VMEM)
ANY = pl.BlockSpec(memory_space=pl.ANY)


def cost(microseconds):
    work = 2**20 + 10**9 * microseconds
    return pl.CostEstimate(flops=work, bytes_accessed=2**20, transcendentals=0)


def kernel(body, shapes, args, scratch, name, placed=False, micros=0, kind=jnp.bfloat16):
    return pl.pallas_call(
        body,
        out_shape=[jax.ShapeDtypeStruct(s, kind) for s in shapes],
        in_specs=[SMEM] * placed + [VMEM] * (len(args) - placed),
        out_specs=[VMEM] * len(shapes),
        scratch_shapes=[pltpu.VMEM(s, jnp.bfloat16) for s in scratch],
        compiler_params=pltpu.CompilerParams(vmem_limit_bytes=20 * 2**20),
        cost_estimate=cost(micros),
        name=name,
    )(*args)


def cut(place, sources, bias, parts, micros):
    local = bias.shape[1]
    shape = (len(parts) * (sources[0].shape[1] // 2 + 8), local)
    body = lambda *refs: cut_kernel(parts, *refs)
    return kernel(body, [shape] * 2, [place, *sources, bias], [], "cut", True, micros)


def exchange(mine, other, near=None):
    sent = {1: other if near is None else near, 2: mine, 3: other}
    held = {k: swap(sent[k], "chan", k) for k in (1, 2, 3)}
    return [mine, held[1], held[2], held[3]]


def after(value, *others):
    return lax.optimization_barrier((value, others))[0]


def gather(value, steps):
    held, order = value[None], [0]
    for step in steps:
        held = jnp.concatenate([held, swap(held, "band", step)])
        order = order + [o ^ step for o in order]
    return held, order


def halving(size):
    steps = []
    while size > 1:
        size //= 2
        steps.append(size)
    return steps


def home_kernel(place, mine, other, out):
    width = mine.shape[2]
    side = place[0] & 1
    for t in range(2):

        @pl.when(side == t)
        def _():
            out[:, :, t * width : (t + 1) * width] = mine[...]
            out[:, :, (1 - t) * width : (2 - t) * width] = other[...]


def home(place, mine, other, rows):
    turn = lambda p: jnp.transpose(p.reshape(rows, -1, p.shape[1]), (2, 0, 1))
    mine, other = turn(mine), turn(other)
    channels, rows, width = mine.shape
    shape = (channels, rows, 2 * width)
    return kernel(home_kernel, [shape], [place, mine, other], [], "home", True)[0]


def token_kernel(*refs):
    refs[-1][...] = jnp.zeros_like(refs[-1])


def token(pieces, micros):
    return kernel(token_kernel, [(16, 128)], pieces, [], "token", False, micros)[0]


def per_device(image, filters, bias, upstream):
    n = lax.axis_size("chan")
    bands = lax.axis_size("band")
    taps, outs, local = filters.shape
    rows, cols = image.shape[1:]
    if n != 4 or local % 128 or cols % 256 or rows != 4 or outs % (32 * bands) or bands < 4:
        return plain(image, filters, bias, upstream)
    me = lax.axis_index("chan")
    band = lax.axis_index("band")
    half = me >> 1
    place = jnp.stack([me, band]).astype(jnp.int32)
    width = cols // 2

    share = outs // bands
    near = lax.dynamic_slice_in_dim(filters, band * share, share, axis=1).reshape(-1, local)
    start = (1 - half) * (outs // 2) + band * (share // 2)
    across = lax.dynamic_slice_in_dim(filters, start, share // 2, axis=1).reshape(-1, local)
    near = swap(near, "chan", 1)
    across = jnp.concatenate([swap(across, "chan", k) for k in (2, 3)])

    upstream, image = [jnp.transpose(v, (1, 2, 0)) for v in (upstream, image)]
    parts = [(i, r) for i in range(2) for r in (0, rows - 1)]
    sent = cut(place, [upstream, image], bias[None], parts, 6)
    pieces = exchange(*sent)
    inner = [[(i, r) for r in range(1, rows - 1)] for i in range(2)]
    sent = cut(place, after([upstream, image], pieces[3]), bias[None], inner[0], 25)
    pieces = after(pieces, sent)
    first = exchange(*sent)
    sent = cut(place, after([upstream, image], first[1:]), bias[None], inner[1], 18)
    first = after(first, sent)
    second = exchange(*sent)

    steps = halving(bands)[:-1]
    near, near_order = gather(near, steps)
    across, across_order = gather(across, steps[::-1])
    near, across = after((near, across), pieces[1])
    there = swap(jnp.concatenate([near, across], axis=1), "band", 1)
    held = [near, there[:, : near.shape[1]], across, there[:, near.shape[1] :]]
    filters = kernel(
        lambda *refs: assemble_kernel((near_order, across_order), *refs),
        [(taps * outs, 2 * local), (taps * 2 * local, 2 * local)],
        [place, filters, *held],
        [],
        "assemble",
        True,
        2,
    )
    pitch = width + 8
    body = lambda *refs: rim_kernel(pitch, *refs)
    packed = kernel(body, [(8 * pitch, local)] * 2, pieces, [], "rim", False, 0)
    rims = neighbours(*packed)

    size = rows * width
    totals = kernel(
        outer_kernel,
        [(size, 2 * local)] * 2,
        [*pieces, *rims, *filters],
        [(3, size, 4 * local)] * 2,
        "outer",
        False,
        2,
        jnp.float32,
    )
    lines = jnp.concatenate([p[width + 2 : width + 3] for p in pieces[:2]]).astype(jnp.float32)
    marks = [[], []]
    marks[0].append(token(first, 2))
    kept, came = [], []
    for which in range(2):
        mine, other = kernel(
            lambda *refs: inner_kernel(which, *refs),
            [(size, local)] * 2,
            [*(first, second)[which], totals[which], *filters, lines, *marks[which]],
            [(3, size // 2, 4 * local)],
            "inner",
            False,
            9,
        )
        kept.append(mine)
        if not which:
            second = after(second, mine)
        came.append(swap(other, "chan", 1))
    image_grad = home(place, kept[0], came[0], rows)
    kept[1] = after(kept[1], image_grad)
    return home(place, kept[1], came[1], rows), image_grad


def solution(mesh):
    return jax.shard_map(
        per_device,
        mesh=mesh,
        in_specs=(
            P("chan", "band", None),
            P(None, None, "chan"),
            P("chan"),
            P("chan", "band", None),
        ),
        out_specs=(P("chan", "band", None), P("chan", "band", None)),
        check_vma=False,
    )
```

```python
import jax
import jax.numpy as jnp
from jax import lax
from jax.experimental import pallas as pl
from jax.experimental.pallas import tpu as pltpu
from jax.sharding import PartitionSpec as P


def swap(value, axis, step):
    size = lax.axis_size(axis)
    return lax.ppermute(value, axis, [(j, j ^ step) for j in range(size)])


def neighbours(first, last):
    size = lax.axis_size("band")
    up = [(j, j + 1) for j in range(size - 1)]
    down = [(j + 1, j) for j in range(size - 1)]
    return lax.ppermute(last, "band", up), lax.ppermute(first, "band", down)


def pick(pieces, index, axis):
    stacked = jnp.stack(pieces)
    return jnp.concatenate(
        [lax.dynamic_index_in_dim(stacked, i, 0, keepdims=False) for i in index], axis=axis
    )


def spread(value, me, width):
    n = lax.axis_size("chan")
    padded = jnp.pad(value, ((0, 0), (1, 1), (0, 0)))
    pieces = []
    for k in range(n):
        piece = lax.dynamic_slice_in_dim(padded, (me ^ k) * width, width + 2, axis=1)
        pieces.append(swap(piece, "chan", k) if k else piece)
    return pieces


def add_rows(value):
    before, after = neighbours(value[:1], value[-1:])
    return jnp.concatenate([before, value, after], axis=0)


def conv(source, taps):
    return lax.conv_general_dilated(
        source[None],
        taps,
        (1, 1),
        "VALID",
        dimension_numbers=("NHWC", "HWIO", "NHWC"),
        preferred_element_type=jnp.float32,
    )[0]


def plain(image, filters, bias, upstream):
    n = lax.axis_size("chan")
    bands = lax.axis_size("band")
    me = lax.axis_index("chan")
    row = lax.axis_index("band")
    local = filters.shape[2]
    outs = filters.shape[1]
    width = image.shape[2] // n

    flat = filters.reshape(-1, local)
    share = flat.shape[0] // bands
    part = lax.dynamic_slice_in_dim(flat, row * share, share, axis=0)
    held = [jnp.concatenate([part, jnp.tile(bias[None], (16, 1))], axis=0)]
    step = n // 2
    while step:
        stacked = jnp.stack(held)
        there = swap(stacked, "chan", step)
        held = held + [there[j] for j in range(len(held))]
        step //= 2
    order = [0]
    step = n // 2
    while step:
        order = order + [o ^ step for o in order]
        step //= 2
    held = [held[order.index(k)] for k in range(n)]
    biases = [h[share] for h in held]
    whole = lax.all_gather(
        jnp.stack([h[:share] for h in held]), "band", axis=1, tiled=True
    ).reshape(n, 3, 3, outs, local)

    x_pieces = spread(jnp.transpose(image, (1, 2, 0)), me, width)
    u_pieces = spread(jnp.transpose(upstream, (1, 2, 0)), me, width)

    natural = [me ^ k for k in range(n)]
    x = add_rows(jnp.concatenate(x_pieces, axis=2))
    forward_taps = jnp.transpose(whole, (1, 2, 0, 4, 3)).reshape(3, 3, n * local, outs)
    total = conv(x, forward_taps) + pick(biases, natural, 0).astype(jnp.float32)
    features = back(total.astype(jnp.bfloat16), me, local, True)

    u = add_rows(pick(u_pieces, natural, 2))
    backward_taps = jnp.transpose(whole[:, ::-1, ::-1], (1, 2, 3, 0, 4)).reshape(
        3, 3, outs, n * local
    )
    image_grad = back(conv(u, backward_taps).astype(jnp.bfloat16), me, local, False)
    return features, image_grad


def back(value, me, local, is_natural):
    n = lax.axis_size("chan")
    pieces = []
    for k in range(n):
        start = (me ^ k) * local if is_natural else k * local
        piece = lax.dynamic_slice_in_dim(value, start, local, axis=2)
        pieces.append(swap(piece, "chan", k) if k else piece)
    whole = pick(pieces, [me ^ k for k in range(n)], 1)
    return jnp.transpose(whole, (2, 0, 1))


def assemble_kernel(orders, place, filters, near, near_far, across, across_far, weights, extra):
    me, band = place[0], place[1]
    taps, channels, local = filters.shape
    share = near.shape[1] // taps
    half = share // 2
    for tap in range(taps):
        for j in range(4):
            start = pl.multiple_of((me ^ j) * local, local)
            weights[pl.ds(tap * channels + j * local, local), :local] = filters[
                tap, pl.ds(start, local), :
            ]
    for bit, held in enumerate((near, near_far)):
        for j, d in enumerate(orders[0]):
            first = (band ^ (d | bit)) * share
            block = lax.div(first, local)
            start = (block ^ me) * local + first - block * local
            for tap in range(taps):
                row = pl.multiple_of(tap * channels + start, 16)
                weights[pl.ds(row, share), local:] = held[j, tap * share : (tap + 1) * share]
    for bit, held in enumerate((across, across_far)):
        for j, d in enumerate(orders[1]):
            first = (band ^ (d | bit)) * half
            block = lax.div(first, local)
            start = (block ^ (me & 1)) * local + first - block * local
            for tap in range(taps):
                row = pl.multiple_of(tap * 2 * local + start, 16)
                for k in range(2):
                    at = (k * taps + tap) * half
                    extra[pl.ds(row, half), k * local : (k + 1) * local] = held[j, at : at + half]


def cut_kernel(parts, place, *refs):
    sources, (bias, mine, other) = refs[:-3], refs[-3:]
    side = place[0] & 1
    local = bias.shape[1]
    width = sources[0].shape[1] // 2
    pitch = width + 8
    line = bias[...].astype(jnp.float32)
    zero = jnp.zeros((1, local), jnp.float32)
    rest = jnp.concatenate([line, zero, zero, zero, zero, zero])
    for n, (i, r) in enumerate(parts):
        source = sources[i]
        left = source[r, width - 16 : width].astype(jnp.float32)[15:]
        right = source[r, width : width + 16].astype(jnp.float32)[:1]
        pieces = []
        for t, (before, behind) in enumerate(((zero, right), (left, zero))):
            tail = jnp.concatenate([behind, line, rest]).astype(jnp.bfloat16)
            middle = source[r, t * width : (t + 1) * width]
            pieces.append(jnp.concatenate([before.astype(jnp.bfloat16), middle, tail[:7]]))
        at = n * pitch
        mine[at : at + pitch] = jnp.where(side == 0, pieces[0], pieces[1])
        other[at : at + pitch] = jnp.where(side == 0, pieces[1], pieces[0])


def rim_kernel(pitch, *refs):
    pieces, (first, last) = refs[:4], refs[4:]
    for k, piece in enumerate(pieces):
        for i in range(2):
            for out, end in ((first, 0), (last, 1)):
                at = (2 * i + end) * pitch
                out[(2 * k + i) * pitch : (2 * k + i + 1) * pitch] = piece[at : at + pitch]


def fill(target, rows):
    width = target.shape[1] // len(rows)
    for r, row in enumerate(rows):
        for k, (ref, start) in enumerate(row):
            local = ref.shape[1]
            for shift in range(3):
                target[
                    shift, r * width : (r + 1) * width, k * local : (k + 1) * local
                ] = ref[start + shift : start + shift + width]


def product(which, source, at, size, weights, extra, down, across):
    half = weights.shape[1]
    if which == 0:
        tap = 3 * (2 - down) + across
        filters = weights[pl.ds(tap * 2 * half, 2 * half), :]
        return jnp.dot(
            source[2 - across, at : at + size], filters, preferred_element_type=jnp.float32
        )
    tap = 3 * down + across
    total = None
    for block in range(2):
        if block:
            filters = extra[pl.ds(tap * half, half), :]
        else:
            filters = weights[pl.ds(tap * 2 * half, half), :]
        term = lax.dot_general(
            source[across, at : at + size, block * half : (block + 1) * half],
            filters,
            (((1,), (1,)), ((), ())),
            preferred_element_type=jnp.float32,
        )
        total = term if total is None else total + term
    return total


def outer_kernel(*refs):
    pieces, (before, after, weights, extra), (*totals, upstream, image) = (
        refs[:4],
        refs[4:8],
        refs[8:],
    )
    pitch = before.shape[0] // 8
    for which, (total, source) in enumerate(zip(totals, (upstream, image))):
        rims = [[(rim, (2 * k + which) * pitch) for k in range(4)] for rim in (before, after)]
        edges = [[(p, (2 * which + end) * pitch) for p in pieces] for end in range(2)]
        fill(source, [rims[0], *edges, rims[1]])
        size = total.shape[0] // 2
        row = size // 2
        top = middle = bottom = None
        for across in range(3):
            terms = [
                product(which, source, at, size, weights, extra, down, across)
                for down, at in ((0, 0), (1, row), (2, size))
            ]
            if across:
                terms = [old + term for old, term in zip((top, middle, bottom), terms)]
            top, middle, bottom = terms
        total[:row] = top[:row] + middle[:row]
        total[row:size] = top[row:]
        total[size : size + row] = bottom[:row]
        total[size + row :] = bottom[row:] + middle[row:]


def inner_kernel(which, *refs):
    inners, (total, weights, extra, lines) = refs[:4], refs[4:8]
    mine, other, source = refs[-3:]
    size = total.shape[0] // 2
    row = size // 2
    local = mine.shape[1]
    pitch = row + 8
    fill(source, [[(p, r * pitch) for p in inners] for r in range(2)])
    top = middle = bottom = None
    for across in range(3):
        terms = [
            product(which, source, 0, size, weights, extra, down, across) for down in (2, 1, 0)
        ]
        if across:
            terms = [old + term for old, term in zip((top, middle, bottom), terms)]
        top, middle, bottom = terms
    parts = [top[:row], top[row:] + middle[:row], middle[row:] + bottom[:row], bottom[row:]]
    for r, part in enumerate(parts):
        value = total[r * row : (r + 1) * row] + part
        for k, out in enumerate((mine, other)):
            block = value[:, k * local : (k + 1) * local]
            if which:
                block = block + lines[k : k + 1, :]
            out[r * row : (r + 1) * row] = block.astype(jnp.bfloat16)


SMEM = pl.BlockSpec(memory_space=pltpu.SMEM)
VMEM = pl.BlockSpec(memory_space=pltpu.VMEM)
ANY = pl.BlockSpec(memory_space=pl.ANY)


def cost(microseconds):
    work = 2**20 + 10**9 * microseconds
    return pl.CostEstimate(flops=work, bytes_accessed=2**20, transcendentals=0)


def kernel(body, shapes, args, scratch, name, placed=False, micros=0, kind=jnp.bfloat16):
    return pl.pallas_call(
        body,
        out_shape=[jax.ShapeDtypeStruct(s, kind) for s in shapes],
        in_specs=[SMEM] * placed + [VMEM] * (len(args) - placed),
        out_specs=[VMEM] * len(shapes),
        scratch_shapes=[pltpu.VMEM(s, jnp.bfloat16) for s in scratch],
        compiler_params=pltpu.CompilerParams(vmem_limit_bytes=20 * 2**20),
        cost_estimate=cost(micros),
        name=name,
    )(*args)


def cut(place, sources, bias, parts, micros):
    local = bias.shape[1]
    shape = (len(parts) * (sources[0].shape[1] // 2 + 8), local)
    body = lambda *refs: cut_kernel(parts, *refs)
    return kernel(body, [shape] * 2, [place, *sources, bias], [], "cut", True, micros)


def exchange(mine, other, near=None):
    sent = {1: other if near is None else near, 2: mine, 3: other}
    held = {k: swap(sent[k], "chan", k) for k in (1, 2, 3)}
    return [mine, held[1], held[2], held[3]]


def after(value, *others):
    return lax.optimization_barrier((value, others))[0]


def gather(value, steps):
    held, order = value[None], [0]
    for step in steps:
        held = jnp.concatenate([held, swap(held, "band", step)])
        order = order + [o ^ step for o in order]
    return held, order


def halving(size):
    steps = []
    while size > 1:
        size //= 2
        steps.append(size)
    return steps


def home_kernel(place, mine, other, out):
    width = mine.shape[2]
    side = place[0] & 1
    for t in range(2):

        @pl.when(side == t)
        def _():
            out[:, :, t * width : (t + 1) * width] = mine[...]
            out[:, :, (1 - t) * width : (2 - t) * width] = other[...]


def home(place, mine, other, rows):
    turn = lambda p: jnp.transpose(p.reshape(rows, -1, p.shape[1]), (2, 0, 1))
    mine, other = turn(mine), turn(other)
    channels, rows, width = mine.shape
    shape = (channels, rows, 2 * width)
    return kernel(home_kernel, [shape], [place, mine, other], [], "home", True)[0]


def token_kernel(*refs):
    refs[-1][...] = jnp.zeros_like(refs[-1])


def token(pieces, micros):
    return kernel(token_kernel, [(16, 128)], pieces, [], "token", False, micros)[0]


def per_device(image, filters, bias, upstream):
    n = lax.axis_size("chan")
    bands = lax.axis_size("band")
    taps, outs, local = filters.shape
    rows, cols = image.shape[1:]
    if n != 4 or local % 128 or cols % 256 or rows != 4 or outs % (32 * bands) or bands < 4:
        return plain(image, filters, bias, upstream)
    me = lax.axis_index("chan")
    band = lax.axis_index("band")
    half = me >> 1
    place = jnp.stack([me, band]).astype(jnp.int32)
    width = cols // 2

    share = outs // bands
    near = lax.dynamic_slice_in_dim(filters, band * share, share, axis=1).reshape(-1, local)
    start = (1 - half) * (outs // 2) + band * (share // 2)
    across = lax.dynamic_slice_in_dim(filters, start, share // 2, axis=1).reshape(-1, local)
    near = swap(near, "chan", 1)
    across = jnp.concatenate([swap(across, "chan", k) for k in (2, 3)])

    upstream, image = [jnp.transpose(v, (1, 2, 0)) for v in (upstream, image)]
    parts = [(i, r) for i in range(2) for r in (0, rows - 1)]
    sent = cut(place, [upstream, image], bias[None], parts, 6)
    pieces = exchange(*sent)
    inner = [[(i, r) for r in range(1, rows - 1)] for i in range(2)]
    sent = cut(place, after([upstream, image], pieces[3]), bias[None], inner[0], 25)
    pieces = after(pieces, sent)
    first = exchange(*sent)
    sent = cut(place, after([upstream, image], first[1:]), bias[None], inner[1], 9)
    first = after(first, sent)
    late = sent

    steps = halving(bands)[:-1]
    near, near_order = gather(near, steps)
    across, across_order = gather(across, steps[::-1])
    near, across = after((near, across), pieces[1])
    there = swap(jnp.concatenate([near, across], axis=1), "band", 1)
    held = [near, there[:, : near.shape[1]], across, there[:, near.shape[1] :]]
    second = [late[0], None, swap(late[0], "chan", 2), swap(late[1], "chan", 3)]
    second[1] = swap(after(late[1], held), "chan", 1)
    filters = kernel(
        lambda *refs: assemble_kernel((near_order, across_order), *refs),
        [(taps * outs, 2 * local), (taps * 2 * local, 2 * local)],
        [place, filters, *held],
        [],
        "assemble",
        True,
        2,
    )
    pitch = width + 8
    body = lambda *refs: rim_kernel(pitch, *refs)
    packed = kernel(body, [(8 * pitch, local)] * 2, pieces, [], "rim", False, 0)
    rims = neighbours(*packed)

    size = rows * width
    totals = kernel(
        outer_kernel,
        [(size, 2 * local)] * 2,
        [*pieces, *rims, *filters],
        [(3, size, 4 * local)] * 2,
        "outer",
        False,
        2,
        jnp.float32,
    )
    lines = jnp.concatenate([p[width + 2 : width + 3] for p in pieces[:2]]).astype(jnp.float32)
    marks = [[], []]
    marks[0].append(token(first, 9))
    kept, came = [], []
    for which in range(2):
        mine, other = kernel(
            lambda *refs: inner_kernel(which, *refs),
            [(size, local)] * 2,
            [*(first, second)[which], totals[which], *filters, lines, *marks[which]],
            [(3, size // 2, 4 * local)],
            "inner",
            False,
            9,
        )
        kept.append(mine)
        if not which:
            second = after(second, mine)
        came.append(swap(other, "chan", 1))
    image_grad = home(place, kept[0], came[0], rows)
    kept[1] = after(kept[1], image_grad)
    return home(place, kept[1], came[1], rows), image_grad


def solution(mesh):
    return jax.shard_map(
        per_device,
        mesh=mesh,
        in_specs=(
            P("chan", "band", None),
            P(None, None, "chan"),
            P("chan"),
            P("chan", "band", None),
        ),
        out_specs=(P("chan", "band", None), P("chan", "band", None)),
        check_vma=False,
    )
```

```python
import jax
import jax.numpy as jnp
from jax import lax
from jax.experimental import pallas as pl
from jax.experimental.pallas import tpu as pltpu
from jax.sharding import PartitionSpec as P


def swap(value, axis, step):
    size = lax.axis_size(axis)
    return lax.ppermute(value, axis, [(j, j ^ step) for j in range(size)])


def neighbours(first, last):
    size = lax.axis_size("band")
    up = [(j, j + 1) for j in range(size - 1)]
    down = [(j + 1, j) for j in range(size - 1)]
    return lax.ppermute(last, "band", up), lax.ppermute(first, "band", down)


def pick(pieces, index, axis):
    stacked = jnp.stack(pieces)
    return jnp.concatenate(
        [lax.dynamic_index_in_dim(stacked, i, 0, keepdims=False) for i in index], axis=axis
    )


def spread(value, me, width):
    n = lax.axis_size("chan")
    padded = jnp.pad(value, ((0, 0), (1, 1), (0, 0)))
    pieces = []
    for k in range(n):
        piece = lax.dynamic_slice_in_dim(padded, (me ^ k) * width, width + 2, axis=1)
        pieces.append(swap(piece, "chan", k) if k else piece)
    return pieces


def add_rows(value):
    before, after = neighbours(value[:1], value[-1:])
    return jnp.concatenate([before, value, after], axis=0)


def conv(source, taps):
    return lax.conv_general_dilated(
        source[None],
        taps,
        (1, 1),
        "VALID",
        dimension_numbers=("NHWC", "HWIO", "NHWC"),
        preferred_element_type=jnp.float32,
    )[0]


def plain(image, filters, bias, upstream):
    n = lax.axis_size("chan")
    bands = lax.axis_size("band")
    me = lax.axis_index("chan")
    row = lax.axis_index("band")
    local = filters.shape[2]
    outs = filters.shape[1]
    width = image.shape[2] // n

    flat = filters.reshape(-1, local)
    share = flat.shape[0] // bands
    part = lax.dynamic_slice_in_dim(flat, row * share, share, axis=0)
    held = [jnp.concatenate([part, jnp.tile(bias[None], (16, 1))], axis=0)]
    step = n // 2
    while step:
        stacked = jnp.stack(held)
        there = swap(stacked, "chan", step)
        held = held + [there[j] for j in range(len(held))]
        step //= 2
    order = [0]
    step = n // 2
    while step:
        order = order + [o ^ step for o in order]
        step //= 2
    held = [held[order.index(k)] for k in range(n)]
    biases = [h[share] for h in held]
    whole = lax.all_gather(
        jnp.stack([h[:share] for h in held]), "band", axis=1, tiled=True
    ).reshape(n, 3, 3, outs, local)

    x_pieces = spread(jnp.transpose(image, (1, 2, 0)), me, width)
    u_pieces = spread(jnp.transpose(upstream, (1, 2, 0)), me, width)

    natural = [me ^ k for k in range(n)]
    x = add_rows(jnp.concatenate(x_pieces, axis=2))
    forward_taps = jnp.transpose(whole, (1, 2, 0, 4, 3)).reshape(3, 3, n * local, outs)
    total = conv(x, forward_taps) + pick(biases, natural, 0).astype(jnp.float32)
    features = back(total.astype(jnp.bfloat16), me, local, True)

    u = add_rows(pick(u_pieces, natural, 2))
    backward_taps = jnp.transpose(whole[:, ::-1, ::-1], (1, 2, 3, 0, 4)).reshape(
        3, 3, outs, n * local
    )
    image_grad = back(conv(u, backward_taps).astype(jnp.bfloat16), me, local, False)
    return features, image_grad


def back(value, me, local, is_natural):
    n = lax.axis_size("chan")
    pieces = []
    for k in range(n):
        start = (me ^ k) * local if is_natural else k * local
        piece = lax.dynamic_slice_in_dim(value, start, local, axis=2)
        pieces.append(swap(piece, "chan", k) if k else piece)
    whole = pick(pieces, [me ^ k for k in range(n)], 1)
    return jnp.transpose(whole, (2, 0, 1))


def assemble_kernel(orders, place, filters, near, near_far, across, across_far, weights, extra):
    me, band = place[0], place[1]
    taps, channels, local = filters.shape
    share = near.shape[1] // taps
    half = share // 2
    for tap in range(taps):
        for j in range(4):
            start = pl.multiple_of((me ^ j) * local, local)
            weights[pl.ds(tap * channels + j * local, local), :local] = filters[
                tap, pl.ds(start, local), :
            ]
    for bit, held in enumerate((near, near_far)):
        for j, d in enumerate(orders[0]):
            first = (band ^ (d | bit)) * share
            block = lax.div(first, local)
            start = (block ^ me) * local + first - block * local
            for tap in range(taps):
                row = pl.multiple_of(tap * channels + start, 16)
                weights[pl.ds(row, share), local:] = held[j, tap * share : (tap + 1) * share]
    for bit, held in enumerate((across, across_far)):
        for j, d in enumerate(orders[1]):
            first = (band ^ (d | bit)) * half
            block = lax.div(first, local)
            start = (block ^ (me & 1)) * local + first - block * local
            for tap in range(taps):
                row = pl.multiple_of(tap * 2 * local + start, 16)
                for k in range(2):
                    at = (k * taps + tap) * half
                    extra[pl.ds(row, half), k * local : (k + 1) * local] = held[j, at : at + half]


def cut_kernel(parts, place, *refs):
    sources, (bias, mine, other) = refs[:-3], refs[-3:]
    side = place[0] & 1
    local = bias.shape[1]
    width = sources[0].shape[1] // 2
    pitch = width + 8
    line = bias[...].astype(jnp.float32)
    zero = jnp.zeros((1, local), jnp.float32)
    rest = jnp.concatenate([line, zero, zero, zero, zero, zero])
    for n, (i, r) in enumerate(parts):
        source = sources[i]
        left = source[r, width - 16 : width].astype(jnp.float32)[15:]
        right = source[r, width : width + 16].astype(jnp.float32)[:1]
        pieces = []
        for t, (before, behind) in enumerate(((zero, right), (left, zero))):
            tail = jnp.concatenate([behind, line, rest]).astype(jnp.bfloat16)
            middle = source[r, t * width : (t + 1) * width]
            pieces.append(jnp.concatenate([before.astype(jnp.bfloat16), middle, tail[:7]]))
        at = n * pitch
        mine[at : at + pitch] = jnp.where(side == 0, pieces[0], pieces[1])
        other[at : at + pitch] = jnp.where(side == 0, pieces[1], pieces[0])


def rim_kernel(pitch, *refs):
    pieces, (first, last) = refs[:4], refs[4:]
    for k, piece in enumerate(pieces):
        for i in range(2):
            for out, end in ((first, 0), (last, 1)):
                at = (2 * i + end) * pitch
                out[(2 * k + i) * pitch : (2 * k + i + 1) * pitch] = piece[at : at + pitch]


def fill(target, rows):
    width = target.shape[1] // len(rows)
    for r, row in enumerate(rows):
        for k, (ref, start) in enumerate(row):
            local = ref.shape[1]
            for shift in range(3):
                target[
                    shift, r * width : (r + 1) * width, k * local : (k + 1) * local
                ] = ref[start + shift : start + shift + width]


def product(which, source, at, size, weights, extra, down, across):
    half = weights.shape[1]
    if which == 0:
        tap = 3 * (2 - down) + across
        filters = weights[pl.ds(tap * 2 * half, 2 * half), :]
        return jnp.dot(
            source[2 - across, at : at + size], filters, preferred_element_type=jnp.float32
        )
    tap = 3 * down + across
    total = None
    for block in range(2):
        if block:
            filters = extra[pl.ds(tap * half, half), :]
        else:
            filters = weights[pl.ds(tap * 2 * half, half), :]
        term = lax.dot_general(
            source[across, at : at + size, block * half : (block + 1) * half],
            filters,
            (((1,), (1,)), ((), ())),
            preferred_element_type=jnp.float32,
        )
        total = term if total is None else total + term
    return total


def outer_kernel(*refs):
    pieces, (before, after, weights, extra), (*totals, upstream, image) = (
        refs[:4],
        refs[4:8],
        refs[8:],
    )
    pitch = before.shape[0] // 8
    for which, (total, source) in enumerate(zip(totals, (upstream, image))):
        rims = [[(rim, (2 * k + which) * pitch) for k in range(4)] for rim in (before, after)]
        edges = [[(p, (2 * which + end) * pitch) for p in pieces] for end in range(2)]
        fill(source, [rims[0], *edges, rims[1]])
        size = total.shape[0] // 2
        row = size // 2
        top = middle = bottom = None
        for across in range(3):
            terms = [
                product(which, source, at, size, weights, extra, down, across)
                for down, at in ((0, 0), (1, row), (2, size))
            ]
            if across:
                terms = [old + term for old, term in zip((top, middle, bottom), terms)]
            top, middle, bottom = terms
        total[:row] = top[:row] + middle[:row]
        total[row:size] = top[row:]
        total[size : size + row] = bottom[:row]
        total[size + row :] = bottom[row:] + middle[row:]


def inner_kernel(which, *refs):
    inners, (total, weights, extra, lines) = refs[:4], refs[4:8]
    mine, other, source = refs[-3:]
    size = total.shape[0] // 2
    row = size // 2
    local = mine.shape[1]
    pitch = row + 8
    fill(source, [[(p, r * pitch) for p in inners] for r in range(2)])
    top = middle = bottom = None
    for across in range(3):
        terms = [
            product(which, source, 0, size, weights, extra, down, across) for down in (2, 1, 0)
        ]
        if across:
            terms = [old + term for old, term in zip((top, middle, bottom), terms)]
        top, middle, bottom = terms
    parts = [top[:row], top[row:] + middle[:row], middle[row:] + bottom[:row], bottom[row:]]
    for r, part in enumerate(parts):
        value = total[r * row : (r + 1) * row] + part
        for k, out in enumerate((mine, other)):
            block = value[:, k * local : (k + 1) * local]
            if which:
                block = block + lines[k : k + 1, :]
            out[r * row : (r + 1) * row] = block.astype(jnp.bfloat16)


SMEM = pl.BlockSpec(memory_space=pltpu.SMEM)
VMEM = pl.BlockSpec(memory_space=pltpu.VMEM)
ANY = pl.BlockSpec(memory_space=pl.ANY)


def cost(microseconds):
    work = 2**20 + 10**9 * microseconds
    return pl.CostEstimate(flops=work, bytes_accessed=2**20, transcendentals=0)


def kernel(body, shapes, args, scratch, name, placed=False, micros=0, kind=jnp.bfloat16):
    return pl.pallas_call(
        body,
        out_shape=[jax.ShapeDtypeStruct(s, kind) for s in shapes],
        in_specs=[SMEM] * placed + [VMEM] * (len(args) - placed),
        out_specs=[VMEM] * len(shapes),
        scratch_shapes=[pltpu.VMEM(s, jnp.bfloat16) for s in scratch],
        compiler_params=pltpu.CompilerParams(vmem_limit_bytes=20 * 2**20),
        cost_estimate=cost(micros),
        name=name,
    )(*args)


def cut(place, sources, bias, parts, micros):
    local = bias.shape[1]
    shape = (len(parts) * (sources[0].shape[1] // 2 + 8), local)
    body = lambda *refs: cut_kernel(parts, *refs)
    return kernel(body, [shape] * 2, [place, *sources, bias], [], "cut", True, micros)


def exchange(mine, other, near=None):
    sent = {1: other if near is None else near, 2: mine, 3: other}
    held = {k: swap(sent[k], "chan", k) for k in (1, 2, 3)}
    return [mine, held[1], held[2], held[3]]


def after(value, *others):
    return lax.optimization_barrier((value, others))[0]


def gather(value, steps):
    held, order = value[None], [0]
    for step in steps:
        held = jnp.concatenate([held, swap(held, "band", step)])
        order = order + [o ^ step for o in order]
    return held, order


def halving(size):
    steps = []
    while size > 1:
        size //= 2
        steps.append(size)
    return steps


def home_kernel(place, mine, other, out):
    width = mine.shape[2]
    block = out.shape[0]
    part = pl.ds(pl.program_id(0) * block, block)
    side = place[0] & 1
    for t in range(2):

        @pl.when(side == t)
        def _():
            out[:, :, t * width : (t + 1) * width] = mine[part]
            out[:, :, (1 - t) * width : (2 - t) * width] = other[part]


def home(place, mine, other, rows):
    turn = lambda p: jnp.transpose(p.reshape(rows, -1, p.shape[1]), (2, 0, 1))
    mine, other = turn(mine), turn(other)
    channels, rows, width = mine.shape
    return pl.pallas_call(
        home_kernel,
        out_shape=jax.ShapeDtypeStruct((channels, rows, 2 * width), jnp.bfloat16),
        grid=(4,),
        in_specs=[SMEM, VMEM, VMEM],
        out_specs=pl.BlockSpec((channels // 4, rows, 2 * width), lambda i: (i, 0, 0)),
        cost_estimate=cost(0),
        name="home",
    )(place, mine, other)


def token_kernel(*refs):
    refs[-1][...] = jnp.zeros_like(refs[-1])


def token(pieces, micros):
    return kernel(token_kernel, [(16, 128)], pieces, [], "token", False, micros)[0]


def per_device(image, filters, bias, upstream):
    n = lax.axis_size("chan")
    bands = lax.axis_size("band")
    taps, outs, local = filters.shape
    rows, cols = image.shape[1:]
    if n != 4 or local % 128 or cols % 256 or rows != 4 or outs % (32 * bands) or bands < 4:
        return plain(image, filters, bias, upstream)
    me = lax.axis_index("chan")
    band = lax.axis_index("band")
    half = me >> 1
    place = jnp.stack([me, band]).astype(jnp.int32)
    width = cols // 2

    share = outs // bands
    near = lax.dynamic_slice_in_dim(filters, band * share, share, axis=1).reshape(-1, local)
    start = (1 - half) * (outs // 2) + band * (share // 2)
    across = lax.dynamic_slice_in_dim(filters, start, share // 2, axis=1).reshape(-1, local)
    near = swap(near, "chan", 1)
    across = jnp.concatenate([swap(across, "chan", k) for k in (2, 3)])

    upstream, image = [jnp.transpose(v, (1, 2, 0)) for v in (upstream, image)]
    parts = [(i, r) for i in range(2) for r in (0, rows - 1)]
    sent = cut(place, [upstream, image], bias[None], parts, 6)
    pieces = exchange(*sent)
    inner = [[(i, r) for r in range(1, rows - 1)] for i in range(2)]
    sent = cut(place, after([upstream, image], pieces[3]), bias[None], inner[0], 25)
    pieces = after(pieces, sent)
    first = exchange(*sent)
    sent = cut(place, after([upstream, image], first[1:]), bias[None], inner[1], 9)
    first = after(first, sent)
    late = sent

    steps = halving(bands)[:-1]
    near, near_order = gather(near, steps)
    across, across_order = gather(across, steps[::-1])
    near, across = after((near, across), pieces[1])
    there = swap(jnp.concatenate([near, across], axis=1), "band", 1)
    held = [near, there[:, : near.shape[1]], across, there[:, near.shape[1] :]]
    second = [late[0], None, swap(late[0], "chan", 2), swap(late[1], "chan", 3)]
    second[1] = swap(after(late[1], held), "chan", 1)
    filters = kernel(
        lambda *refs: assemble_kernel((near_order, across_order), *refs),
        [(taps * outs, 2 * local), (taps * 2 * local, 2 * local)],
        [place, filters, *held],
        [],
        "assemble",
        True,
        2,
    )
    pitch = width + 8
    body = lambda *refs: rim_kernel(pitch, *refs)
    packed = kernel(body, [(8 * pitch, local)] * 2, pieces, [], "rim", False, 0)
    rims = neighbours(*packed)

    size = rows * width
    totals = kernel(
        outer_kernel,
        [(size, 2 * local)] * 2,
        [*pieces, *rims, *filters],
        [(3, size, 4 * local)] * 2,
        "outer",
        False,
        2,
        jnp.float32,
    )
    lines = jnp.concatenate([p[width + 2 : width + 3] for p in pieces[:2]]).astype(jnp.float32)
    marks = [[], []]
    marks[0].append(token(first, 9))
    kept, came = [], []
    for which in range(2):
        mine, other = kernel(
            lambda *refs: inner_kernel(which, *refs),
            [(size, local)] * 2,
            [*(first, second)[which], totals[which], *filters, lines, *marks[which]],
            [(3, size // 2, 4 * local)],
            "inner",
            False,
            9,
        )
        kept.append(mine)
        if not which:
            second = after(second, mine)
        came.append(swap(other, "chan", 1))
    image_grad = home(place, kept[0], came[0], rows)
    kept[1] = after(kept[1], image_grad)
    return home(place, kept[1], came[1], rows), image_grad


def solution(mesh):
    return jax.shard_map(
        per_device,
        mesh=mesh,
        in_specs=(
            P("chan", "band", None),
            P(None, None, "chan"),
            P("chan"),
            P("chan", "band", None),
        ),
        out_specs=(P("chan", "band", None), P("chan", "band", None)),
        check_vma=False,
    )
```

```python
import jax
import jax.numpy as jnp
from jax import lax
from jax.experimental import pallas as pl
from jax.experimental.pallas import tpu as pltpu
from jax.sharding import PartitionSpec as P


def swap(value, axis, step):
    size = lax.axis_size(axis)
    return lax.ppermute(value, axis, [(j, j ^ step) for j in range(size)])


def neighbours(first, last):
    size = lax.axis_size("band")
    up = [(j, j + 1) for j in range(size - 1)]
    down = [(j + 1, j) for j in range(size - 1)]
    return lax.ppermute(last, "band", up), lax.ppermute(first, "band", down)


def pick(pieces, index, axis):
    stacked = jnp.stack(pieces)
    return jnp.concatenate(
        [lax.dynamic_index_in_dim(stacked, i, 0, keepdims=False) for i in index], axis=axis
    )


def spread(value, me, width):
    n = lax.axis_size("chan")
    padded = jnp.pad(value, ((0, 0), (1, 1), (0, 0)))
    pieces = []
    for k in range(n):
        piece = lax.dynamic_slice_in_dim(padded, (me ^ k) * width, width + 2, axis=1)
        pieces.append(swap(piece, "chan", k) if k else piece)
    return pieces


def add_rows(value):
    before, after = neighbours(value[:1], value[-1:])
    return jnp.concatenate([before, value, after], axis=0)


def conv(source, taps):
    return lax.conv_general_dilated(
        source[None],
        taps,
        (1, 1),
        "VALID",
        dimension_numbers=("NHWC", "HWIO", "NHWC"),
        preferred_element_type=jnp.float32,
    )[0]


def plain(image, filters, bias, upstream):
    n = lax.axis_size("chan")
    bands = lax.axis_size("band")
    me = lax.axis_index("chan")
    row = lax.axis_index("band")
    local = filters.shape[2]
    outs = filters.shape[1]
    width = image.shape[2] // n

    flat = filters.reshape(-1, local)
    share = flat.shape[0] // bands
    part = lax.dynamic_slice_in_dim(flat, row * share, share, axis=0)
    held = [jnp.concatenate([part, jnp.tile(bias[None], (16, 1))], axis=0)]
    step = n // 2
    while step:
        stacked = jnp.stack(held)
        there = swap(stacked, "chan", step)
        held = held + [there[j] for j in range(len(held))]
        step //= 2
    order = [0]
    step = n // 2
    while step:
        order = order + [o ^ step for o in order]
        step //= 2
    held = [held[order.index(k)] for k in range(n)]
    biases = [h[share] for h in held]
    whole = lax.all_gather(
        jnp.stack([h[:share] for h in held]), "band", axis=1, tiled=True
    ).reshape(n, 3, 3, outs, local)

    x_pieces = spread(jnp.transpose(image, (1, 2, 0)), me, width)
    u_pieces = spread(jnp.transpose(upstream, (1, 2, 0)), me, width)

    natural = [me ^ k for k in range(n)]
    x = add_rows(jnp.concatenate(x_pieces, axis=2))
    forward_taps = jnp.transpose(whole, (1, 2, 0, 4, 3)).reshape(3, 3, n * local, outs)
    total = conv(x, forward_taps) + pick(biases, natural, 0).astype(jnp.float32)
    features = back(total.astype(jnp.bfloat16), me, local, True)

    u = add_rows(pick(u_pieces, natural, 2))
    backward_taps = jnp.transpose(whole[:, ::-1, ::-1], (1, 2, 3, 0, 4)).reshape(
        3, 3, outs, n * local
    )
    image_grad = back(conv(u, backward_taps).astype(jnp.bfloat16), me, local, False)
    return features, image_grad


def back(value, me, local, is_natural):
    n = lax.axis_size("chan")
    pieces = []
    for k in range(n):
        start = (me ^ k) * local if is_natural else k * local
        piece = lax.dynamic_slice_in_dim(value, start, local, axis=2)
        pieces.append(swap(piece, "chan", k) if k else piece)
    whole = pick(pieces, [me ^ k for k in range(n)], 1)
    return jnp.transpose(whole, (2, 0, 1))


def assemble_kernel(orders, place, filters, near, near_far, across, across_far, weights, extra):
    me, band = place[0], place[1]
    taps, channels, local = filters.shape
    share = near.shape[1] // taps
    half = share // 2
    for tap in range(taps):
        for j in range(4):
            start = pl.multiple_of((me ^ j) * local, local)
            weights[pl.ds(tap * channels + j * local, local), :local] = filters[
                tap, pl.ds(start, local), :
            ]
    for bit, held in enumerate((near, near_far)):
        for j, d in enumerate(orders[0]):
            first = (band ^ (d | bit)) * share
            block = lax.div(first, local)
            start = (block ^ me) * local + first - block * local
            for tap in range(taps):
                row = pl.multiple_of(tap * channels + start, 16)
                weights[pl.ds(row, share), local:] = held[j, tap * share : (tap + 1) * share]
    for bit, held in enumerate((across, across_far)):
        for j, d in enumerate(orders[1]):
            first = (band ^ (d | bit)) * half
            block = lax.div(first, local)
            start = (block ^ (me & 1)) * local + first - block * local
            for tap in range(taps):
                row = pl.multiple_of(tap * 2 * local + start, 16)
                for k in range(2):
                    at = (k * taps + tap) * half
                    extra[pl.ds(row, half), k * local : (k + 1) * local] = held[j, at : at + half]


def cut_kernel(parts, place, *refs):
    sources, (bias, mine, other) = refs[:-3], refs[-3:]
    side = place[0] & 1
    local = bias.shape[1]
    width = sources[0].shape[1] // 2
    pitch = width + 8
    line = bias[...].astype(jnp.float32)
    zero = jnp.zeros((1, local), jnp.float32)
    rest = jnp.concatenate([line, zero, zero, zero, zero, zero])
    for n, (i, r) in enumerate(parts):
        source = sources[i]
        left = source[r, width - 16 : width].astype(jnp.float32)[15:]
        right = source[r, width : width + 16].astype(jnp.float32)[:1]
        pieces = []
        for t, (before, behind) in enumerate(((zero, right), (left, zero))):
            tail = jnp.concatenate([behind, line, rest]).astype(jnp.bfloat16)
            middle = source[r, t * width : (t + 1) * width]
            pieces.append(jnp.concatenate([before.astype(jnp.bfloat16), middle, tail[:7]]))
        at = n * pitch
        mine[at : at + pitch] = jnp.where(side == 0, pieces[0], pieces[1])
        other[at : at + pitch] = jnp.where(side == 0, pieces[1], pieces[0])


def rim_kernel(pitch, *refs):
    pieces, (first, last) = refs[:4], refs[4:]
    for k, piece in enumerate(pieces):
        for i in range(2):
            for out, end in ((first, 0), (last, 1)):
                at = (2 * i + end) * pitch
                out[(2 * k + i) * pitch : (2 * k + i + 1) * pitch] = piece[at : at + pitch]


def fill(target, rows):
    width = target.shape[1] // len(rows)
    for r, row in enumerate(rows):
        for k, (ref, start) in enumerate(row):
            local = ref.shape[1]
            for shift in range(3):
                target[
                    shift, r * width : (r + 1) * width, k * local : (k + 1) * local
                ] = ref[start + shift : start + shift + width]


def product(which, source, at, size, weights, extra, down, across):
    half = weights.shape[1]
    if which == 0:
        tap = 3 * (2 - down) + across
        filters = weights[pl.ds(tap * 2 * half, 2 * half), :]
        return jnp.dot(
            source[2 - across, at : at + size], filters, preferred_element_type=jnp.float32
        )
    tap = 3 * down + across
    total = None
    for block in range(2):
        if block:
            filters = extra[pl.ds(tap * half, half), :]
        else:
            filters = weights[pl.ds(tap * 2 * half, half), :]
        term = lax.dot_general(
            source[across, at : at + size, block * half : (block + 1) * half],
            filters,
            (((1,), (1,)), ((), ())),
            preferred_element_type=jnp.float32,
        )
        total = term if total is None else total + term
    return total


def outer_kernel(*refs):
    pieces, (before, after, weights, extra), (*totals, upstream, image) = (
        refs[:4],
        refs[4:8],
        refs[8:],
    )
    pitch = before.shape[0] // 8
    for which, (total, source) in enumerate(zip(totals, (upstream, image))):
        rims = [[(rim, (2 * k + which) * pitch) for k in range(4)] for rim in (before, after)]
        edges = [[(p, (2 * which + end) * pitch) for p in pieces] for end in range(2)]
        fill(source, [rims[0], *edges, rims[1]])
        size = total.shape[0] // 2
        row = size // 2
        top = middle = bottom = None
        for across in range(3):
            terms = [
                product(which, source, at, size, weights, extra, down, across)
                for down, at in ((0, 0), (1, row), (2, size))
            ]
            if across:
                terms = [old + term for old, term in zip((top, middle, bottom), terms)]
            top, middle, bottom = terms
        total[:row] = top[:row] + middle[:row]
        total[row:size] = top[row:]
        total[size : size + row] = bottom[:row]
        total[size + row :] = bottom[row:] + middle[row:]


def inner_kernel(which, *refs):
    inners, (total, weights, extra, lines) = refs[:4], refs[4:8]
    mine, other, source = refs[-3:]
    size = total.shape[0] // 2
    row = size // 2
    local = mine.shape[1]
    pitch = row + 8
    fill(source, [[(p, r * pitch) for p in inners] for r in range(2)])
    top = middle = bottom = None
    for across in range(3):
        terms = [
            product(which, source, 0, size, weights, extra, down, across) for down in (2, 1, 0)
        ]
        if across:
            terms = [old + term for old, term in zip((top, middle, bottom), terms)]
        top, middle, bottom = terms
    parts = [top[:row], top[row:] + middle[:row], middle[row:] + bottom[:row], bottom[row:]]
    for r, part in enumerate(parts):
        value = total[r * row : (r + 1) * row] + part
        for k, out in enumerate((mine, other)):
            block = value[:, k * local : (k + 1) * local]
            if which:
                block = block + lines[k : k + 1, :]
            out[r * row : (r + 1) * row] = block.astype(jnp.bfloat16)


SMEM = pl.BlockSpec(memory_space=pltpu.SMEM)
VMEM = pl.BlockSpec(memory_space=pltpu.VMEM)
ANY = pl.BlockSpec(memory_space=pl.ANY)


def cost(microseconds):
    work = 2**20 + 10**9 * microseconds
    return pl.CostEstimate(flops=work, bytes_accessed=2**20, transcendentals=0)


def kernel(body, shapes, args, scratch, name, placed=False, micros=0, kind=jnp.bfloat16):
    return pl.pallas_call(
        body,
        out_shape=[jax.ShapeDtypeStruct(s, kind) for s in shapes],
        in_specs=[SMEM] * placed + [VMEM] * (len(args) - placed),
        out_specs=[VMEM] * len(shapes),
        scratch_shapes=[pltpu.VMEM(s, jnp.bfloat16) for s in scratch],
        compiler_params=pltpu.CompilerParams(vmem_limit_bytes=20 * 2**20),
        cost_estimate=cost(micros),
        name=name,
    )(*args)


def cut(place, sources, bias, parts, micros):
    local = bias.shape[1]
    shape = (len(parts) * (sources[0].shape[1] // 2 + 8), local)
    body = lambda *refs: cut_kernel(parts, *refs)
    return kernel(body, [shape] * 2, [place, *sources, bias], [], "cut", True, micros)


def exchange(mine, other, near=None):
    sent = {1: other if near is None else near, 2: mine, 3: other}
    held = {k: swap(sent[k], "chan", k) for k in (1, 2, 3)}
    return [mine, held[1], held[2], held[3]]


def after(value, *others):
    return lax.optimization_barrier((value, others))[0]


def gather(value, steps):
    held, order = value[None], [0]
    for step in steps:
        held = jnp.concatenate([held, swap(held, "band", step)])
        order = order + [o ^ step for o in order]
    return held, order


def halving(size):
    steps = []
    while size > 1:
        size //= 2
        steps.append(size)
    return steps


def home_kernel(place, mine, other, out):
    width = mine.shape[2]
    side = place[0] & 1
    for t in range(2):

        @pl.when(side == t)
        def _():
            out[:, :, t * width : (t + 1) * width] = mine[...]
            out[:, :, (1 - t) * width : (2 - t) * width] = other[...]


def home(place, mine, other, rows):
    turn = lambda p: jnp.transpose(p.reshape(rows, -1, p.shape[1]), (2, 0, 1))
    mine, other = turn(mine), turn(other)
    channels, rows, width = mine.shape
    shape = (channels, rows, 2 * width)
    return kernel(home_kernel, [shape], [place, mine, other], [], "home", True)[0]


def token_kernel(*refs):
    refs[-1][...] = jnp.zeros_like(refs[-1])


def token(pieces, micros):
    return kernel(token_kernel, [(16, 128)], pieces, [], "token", False, micros)[0]


def per_device(image, filters, bias, upstream):
    n = lax.axis_size("chan")
    bands = lax.axis_size("band")
    taps, outs, local = filters.shape
    rows, cols = image.shape[1:]
    if n != 4 or local % 128 or cols % 256 or rows != 4 or outs % (32 * bands) or bands < 4:
        return plain(image, filters, bias, upstream)
    me = lax.axis_index("chan")
    band = lax.axis_index("band")
    half = me >> 1
    place = jnp.stack([me, band]).astype(jnp.int32)
    width = cols // 2

    share = outs // bands
    near = lax.dynamic_slice_in_dim(filters, band * share, share, axis=1).reshape(-1, local)
    start = (1 - half) * (outs // 2) + band * (share // 2)
    across = lax.dynamic_slice_in_dim(filters, start, share // 2, axis=1).reshape(-1, local)
    near = swap(near, "chan", 1)
    across = swap(across, "chan", 2)
    across = jnp.concatenate([across, swap(across, "chan", 1)])

    upstream, image = [jnp.transpose(v, (1, 2, 0)) for v in (upstream, image)]
    parts = [(i, r) for i in range(2) for r in (0, rows - 1)]
    sent = cut(place, [upstream, image], bias[None], parts, 6)
    pieces = exchange(*sent)
    inner = [[(i, r) for r in range(1, rows - 1)] for i in range(2)]
    sent = cut(place, after([upstream, image], pieces[3]), bias[None], inner[0], 25)
    pieces = after(pieces, sent)
    first = exchange(*sent)
    sent = cut(place, after([upstream, image], first[1:]), bias[None], inner[1], 18)
    first = after(first, sent)
    second = exchange(*sent)

    steps = halving(bands)[:-1]
    near, near_order = gather(near, steps)
    across, across_order = gather(across, steps[::-1])
    there = swap(jnp.concatenate([near, across], axis=1), "band", 1)
    held = [near, there[:, : near.shape[1]], across, there[:, near.shape[1] :]]
    filters = kernel(
        lambda *refs: assemble_kernel((near_order, across_order), *refs),
        [(taps * outs, 2 * local), (taps * 2 * local, 2 * local)],
        [place, filters, *held],
        [],
        "assemble",
        True,
        2,
    )
    pitch = width + 8
    body = lambda *refs: rim_kernel(pitch, *refs)
    packed = kernel(body, [(8 * pitch, local)] * 2, pieces, [], "rim", False, 0)
    rims = neighbours(*packed)

    size = rows * width
    totals = kernel(
        outer_kernel,
        [(size, 2 * local)] * 2,
        [*pieces, *rims, *filters],
        [(3, size, 4 * local)] * 2,
        "outer",
        False,
        2,
        jnp.float32,
    )
    lines = jnp.concatenate([p[width + 2 : width + 3] for p in pieces[:2]]).astype(jnp.float32)
    marks = [[], []]
    marks[0].append(token(first, 2))
    kept, came = [], []
    for which in range(2):
        mine, other = kernel(
            lambda *refs: inner_kernel(which, *refs),
            [(size, local)] * 2,
            [*(first, second)[which], totals[which], *filters, lines, *marks[which]],
            [(3, size // 2, 4 * local)],
            "inner",
            False,
            9,
        )
        kept.append(mine)
        if not which:
            second = after(second, mine)
        came.append(swap(other, "chan", 1))
    image_grad = home(place, kept[0], came[0], rows)
    kept[1] = after(kept[1], image_grad)
    return home(place, kept[1], came[1], rows), image_grad


def solution(mesh):
    return jax.shard_map(
        per_device,
        mesh=mesh,
        in_specs=(
            P("chan", "band", None),
            P(None, None, "chan"),
            P("chan"),
            P("chan", "band", None),
        ),
        out_specs=(P("chan", "band", None), P("chan", "band", None)),
        check_vma=False,
    )
```
